32 devices in a mesh: groups: 2 (over y), tm: 4 (over z), space: 4 (over x, core).
Axes of the slice: x: 2, y: 2, z: 4, core: 2. Of those that a mesh axis runs over, the one named last changes fastest.
Arguments:
- multipliers: float32 [8, 50, 8192], P(('groups', 'tm'), None, 'space'), parts along dimension 0, may hold values from -6 to 6
- coefficients: float32 [8, 50, 8192], P(('groups', 'tm'), None, 'space'), parts along dimension 0, may hold values from 0.2 to 5
- neighbours: int32 [4, 8192], P(None, 'space'), may hold values from 0 to 10240, as said below
- send_list: int32 [8192], P('space'), may hold values from 0 to 8191, as said below
- interior: float32 [50, 50], replicated, may hold values from -0.875 to 0.875
- extract: float32 [4, 30, 50], replicated, may hold values from -0.875 to 0.875
- lift: float32 [4, 50, 30], replicated, may hold values from -0.5 to 0.5
Outputs:
- schur_product: float32 [8, 50, 8192], P(('groups', 'tm'), None, 'space'), parts along dimension 0
The draws below stay inside these ranges and needn't reach their ends.
There are 2 independent parts, one for each index of `groups`. The reference program is written for one: setup_inputs(seed, part) draws one part's arguments, and reference() takes and returns one part's arrays. A program takes and returns all parts, laid end to end along the dimension named above; an argument that names none is the same for every part. Nothing has to cross between parts.
Inputs may be any that keep to these rules, and one draw needn't show every extreme that they name: `neighbours`: in each partition's block, the entries name each of the 2048 received columns 8192 .. 10239 exactly once, the zero column 10240 exactly 256 times, and own face columns below 8192 at most once each, column 0 among them. `send_list`: distinct within each partition's block of 2048 entries, each block naming columns 0 and 8191.
All inputs are finite; a program needn't handle non-finite values.
Results may differ from the reference program's by a relative error of at most 0.00005.
Values sent between devices are 32-bit elements; how exact they have to be, the bound alone decides.
No kernel may reach another device: no remote copies, remote signals or barrier semaphores. Data moves between devices by JAX's collectives and lax.ppermute only.
A program may use at most 64 MiB of HBM per device.

```python
import math
import jax
import jax.numpy as jnp
from jax import lax

NC = 50
NF = 30
E_DEV = 2048
HALO = 1024
WALLS = 256
ELEMS = 8192
SEGS = 4
N_SPACE = 4


def one_partition(key):
    first, second = jax.random.split(key, 2)
    local = 1 + jax.random.permutation(first, 4 * E_DEV - 1)[:4 * E_DEV - 2 * HALO - WALLS - 1]
    values = jnp.concatenate([jnp.zeros((1,), jnp.int32), local.astype(jnp.int32), (4 * E_DEV + jnp.arange(2 * HALO)).astype(jnp.int32), jnp.full((WALLS,), 4 * E_DEV + 2 * HALO, jnp.int32)])
    values = jax.random.permutation(second, values)
    return values.reshape(4, E_DEV).astype(jnp.int32)


def draw_neighbours(key, part):
    key = jax.random.fold_in(key, 11)
    keys = jax.random.split(key, ELEMS // E_DEV)
    tables = jax.vmap(one_partition)(keys)
    return tables.transpose(1, 0, 2).reshape(4, ELEMS).astype(jnp.int32)


def one_sender(key):
    first, second = jax.random.split(key, 2)
    middle = 1 + jax.random.permutation(first, 4 * E_DEV - 2)[:2 * HALO - 2]
    values = jnp.concatenate([jnp.zeros((1,), jnp.int32), jnp.full((1,), 4 * E_DEV - 1, jnp.int32), middle.astype(jnp.int32)])
    return jax.random.permutation(second, values).astype(jnp.int32)


def draw_send_list(key, part):
    key = jax.random.fold_in(key, 12)
    keys = jax.random.split(key, ELEMS // E_DEV)
    return jax.vmap(one_sender)(keys).reshape(-1).astype(jnp.int32)


def level_of(rng, shape, pieces, low, largest):
    def one(dim, blocks):
        heights = jax.random.uniform(jax.random.fold_in(jax.random.fold_in(rng, 6), dim), (blocks,), jnp.float32, low / len(pieces), largest / len(pieces))
        return jnp.repeat(jnp.exp(heights), shape[dim] // blocks).reshape((-1,) + (1,) * (len(shape) - dim - 1))

    level = one(*pieces[0])
    for cut in pieces[1:]:
        level = level * one(*cut)
    return level


def centred(stream_key, dims, spread, bound, shards=(), dtype=jnp.bfloat16):
    array = jax.random.normal(stream_key, dims, jnp.float32) * spread
    if len(shards) > 0:
        array = level_of(stream_key, dims, shards, -0.22, 0.18) * array
    return jnp.clip(array, min=-bound, max=bound).astype(dtype)


def setup_inputs(seed: int = 0, part: int = 0) -> dict:
    splits = jax.random.split(jax.random.key(seed), 8)
    part_splits = jax.random.split(jax.random.fold_in(splits[7], part), 8)
    return {
        "multipliers": centred(part_splits[0], (SEGS, NC, ELEMS), 1.0, 6.0, ((0, 4), (2, 4)), jnp.float32),
        "coefficients": jnp.clip(jnp.exp(math.log(5.0) - 3.218876 * jax.random.uniform(part_splits[1], (SEGS, NC, ELEMS), jnp.float32) ** level_of(part_splits[1], (SEGS, NC, ELEMS), ((0, 4), (2, 4)), -0.2, 0.2)), 0.2, 5.0),
        "neighbours": draw_neighbours(jax.random.fold_in(splits[7], 71), part),
        "send_list": draw_send_list(jax.random.fold_in(splits[7], 71), part),
        "interior": centred(splits[4], (NC, NC), NC ** -0.5, 0.875, (), jnp.float32),
        "extract": centred(splits[5], (4, NF, NC), NC ** -0.5, 0.875, (), jnp.float32),
        "lift": centred(splits[6], (4, NC, NF), (4 * NF) ** -0.5, 0.5, (), jnp.float32),
    }


HIGHEST = lax.Precision.HIGHEST


def product(left, right):
    return jnp.dot(left, right, precision=HIGHEST, preferred_element_type=jnp.float32)


def split_parts(field):
    return field.reshape(field.shape[0], N_SPACE, E_DEV).transpose(1, 0, 2)


def join_parts(field):
    return field.transpose(1, 0, 2).reshape(field.shape[1], N_SPACE * E_DEV)


def face_values(state, extract):
    return jnp.concatenate([product(extract[face], state) for face in range(4)], axis=1)


def tangent_step(state, coefs, neighbours, send_list, interior, extract, lift):
    parts_state = split_parts(state)
    parts_coef = split_parts(coefs)
    parts_links = split_parts(neighbours)
    sends = send_list.reshape(N_SPACE, 2 * HALO)
    faces = jax.vmap(face_values, (0, None))(parts_state, extract)
    outgoing = jax.vmap(lambda table, index: table[:, index])(faces, sends)
    from_prev = jnp.roll(outgoing, 1, axis=0)[:, :, HALO:]
    from_next = jnp.roll(outgoing, -1, axis=0)[:, :, :HALO]
    pool = jnp.concatenate([faces, from_prev, from_next, jnp.zeros((N_SPACE, NF, 1), jnp.float32)], axis=2)
    across = jax.vmap(lambda table, index: table[:, index.reshape(-1)])(pool, parts_links)
    trace = 0.5 * (faces + across)
    lifted = jnp.einsum("fcm,pmfe->pce", lift, trace.reshape(N_SPACE, NF, 4, E_DEV), precision=HIGHEST)
    inner = jnp.einsum("cd,pde->pce", interior, parts_coef * parts_state, precision=HIGHEST)
    return join_parts(parts_state + inner + lifted)


def adjoint_step(state, coefs, neighbours, send_list, interior, extract, lift):
    parts_state = split_parts(state)
    parts_coef = split_parts(coefs)
    parts_links = split_parts(neighbours)
    sends = send_list.reshape(N_SPACE, 2 * HALO)
    pooled = 4 * E_DEV + 2 * HALO + 1
    back = jnp.einsum("fcm,pce->pmfe", lift, parts_state, precision=HIGHEST).reshape(N_SPACE, NF, 4 * E_DEV)
    half = 0.5 * back
    sums = jax.vmap(lambda part, index: jnp.zeros((NF, pooled), jnp.float32).at[:, index.reshape(-1)].add(part))(half, parts_links)
    acc_prev = sums[:, :, 4 * E_DEV:4 * E_DEV + HALO]
    acc_next = sums[:, :, 4 * E_DEV + HALO:4 * E_DEV + 2 * HALO]
    returned = jnp.concatenate([jnp.roll(acc_next, 1, axis=0), jnp.roll(acc_prev, -1, axis=0)], axis=2)
    dfaces = half + sums[:, :, :4 * E_DEV]
    dfaces = jax.vmap(lambda table, index, extra: table.at[:, index].add(extra))(dfaces, sends, returned)
    faces_back = jnp.einsum("fmc,pmfe->pce", extract, dfaces.reshape(N_SPACE, NF, 4, E_DEV), precision=HIGHEST)
    inner = parts_coef * jnp.einsum("dc,pde->pce", interior, parts_state, precision=HIGHEST)
    return join_parts(parts_state + inner + faces_back)


def reference(multipliers, coefficients, neighbours, send_list, interior, extract, lift):
    adjoint_image = lax.map(lambda pair: adjoint_step(pair[0], pair[1], neighbours, send_list, interior, extract, lift), (multipliers, coefficients))
    earlier = jnp.concatenate([jnp.zeros_like(multipliers[:1]), multipliers[:-1]], axis=0)
    combined = adjoint_image - earlier
    later = jnp.concatenate([combined[1:], jnp.zeros_like(combined[:1])], axis=0)
    forward = lax.map(lambda pair: tangent_step(pair[0], pair[1], neighbours, send_list, interior, extract, lift), (combined, coefficients))
    return forward - later
```

```python
import functools

import jax
import jax.numpy as jnp
from jax import lax
from jax.experimental import pallas as pl
from jax.experimental.pallas import tpu as pltpu
from jax.sharding import PartitionSpec as P

LANES = 128
SLOT = 32
UNROLL = 16
VMEM_LIMIT = 48 * 1024 * 1024


def halves(value):
    high = value.astype(jnp.bfloat16)
    low = (value - high.astype(jnp.float32)).astype(jnp.bfloat16)
    return high, low


def product(left, right, left_dim, right_dim):
    dims = (((left_dim,), (right_dim,)), ((), ()))
    left_high, left_low = halves(left)
    right_high, right_low = halves(right)

    def one(a, b):
        return lax.dot_general(a, b, dims, preferred_element_type=jnp.float32)

    return one(left_high, right_high) + (one(left_high, right_low) + one(left_low, right_high))


def pad_rows(value, rows):
    missing = rows - value.shape[0]
    if missing == 0:
        return value
    return jnp.concatenate([value, jnp.zeros((missing, value.shape[1]), value.dtype)], axis=0)


def pad_columns(value, columns):
    missing = columns - value.shape[1]
    if missing == 0:
        return value
    return jnp.concatenate([value, jnp.zeros((value.shape[0], missing), value.dtype)], axis=1)


def slot_of_lane(shape):
    return lax.broadcasted_iota(jnp.int32, shape, 1) // SLOT


def choose_slots(blocks):
    slot = slot_of_lane(blocks[0].shape)
    result = blocks[0]
    for q in range(1, len(blocks)):
        result = jnp.where(slot == q, blocks[q], result)
    return result


def repeat_slot(block, q):
    only = jnp.where(slot_of_lane(block.shape) == q, block, 0.0)
    twice = only + pltpu.roll(only, SLOT, 1)
    return twice + pltpu.roll(twice, 2 * SLOT, 1)


def for_rows(count, step):
    def body(i, carry):
        base = i * UNROLL
        step(base)
        return carry

    lax.fori_loop(0, count // UNROLL, body, 0)


def face_tables(transposed, extract_ref, table, count):
    for f in range(4):
        padded = pad_rows(extract_ref[f], SLOT)
        repeated = jnp.concatenate([padded] * 4, axis=0)
        table[f * count : (f + 1) * count, :] = product(transposed, repeated, 1, 1)


def packed_extract(extract_ref):
    return jnp.concatenate([pad_rows(extract_ref[f], SLOT) for f in range(4)], axis=0)


def adjoint_local(width, links, state_ref, coefs_ref, interior, extract, lift, partial, to_prev, to_next, half, sums):
    count = state_ref.shape[2]
    state = state_ref[0]
    transposed = state.T
    for f in range(4):
        slot = pad_columns(0.5 * lift[f], SLOT)
        half[f * count : (f + 1) * count, :] = product(transposed, jnp.concatenate([slot] * 4, axis=1), 1, 0)
    sums[...] = jnp.zeros_like(sums)
    for f in range(4):

        def scatter(base):
            for u in range(UNROLL):
                row = half[pl.ds(f * count + base + u, 1), :]
                sums[pl.ds(links[f, base + u], 1), :] = row

        for_rows(count, scatter)
    quarter = width // 4
    for out, start in ((to_prev, 4 * count), (to_next, 4 * count + width)):
        out[...] = choose_slots([sums[start + q * quarter : start + (q + 1) * quarter, :] for q in range(4)])
    dfaces = choose_slots(
        [half[f * count : (f + 1) * count, :] + sums[f * count : (f + 1) * count, :] for f in range(4)]
    )
    back = product(packed_extract(extract).T, dfaces, 1, 1)
    partial[...] = state + coefs_ref[0] * product(interior[...].T, state, 1, 0) + back


def join_and_pick(
    width, sends, partial, earlier, from_prev, from_next, extract, combined, to_prev, to_next, received, extra, faces
):
    count = partial.shape[1]
    quarter = width // 4
    for source, start in ((from_prev, 0), (from_next, width)):
        for q in range(4):
            received[start + q * quarter : start + (q + 1) * quarter, :] = repeat_slot(source[...], q)
    extra[...] = jnp.zeros_like(extra)

    def scatter(base):
        for u in range(UNROLL):
            extra[pl.ds(sends[base + u], 1), :] = received[pl.ds(base + u, 1), :]

    for_rows(2 * width, scatter)
    dfaces = choose_slots([extra[f * count : (f + 1) * count, :] for f in range(4)])
    total = partial[...] - earlier[...] + product(packed_extract(extract).T, dfaces, 1, 1)
    combined[...] = total
    face_tables(total.T, extract, faces, count)
    for out, start in ((to_prev, 0), (to_next, width)):
        for q in range(4):
            lanes = slice(q * SLOT, (q + 1) * SLOT)

            def pick(base):
                for u in range(UNROLL):
                    row = faces[pl.ds(sends[start + q * quarter + base + u], 1), lanes]
                    out[pl.ds(base + u, 1), lanes] = row

            for_rows(quarter, pick)


def tangent_rest(
    width, links, combined, coefs_ref, from_prev, from_next, later, interior, extract, lift, result, pool, across
):
    count = combined.shape[1]
    quarter = width // 4
    state = combined[...]
    transposed = state.T
    face_tables(transposed, extract, pool, count)
    for source, start in ((from_prev, 4 * count), (from_next, 4 * count + width)):
        for q in range(4):
            pool[start + q * quarter : start + (q + 1) * quarter, :] = repeat_slot(source[...], q)
    pool[4 * count + 2 * width :, :] = jnp.zeros((8, LANES), jnp.float32)
    for f in range(4):
        lanes = slice(f * SLOT, (f + 1) * SLOT)

        def pick(base):
            for u in range(UNROLL):
                row = pool[pl.ds(links[f, base + u], 1), lanes]
                across[pl.ds(base + u, 1), lanes] = row

        for_rows(count, pick)
    faces = product(transposed, packed_extract(extract), 1, 1)
    trace = 0.5 * (faces + across[...])
    packed_lift = jnp.concatenate([pad_columns(lift[f], SLOT) for f in range(4)], axis=1)
    lifted = product(interior[...], coefs_ref[0] * state, 1, 0) + product(packed_lift, trace, 1, 1)
    result[0] = state + lifted - later[...]


def call(kernel, width, outs, scratch, table, operands, name):
    vmem = pl.BlockSpec(memory_space=pltpu.VMEM)
    return pl.pallas_call(
        functools.partial(kernel, width),
        out_shape=[jax.ShapeDtypeStruct(shape, jnp.float32) for shape in outs],
        in_specs=[pl.BlockSpec(memory_space=pltpu.SMEM)] + [vmem] * len(operands),
        out_specs=[vmem] * len(outs),
        scratch_shapes=[pltpu.VMEM((rows, LANES), jnp.float32) for rows in scratch],
        compiler_params=pltpu.CompilerParams(vmem_limit_bytes=VMEM_LIMIT),
        name=name,
    )(table, *operands)


def around(to_prev, to_next, axis):
    devices = lax.axis_size(axis)
    up = [(i, (i + 1) % devices) for i in range(devices)]
    down = [(j, i) for i, j in up]
    return lax.ppermute(to_next, axis, up), lax.ppermute(to_prev, axis, down)


def from_behind(array, axis, by):
    devices = lax.axis_size(axis)
    pairs = [(i, i + by) for i in range(devices) if 0 <= i + by < devices]
    return lax.ppermute(array, axis, pairs)


def per_device(multipliers, coefficients, neighbours, send_list, interior, extract, lift):
    rows, count = multipliers.shape[1:]
    width = send_list.shape[0] // 2
    message = (width // 4, LANES)
    earlier = from_behind(multipliers[0], "tm", 1)
    partial, to_prev, to_next = call(
        adjoint_local,
        width,
        [(rows, count), message, message],
        [4 * count, 4 * count + 2 * width + 8],
        neighbours,
        (multipliers, coefficients, interior, extract, lift),
        "adjoint_local",
    )
    from_prev, from_next = around(to_prev, to_next, "space")
    combined, to_prev, to_next = call(
        join_and_pick,
        width,
        [(rows, count), message, message],
        [2 * width, 4 * count, 4 * count],
        send_list,
        (partial, earlier, from_prev, from_next, extract),
        "join_and_pick",
    )
    later = from_behind(combined, "tm", -1)
    from_prev, from_next = around(to_prev, to_next, "space")
    (result,) = call(
        tangent_rest,
        width,
        [(1, rows, count)],
        [4 * count + 2 * width + 8, count],
        neighbours,
        (combined, coefficients, from_prev, from_next, later, interior, extract, lift),
        "tangent_rest",
    )
    return result


def solution(mesh):
    placed = (
        P(("groups", "tm"), None, "space"),
        P(("groups", "tm"), None, "space"),
        P(None, "space"),
        P("space"),
        P(),
        P(),
        P(),
    )
    return jax.shard_map(
        per_device,
        mesh=mesh,
        in_specs=placed,
        out_specs=P(("groups", "tm"), None, "space"),
        check_vma=False,
    )
```

```python
import functools

import jax
import jax.numpy as jnp
from jax import lax
from jax.experimental import pallas as pl
from jax.experimental.pallas import tpu as pltpu
from jax.sharding import PartitionSpec as P

LANES = 128
SLOT = 32
UNROLL = 16
VMEM_LIMIT = 48 * 1024 * 1024


def halves(value):
    high = value.astype(jnp.bfloat16)
    low = (value - high.astype(jnp.float32)).astype(jnp.bfloat16)
    return high, low


def product(left, right, left_dim, right_dim):
    dims = (((left_dim,), (right_dim,)), ((), ()))
    left_high, left_low = halves(left)
    right_high, right_low = halves(right)

    def one(a, b):
        return lax.dot_general(a, b, dims, preferred_element_type=jnp.float32)

    return one(left_high, right_high) + (one(left_high, right_low) + one(left_low, right_high))


def pad_rows(value, rows):
    missing = rows - value.shape[0]
    if missing == 0:
        return value
    return jnp.concatenate([value, jnp.zeros((missing, value.shape[1]), value.dtype)], axis=0)


def pad_columns(value, columns):
    missing = columns - value.shape[1]
    if missing == 0:
        return value
    return jnp.concatenate([value, jnp.zeros((value.shape[0], missing), value.dtype)], axis=1)


def slot_of_lane(shape):
    return lax.broadcasted_iota(jnp.int32, shape, 1) // SLOT


def choose_slots(blocks):
    slot = slot_of_lane(blocks[0].shape)
    result = blocks[0]
    for q in range(1, len(blocks)):
        result = jnp.where(slot == q, blocks[q], result)
    return result


def repeat_slot(block, q):
    only = jnp.where(slot_of_lane(block.shape) == q, block, 0.0)
    twice = only + pltpu.roll(only, SLOT, 1)
    return twice + pltpu.roll(twice, 2 * SLOT, 1)


def for_rows(count, step):
    def body(i, carry):
        base = i * UNROLL
        step(base)
        return carry

    lax.fori_loop(0, count // UNROLL, body, 0)


def face_tables(transposed, extract_ref, table, count):
    for f in range(4):
        padded = pad_rows(extract_ref[f], SLOT)
        repeated = jnp.concatenate([padded] * 4, axis=0)
        table[f * count : (f + 1) * count, :] = product(transposed, repeated, 1, 1)


def packed_extract(extract_ref):
    return jnp.concatenate([pad_rows(extract_ref[f], SLOT) for f in range(4)], axis=0)


def adjoint_local(width, links, state_ref, coefs_ref, interior, extract, lift, partial, to_prev, to_next, half, sums):
    count = state_ref.shape[2]
    state = state_ref[0]
    transposed = state.T
    for f in range(4):
        slot = pad_columns(0.5 * lift[f], SLOT)
        half[f * count : (f + 1) * count, :] = product(transposed, jnp.concatenate([slot] * 4, axis=1), 1, 0)
    sums[...] = jnp.zeros_like(sums)
    for f in range(4):

        def scatter(base):
            rows = [half[pl.ds(f * count + base + u, 1), :] for u in range(UNROLL)]
            for u in range(UNROLL):
                sums[pl.ds(links[f, base + u], 1), :] = rows[u]

        for_rows(count, scatter)
    quarter = width // 4
    for out, start in ((to_prev, 4 * count), (to_next, 4 * count + width)):
        out[...] = choose_slots([sums[start + q * quarter : start + (q + 1) * quarter, :] for q in range(4)])
    dfaces = choose_slots(
        [half[f * count : (f + 1) * count, :] + sums[f * count : (f + 1) * count, :] for f in range(4)]
    )
    back = product(packed_extract(extract).T, dfaces, 1, 1)
    partial[...] = state + coefs_ref[0] * product(interior[...].T, state, 1, 0) + back


def join_and_pick(
    width, sends, partial, earlier, from_prev, from_next, extract, combined, to_prev, to_next, received, extra, faces
):
    count = partial.shape[1]
    quarter = width // 4
    for source, start in ((from_prev, 0), (from_next, width)):
        for q in range(4):
            received[start + q * quarter : start + (q + 1) * quarter, :] = repeat_slot(source[...], q)
    extra[...] = jnp.zeros_like(extra)

    def scatter(base):
        rows = [received[pl.ds(base + u, 1), :] for u in range(UNROLL)]
        for u in range(UNROLL):
            extra[pl.ds(sends[base + u], 1), :] = rows[u]

    for_rows(2 * width, scatter)
    dfaces = choose_slots([extra[f * count : (f + 1) * count, :] for f in range(4)])
    total = partial[...] - earlier[...] + product(packed_extract(extract).T, dfaces, 1, 1)
    combined[...] = total
    face_tables(total.T, extract, faces, count)
    for out, start in ((to_prev, 0), (to_next, width)):
        for q in range(4):
            lanes = slice(q * SLOT, (q + 1) * SLOT)

            def pick(base):
                first = start + q * quarter + base
                rows = [faces[pl.ds(sends[first + u], 1), lanes] for u in range(UNROLL)]
                for u in range(UNROLL):
                    out[pl.ds(base + u, 1), lanes] = rows[u]

            for_rows(quarter, pick)


def tangent_rest(
    width, links, combined, coefs_ref, from_prev, from_next, interior, extract, lift, result, pool, across
):
    count = combined.shape[1]
    quarter = width // 4
    state = combined[...]
    transposed = state.T
    face_tables(transposed, extract, pool, count)
    for source, start in ((from_prev, 4 * count), (from_next, 4 * count + width)):
        for q in range(4):
            pool[start + q * quarter : start + (q + 1) * quarter, :] = repeat_slot(source[...], q)
    pool[4 * count + 2 * width :, :] = jnp.zeros((8, LANES), jnp.float32)
    for f in range(4):
        lanes = slice(f * SLOT, (f + 1) * SLOT)

        def pick(base):
            rows = [pool[pl.ds(links[f, base + u], 1), lanes] for u in range(UNROLL)]
            for u in range(UNROLL):
                across[pl.ds(base + u, 1), lanes] = rows[u]

        for_rows(count, pick)
    faces = product(transposed, packed_extract(extract), 1, 1)
    trace = 0.5 * (faces + across[...])
    packed_lift = jnp.concatenate([pad_columns(lift[f], SLOT) for f in range(4)], axis=1)
    lifted = product(interior[...], coefs_ref[0] * state, 1, 0) + product(packed_lift, trace, 1, 1)
    result[...] = state + lifted


def call(kernel, width, outs, scratch, table, operands, name):
    vmem = pl.BlockSpec(memory_space=pltpu.VMEM)
    return pl.pallas_call(
        functools.partial(kernel, width),
        out_shape=[jax.ShapeDtypeStruct(shape, jnp.float32) for shape in outs],
        in_specs=[pl.BlockSpec(memory_space=pltpu.SMEM)] + [vmem] * len(operands),
        out_specs=[vmem] * len(outs),
        scratch_shapes=[pltpu.VMEM((rows, LANES), jnp.float32) for rows in scratch],
        compiler_params=pltpu.CompilerParams(vmem_limit_bytes=VMEM_LIMIT),
        name=name,
    )(table, *operands)


def around(to_prev, to_next, axis):
    devices = lax.axis_size(axis)
    up = [(i, (i + 1) % devices) for i in range(devices)]
    down = [(j, i) for i, j in up]
    return lax.ppermute(to_next, axis, up), lax.ppermute(to_prev, axis, down)


def from_behind(array, axis, by):
    devices = lax.axis_size(axis)
    pairs = [(i, i + by) for i in range(devices) if 0 <= i + by < devices]
    return lax.ppermute(array, axis, pairs)


def per_device(multipliers, coefficients, neighbours, send_list, interior, extract, lift):
    rows, count = multipliers.shape[1:]
    width = send_list.shape[0] // 2
    message = (width // 4, LANES)
    earlier = from_behind(multipliers[0], "tm", 1)
    partial, to_prev, to_next = call(
        adjoint_local,
        width,
        [(rows, count), message, message],
        [4 * count, 4 * count + 2 * width + 8],
        neighbours,
        (multipliers, coefficients, interior, extract, lift),
        "adjoint_local",
    )
    from_prev, from_next = around(to_prev, to_next, "space")
    combined, to_prev, to_next = call(
        join_and_pick,
        width,
        [(rows, count), message, message],
        [2 * width, 4 * count, 4 * count],
        send_list,
        (partial, earlier, from_prev, from_next, extract),
        "join_and_pick",
    )
    later = from_behind(combined, "tm", -1)
    from_prev, from_next = around(to_prev, to_next, "space")
    (forward,) = call(
        tangent_rest,
        width,
        [(rows, count)],
        [4 * count + 2 * width + 8, count],
        neighbours,
        (combined, coefficients, from_prev, from_next, interior, extract, lift),
        "tangent_rest",
    )
    return (forward - later)[None]


def solution(mesh):
    placed = (
        P(("groups", "tm"), None, "space"),
        P(("groups", "tm"), None, "space"),
        P(None, "space"),
        P("space"),
        P(),
        P(),
        P(),
    )
    return jax.shard_map(
        per_device,
        mesh=mesh,
        in_specs=placed,
        out_specs=P(("groups", "tm"), None, "space"),
        check_vma=False,
    )
```

```python
import functools

import jax
import jax.numpy as jnp
from jax import lax
from jax.experimental import pallas as pl
from jax.experimental.pallas import tpu as pltpu
from jax.sharding import PartitionSpec as P

LANES = 128
SLOT = 32
UNROLL = 16
VMEM_LIMIT = 48 * 1024 * 1024


def halves(value):
    high = value.astype(jnp.bfloat16)
    low = (value - high.astype(jnp.float32)).astype(jnp.bfloat16)
    return high, low


def product(left, right, left_dim, right_dim):
    dims = (((left_dim,), (right_dim,)), ((), ()))
    left_high, left_low = halves(left)
    right_high, right_low = halves(right)

    def one(a, b):
        return lax.dot_general(a, b, dims, preferred_element_type=jnp.float32)

    return one(left_high, right_high) + (one(left_high, right_low) + one(left_low, right_high))


def pad_rows(value, rows):
    missing = rows - value.shape[0]
    if missing == 0:
        return value
    return jnp.concatenate([value, jnp.zeros((missing, value.shape[1]), value.dtype)], axis=0)


def pad_columns(value, columns):
    missing = columns - value.shape[1]
    if missing == 0:
        return value
    return jnp.concatenate([value, jnp.zeros((value.shape[0], missing), value.dtype)], axis=1)


def slot_of_lane(shape):
    return lax.broadcasted_iota(jnp.int32, shape, 1) // SLOT


def choose_slots(blocks):
    slot = slot_of_lane(blocks[0].shape)
    result = blocks[0]
    for q in range(1, len(blocks)):
        result = jnp.where(slot == q, blocks[q], result)
    return result


def repeat_slot(block, q):
    only = jnp.where(slot_of_lane(block.shape) == q, block, 0.0)
    twice = only + pltpu.roll(only, SLOT, 1)
    return twice + pltpu.roll(twice, 2 * SLOT, 1)


def for_rows(count, step):
    def body(i, carry):
        base = i * UNROLL
        step(base)
        return carry

    lax.fori_loop(0, count // UNROLL, body, 0)


def flat_links(neighbours):
    count = neighbours.shape[1]
    return neighbours.reshape(4, count // LANES, LANES).transpose(1, 0, 2).reshape(-1)


def for_faces(count, step):
    groups = LANES // UNROLL

    def body(i, carry):
        block, inside = i // groups, (i % groups) * UNROLL
        for f in range(4):
            step(f, block * LANES + inside, block * (4 * LANES) + f * LANES + inside)
        return carry

    lax.fori_loop(0, count // UNROLL, body, 0)


def face_tables(transposed, extract_ref, table, count):
    for f in range(4):
        padded = pad_rows(extract_ref[f], SLOT)
        repeated = jnp.concatenate([padded] * 4, axis=0)
        table[f * count : (f + 1) * count, :] = product(transposed, repeated, 1, 1)


def packed_extract(extract_ref):
    return jnp.concatenate([pad_rows(extract_ref[f], SLOT) for f in range(4)], axis=0)


def adjoint_local(width, links, state_ref, coefs_ref, interior, extract, lift, partial, to_prev, to_next, half, sums):
    count = state_ref.shape[2]
    state = state_ref[0]
    transposed = state.T
    for f in range(4):
        slot = pad_columns(0.5 * lift[f], SLOT)
        half[f * count : (f + 1) * count, :] = product(transposed, jnp.concatenate([slot] * 4, axis=1), 1, 0)
    sums[...] = jnp.zeros_like(sums)

    def scatter(f, base, first):
        rows = [half[pl.ds(f * count + base + u, 1), :] for u in range(UNROLL)]
        for u in range(UNROLL):
            sums[pl.ds(links[first + u], 1), :] = rows[u]

    for_faces(count, scatter)
    quarter = width // 4
    for out, start in ((to_prev, 4 * count), (to_next, 4 * count + width)):
        out[...] = choose_slots([sums[start + q * quarter : start + (q + 1) * quarter, :] for q in range(4)])
    dfaces = choose_slots(
        [half[f * count : (f + 1) * count, :] + sums[f * count : (f + 1) * count, :] for f in range(4)]
    )
    back = product(packed_extract(extract).T, dfaces, 1, 1)
    partial[...] = state + coefs_ref[0] * product(interior[...].T, state, 1, 0) + back


def join_and_pick(
    width, sends, partial, earlier, from_prev, from_next, extract, combined, to_prev, to_next, received, extra, faces
):
    count = partial.shape[1]
    quarter = width // 4
    for source, start in ((from_prev, 0), (from_next, width)):
        for q in range(4):
            received[start + q * quarter : start + (q + 1) * quarter, :] = repeat_slot(source[...], q)
    extra[...] = jnp.zeros_like(extra)

    def scatter(base):
        rows = [received[pl.ds(base + u, 1), :] for u in range(UNROLL)]
        for u in range(UNROLL):
            extra[pl.ds(sends[base + u], 1), :] = rows[u]

    for_rows(2 * width, scatter)
    dfaces = choose_slots([extra[f * count : (f + 1) * count, :] for f in range(4)])
    total = partial[...] - earlier[...] + product(packed_extract(extract).T, dfaces, 1, 1)
    combined[...] = total
    face_tables(total.T, extract, faces, count)
    for out, start in ((to_prev, 0), (to_next, width)):
        for q in range(4):
            lanes = slice(q * SLOT, (q + 1) * SLOT)

            def pick(base):
                first = start + q * quarter + base
                rows = [faces[pl.ds(sends[first + u], 1), lanes] for u in range(UNROLL)]
                for u in range(UNROLL):
                    out[pl.ds(base + u, 1), lanes] = rows[u]

            for_rows(quarter, pick)


def tangent_rest(
    width, links, combined, coefs_ref, from_prev, from_next, interior, extract, lift, result, pool, across
):
    count = combined.shape[1]
    quarter = width // 4
    state = combined[...]
    transposed = state.T
    face_tables(transposed, extract, pool, count)
    for source, start in ((from_prev, 4 * count), (from_next, 4 * count + width)):
        for q in range(4):
            pool[start + q * quarter : start + (q + 1) * quarter, :] = repeat_slot(source[...], q)
    pool[4 * count + 2 * width :, :] = jnp.zeros((8, LANES), jnp.float32)

    def pick(f, base, first):
        lanes = slice(f * SLOT, (f + 1) * SLOT)
        rows = [pool[pl.ds(links[first + u], 1), lanes] for u in range(UNROLL)]
        for u in range(UNROLL):
            across[pl.ds(base + u, 1), lanes] = rows[u]

    for_faces(count, pick)
    faces = product(transposed, packed_extract(extract), 1, 1)
    trace = 0.5 * (faces + across[...])
    packed_lift = jnp.concatenate([pad_columns(lift[f], SLOT) for f in range(4)], axis=1)
    lifted = product(interior[...], coefs_ref[0] * state, 1, 0) + product(packed_lift, trace, 1, 1)
    result[...] = state + lifted


def call(kernel, width, outs, scratch, table, operands, name):
    vmem = pl.BlockSpec(memory_space=pltpu.VMEM)
    return pl.pallas_call(
        functools.partial(kernel, width),
        out_shape=[jax.ShapeDtypeStruct(shape, jnp.float32) for shape in outs],
        in_specs=[pl.BlockSpec(memory_space=pltpu.SMEM)] + [vmem] * len(operands),
        out_specs=[vmem] * len(outs),
        scratch_shapes=[pltpu.VMEM((rows, LANES), jnp.float32) for rows in scratch],
        compiler_params=pltpu.CompilerParams(vmem_limit_bytes=VMEM_LIMIT),
        name=name,
    )(table, *operands)


def around(to_prev, to_next, axis):
    devices = lax.axis_size(axis)
    up = [(i, (i + 1) % devices) for i in range(devices)]
    down = [(j, i) for i, j in up]
    return lax.ppermute(to_next, axis, up), lax.ppermute(to_prev, axis, down)


def from_behind(array, axis, by):
    devices = lax.axis_size(axis)
    pairs = [(i, i + by) for i in range(devices) if 0 <= i + by < devices]
    return lax.ppermute(array, axis, pairs)


def per_device(multipliers, coefficients, neighbours, send_list, interior, extract, lift):
    rows, count = multipliers.shape[1:]
    width = send_list.shape[0] // 2
    message = (width // 4, LANES)
    links = flat_links(neighbours)
    earlier = from_behind(multipliers[0], "tm", 1)
    partial, to_prev, to_next = call(
        adjoint_local,
        width,
        [(rows, count), message, message],
        [4 * count, 4 * count + 2 * width + 8],
        links,
        (multipliers, coefficients, interior, extract, lift),
        "adjoint_local",
    )
    from_prev, from_next = around(to_prev, to_next, "space")
    combined, to_prev, to_next = call(
        join_and_pick,
        width,
        [(rows, count), message, message],
        [2 * width, 4 * count, 4 * count],
        send_list,
        (partial, earlier, from_prev, from_next, extract),
        "join_and_pick",
    )
    later = from_behind(combined, "tm", -1)
    from_prev, from_next = around(to_prev, to_next, "space")
    (forward,) = call(
        tangent_rest,
        width,
        [(rows, count)],
        [4 * count + 2 * width + 8, count],
        links,
        (combined, coefficients, from_prev, from_next, interior, extract, lift),
        "tangent_rest",
    )
    return (forward - later)[None]


def solution(mesh):
    placed = (
        P(("groups", "tm"), None, "space"),
        P(("groups", "tm"), None, "space"),
        P(None, "space"),
        P("space"),
        P(),
        P(),
        P(),
    )
    return jax.shard_map(
        per_device,
        mesh=mesh,
        in_specs=placed,
        out_specs=P(("groups", "tm"), None, "space"),
        check_vma=False,
    )
```

```python
import functools

import jax
import jax.numpy as jnp
from jax import lax
from jax.experimental import pallas as pl
from jax.experimental.pallas import tpu as pltpu
from jax.sharding import PartitionSpec as P

LANES = 128
SLOT = 32
UNROLL = 16
VMEM_LIMIT = 48 * 1024 * 1024


def halves(value):
    high = value.astype(jnp.bfloat16)
    low = (value - high.astype(jnp.float32)).astype(jnp.bfloat16)
    return high, low


def product(left, right, left_dim, right_dim):
    dims = (((left_dim,), (right_dim,)), ((), ()))
    left_high, left_low = halves(left)
    right_high, right_low = halves(right)

    def one(a, b):
        return lax.dot_general(a, b, dims, preferred_element_type=jnp.float32)

    return one(left_high, right_high) + (one(left_high, right_low) + one(left_low, right_high))


def pad_rows(value, rows):
    missing = rows - value.shape[0]
    if missing == 0:
        return value
    return jnp.concatenate([value, jnp.zeros((missing, value.shape[1]), value.dtype)], axis=0)


def pad_columns(value, columns):
    missing = columns - value.shape[1]
    if missing == 0:
        return value
    return jnp.concatenate([value, jnp.zeros((value.shape[0], missing), value.dtype)], axis=1)


def slot_of_lane(shape):
    return lax.broadcasted_iota(jnp.int32, shape, 1) // SLOT


def choose_slots(blocks):
    slot = slot_of_lane(blocks[0].shape)
    result = blocks[0]
    for q in range(1, len(blocks)):
        result = jnp.where(slot == q, blocks[q], result)
    return result


def flat(ref):
    return ref.reshape(ref.shape[0], ref.shape[2])


def repeat_slot(block, q):
    only = jnp.where(slot_of_lane(block.shape) == q, block, 0.0)
    twice = only + pltpu.roll(only, SLOT, 1)
    return twice + pltpu.roll(twice, 2 * SLOT, 1)


def for_rows(count, step):
    def body(i, carry):
        base = i * UNROLL
        step(base)
        return carry

    lax.fori_loop(0, count // UNROLL, body, 0)


def flat_links(neighbours):
    count = neighbours.shape[1]
    return neighbours.reshape(4, count // LANES, LANES).transpose(1, 0, 2).reshape(-1)


def for_faces(count, step):
    groups = LANES // UNROLL

    def body(i, carry):
        block, inside = i // groups, (i % groups) * UNROLL
        for f in range(4):
            step(f, block * LANES + inside, block * (4 * LANES) + f * LANES + inside)
        return carry

    lax.fori_loop(0, count // UNROLL, body, 0)


def face_tables(transposed, extract_ref, table, count):
    for f in range(4):
        padded = pad_rows(extract_ref[f], SLOT)
        repeated = jnp.concatenate([padded] * 4, axis=0)
        table[f * count : (f + 1) * count, :] = product(transposed, repeated, 1, 1)


def packed_extract(extract_ref):
    return jnp.concatenate([pad_rows(extract_ref[f], SLOT) for f in range(4)], axis=0)


def adjoint_local(width, links, state_ref, coefs_ref, interior, extract, lift, partial, to_prev, to_next, half, sums):
    count = state_ref.shape[2]
    state = state_ref[0]
    transposed = state.T
    half_rows, sums_rows = half, sums
    half, sums = flat(half), flat(sums)
    for f in range(4):
        slot = pad_columns(0.5 * lift[f], SLOT)
        half[f * count : (f + 1) * count, :] = product(transposed, jnp.concatenate([slot] * 4, axis=1), 1, 0)
    sums[...] = jnp.zeros_like(sums)

    def scatter(f, base, first):
        rows = [half_rows[f * count + base + u] for u in range(UNROLL)]
        for u in range(UNROLL):
            sums_rows[links[first + u]] = rows[u]

    for_faces(count, scatter)
    quarter = width // 4
    for out, start in ((to_prev, 4 * count), (to_next, 4 * count + width)):
        flat(out)[...] = choose_slots([sums[start + q * quarter : start + (q + 1) * quarter, :] for q in range(4)])
    dfaces = choose_slots(
        [half[f * count : (f + 1) * count, :] + sums[f * count : (f + 1) * count, :] for f in range(4)]
    )
    back = product(packed_extract(extract).T, dfaces, 1, 1)
    partial[...] = state + coefs_ref[0] * product(interior[...].T, state, 1, 0) + back


def join_and_pick(
    width, sends, partial, earlier, from_prev, from_next, extract, combined, to_prev, to_next, received, extra, faces
):
    count = partial.shape[1]
    quarter = width // 4
    received_rows, extra_rows, faces_rows = received, extra, faces
    received, extra, faces = flat(received), flat(extra), flat(faces)
    for source, start in ((from_prev, 0), (from_next, width)):
        for q in range(4):
            received[start + q * quarter : start + (q + 1) * quarter, :] = repeat_slot(flat(source)[...], q)
    extra[...] = jnp.zeros_like(extra)

    def scatter(base):
        rows = [received_rows[base + u] for u in range(UNROLL)]
        for u in range(UNROLL):
            extra_rows[sends[base + u]] = rows[u]

    for_rows(2 * width, scatter)
    dfaces = choose_slots([extra[f * count : (f + 1) * count, :] for f in range(4)])
    total = partial[...] - earlier[...] + product(packed_extract(extract).T, dfaces, 1, 1)
    combined[...] = total
    face_tables(total.T, extract, faces, count)
    for out, start in ((to_prev, 0), (to_next, width)):
        for q in range(4):
            lanes = slice(q * SLOT, (q + 1) * SLOT)

            def pick(base):
                first = start + q * quarter + base
                rows = [faces_rows[sends[first + u], :, lanes] for u in range(UNROLL)]
                for u in range(UNROLL):
                    out[base + u, :, lanes] = rows[u]

            for_rows(quarter, pick)


def tangent_rest(
    width, links, combined, coefs_ref, from_prev, from_next, interior, extract, lift, result, pool, across
):
    count = combined.shape[1]
    quarter = width // 4
    state = combined[...]
    pool_rows, across_rows = pool, across
    pool, across = flat(pool), flat(across)
    transposed = state.T
    face_tables(transposed, extract, pool, count)
    for source, start in ((from_prev, 4 * count), (from_next, 4 * count + width)):
        for q in range(4):
            pool[start + q * quarter : start + (q + 1) * quarter, :] = repeat_slot(flat(source)[...], q)
    pool[4 * count + 2 * width :, :] = jnp.zeros((8, LANES), jnp.float32)

    def pick(f, base, first):
        lanes = slice(f * SLOT, (f + 1) * SLOT)
        rows = [pool_rows[links[first + u], :, lanes] for u in range(UNROLL)]
        for u in range(UNROLL):
            across_rows[base + u, :, lanes] = rows[u]

    for_faces(count, pick)
    faces = product(transposed, packed_extract(extract), 1, 1)
    trace = 0.5 * (faces + across[...])
    packed_lift = jnp.concatenate([pad_columns(lift[f], SLOT) for f in range(4)], axis=1)
    lifted = product(interior[...], coefs_ref[0] * state, 1, 0) + product(packed_lift, trace, 1, 1)
    result[...] = state + lifted


def call(kernel, width, outs, scratch, table, operands, name):
    vmem = pl.BlockSpec(memory_space=pltpu.VMEM)
    return pl.pallas_call(
        functools.partial(kernel, width),
        out_shape=[jax.ShapeDtypeStruct(shape, jnp.float32) for shape in outs],
        in_specs=[pl.BlockSpec(memory_space=pltpu.SMEM)] + [vmem] * len(operands),
        out_specs=[vmem] * len(outs),
        scratch_shapes=[pltpu.VMEM((rows, 1, LANES), jnp.float32) for rows in scratch],
        compiler_params=pltpu.CompilerParams(vmem_limit_bytes=VMEM_LIMIT),
        name=name,
    )(table, *operands)


def around(to_prev, to_next, axis):
    devices = lax.axis_size(axis)
    up = [(i, (i + 1) % devices) for i in range(devices)]
    down = [(j, i) for i, j in up]
    return lax.ppermute(to_next, axis, up), lax.ppermute(to_prev, axis, down)


def from_behind(array, axis, by):
    devices = lax.axis_size(axis)
    pairs = [(i, i + by) for i in range(devices) if 0 <= i + by < devices]
    return lax.ppermute(array, axis, pairs)


def per_device(multipliers, coefficients, neighbours, send_list, interior, extract, lift):
    rows, count = multipliers.shape[1:]
    width = send_list.shape[0] // 2
    message = (width // 4, 1, LANES)
    links = flat_links(neighbours)
    earlier = from_behind(multipliers[0], "tm", 1)
    partial, to_prev, to_next = call(
        adjoint_local,
        width,
        [(rows, count), message, message],
        [4 * count, 4 * count + 2 * width + 8],
        links,
        (multipliers, coefficients, interior, extract, lift),
        "adjoint_local",
    )
    from_prev, from_next = around(to_prev, to_next, "space")
    combined, to_prev, to_next = call(
        join_and_pick,
        width,
        [(rows, count), message, message],
        [2 * width, 4 * count, 4 * count],
        send_list,
        (partial, earlier, from_prev, from_next, extract),
        "join_and_pick",
    )
    later = from_behind(combined, "tm", -1)
    from_prev, from_next = around(to_prev, to_next, "space")
    (forward,) = call(
        tangent_rest,
        width,
        [(rows, count)],
        [4 * count + 2 * width + 8, count],
        links,
        (combined, coefficients, from_prev, from_next, interior, extract, lift),
        "tangent_rest",
    )
    return (forward - later)[None]


def solution(mesh):
    placed = (
        P(("groups", "tm"), None, "space"),
        P(("groups", "tm"), None, "space"),
        P(None, "space"),
        P("space"),
        P(),
        P(),
        P(),
    )
    return jax.shard_map(
        per_device,
        mesh=mesh,
        in_specs=placed,
        out_specs=P(("groups", "tm"), None, "space"),
        check_vma=False,
    )
```

```python
import functools

import jax
import jax.numpy as jnp
from jax import lax
from jax.experimental import pallas as pl
from jax.experimental.pallas import tpu as pltpu
from jax.sharding import PartitionSpec as P

LANES = 128
SLOT = 32
UNROLL = 32
SENDS_UNROLL = 64
VMEM_LIMIT = 48 * 1024 * 1024


def halves(value):
    high = value.astype(jnp.bfloat16)
    low = (value - high.astype(jnp.float32)).astype(jnp.bfloat16)
    return high, low


def product(left, right, left_dim, right_dim):
    dims = (((left_dim,), (right_dim,)), ((), ()))
    left_high, left_low = halves(left)
    right_high, right_low = halves(right)

    def one(a, b):
        return lax.dot_general(a, b, dims, preferred_element_type=jnp.float32)

    return one(left_high, right_high) + (one(left_high, right_low) + one(left_low, right_high))


def pad_rows(value, rows):
    missing = rows - value.shape[0]
    if missing == 0:
        return value
    return jnp.concatenate([value, jnp.zeros((missing, value.shape[1]), value.dtype)], axis=0)


def pad_columns(value, columns):
    missing = columns - value.shape[1]
    if missing == 0:
        return value
    return jnp.concatenate([value, jnp.zeros((value.shape[0], missing), value.dtype)], axis=1)


def slot_of_lane(shape):
    return lax.broadcasted_iota(jnp.int32, shape, 1) // SLOT


def choose_slots(blocks):
    slot = slot_of_lane(blocks[0].shape)
    result = blocks[0]
    for q in range(1, len(blocks)):
        result = jnp.where(slot == q, blocks[q], result)
    return result


def flat(ref):
    return ref.reshape(ref.shape[0], ref.shape[2])


def repeat_slot(block, q):
    only = jnp.where(slot_of_lane(block.shape) == q, block, 0.0)
    twice = only + pltpu.roll(only, SLOT, 1)
    return twice + pltpu.roll(twice, 2 * SLOT, 1)


def for_rows(count, step):
    def body(i, carry):
        base = i * SENDS_UNROLL
        step(base)
        return carry

    lax.fori_loop(0, count // SENDS_UNROLL, body, 0)


def flat_links(neighbours):
    count = neighbours.shape[1]
    return neighbours.reshape(4, count // LANES, LANES).transpose(1, 0, 2).reshape(-1)


def for_faces(count, step):
    groups = LANES // UNROLL

    def body(i, carry):
        block, inside = i // groups, (i % groups) * UNROLL
        for f in range(4):
            step(f, block * LANES + inside, block * (4 * LANES) + f * LANES + inside)
        return carry

    lax.fori_loop(0, count // UNROLL, body, 0)


def face_tables(transposed, extract_ref, table, count):
    for f in range(4):
        padded = pad_rows(extract_ref[f], SLOT)
        repeated = jnp.concatenate([padded] * 4, axis=0)
        table[f * count : (f + 1) * count, :] = product(transposed, repeated, 1, 1)


def packed_extract(extract_ref):
    return jnp.concatenate([pad_rows(extract_ref[f], SLOT) for f in range(4)], axis=0)


def adjoint_local(width, links, state_ref, coefs_ref, interior, extract, lift, partial, to_prev, to_next, half, sums):
    count = state_ref.shape[2]
    state = state_ref[0]
    transposed = state.T
    half_rows, sums_rows = half, sums
    half, sums = flat(half), flat(sums)
    for f in range(4):
        slot = pad_columns(0.5 * lift[f], SLOT)
        half[f * count : (f + 1) * count, :] = product(transposed, jnp.concatenate([slot] * 4, axis=1), 1, 0)
    sums[...] = jnp.zeros_like(sums)

    def scatter(f, base, first):
        rows = [half_rows[f * count + base + u] for u in range(UNROLL)]
        for u in range(UNROLL):
            sums_rows[links[first + u]] = rows[u]

    for_faces(count, scatter)
    quarter = width // 4
    for out, start in ((to_prev, 4 * count), (to_next, 4 * count + width)):
        flat(out)[...] = choose_slots([sums[start + q * quarter : start + (q + 1) * quarter, :] for q in range(4)])
    dfaces = choose_slots(
        [half[f * count : (f + 1) * count, :] + sums[f * count : (f + 1) * count, :] for f in range(4)]
    )
    back = product(packed_extract(extract).T, dfaces, 1, 1)
    partial[...] = state + coefs_ref[0] * product(interior[...].T, state, 1, 0) + back


def join_and_pick(
    width, sends, partial, earlier, from_prev, from_next, extract, combined, to_prev, to_next, received, extra, faces
):
    count = partial.shape[1]
    quarter = width // 4
    received_rows, extra_rows, faces_rows = received, extra, faces
    received, extra, faces = flat(received), flat(extra), flat(faces)
    for source, start in ((from_prev, 0), (from_next, width)):
        for q in range(4):
            received[start + q * quarter : start + (q + 1) * quarter, :] = repeat_slot(flat(source)[...], q)
    extra[...] = jnp.zeros_like(extra)

    def scatter(base):
        rows = [received_rows[base + u] for u in range(SENDS_UNROLL)]
        for u in range(SENDS_UNROLL):
            extra_rows[sends[base + u]] = rows[u]

    for_rows(2 * width, scatter)
    dfaces = choose_slots([extra[f * count : (f + 1) * count, :] for f in range(4)])
    total = partial[...] - earlier[...] + product(packed_extract(extract).T, dfaces, 1, 1)
    combined[...] = total
    face_tables(total.T, extract, faces, count)
    for out, start in ((to_prev, 0), (to_next, width)):
        for q in range(4):
            lanes = slice(q * SLOT, (q + 1) * SLOT)

            def pick(base):
                first = start + q * quarter + base
                rows = [faces_rows[sends[first + u], :, lanes] for u in range(SENDS_UNROLL)]
                for u in range(SENDS_UNROLL):
                    out[base + u, :, lanes] = rows[u]

            for_rows(quarter, pick)


def tangent_rest(
    width, links, combined, coefs_ref, from_prev, from_next, interior, extract, lift, result, pool, across
):
    count = combined.shape[1]
    quarter = width // 4
    state = combined[...]
    pool_rows, across_rows = pool, across
    pool, across = flat(pool), flat(across)
    transposed = state.T
    face_tables(transposed, extract, pool, count)
    for source, start in ((from_prev, 4 * count), (from_next, 4 * count + width)):
        for q in range(4):
            pool[start + q * quarter : start + (q + 1) * quarter, :] = repeat_slot(flat(source)[...], q)
    pool[4 * count + 2 * width :, :] = jnp.zeros((8, LANES), jnp.float32)

    def pick(f, base, first):
        lanes = slice(f * SLOT, (f + 1) * SLOT)
        rows = [pool_rows[links[first + u], :, lanes] for u in range(UNROLL)]
        for u in range(UNROLL):
            across_rows[base + u, :, lanes] = rows[u]

    for_faces(count, pick)
    faces = product(transposed, packed_extract(extract), 1, 1)
    trace = 0.5 * (faces + across[...])
    packed_lift = jnp.concatenate([pad_columns(lift[f], SLOT) for f in range(4)], axis=1)
    lifted = product(interior[...], coefs_ref[0] * state, 1, 0) + product(packed_lift, trace, 1, 1)
    result[...] = state + lifted


def call(kernel, width, outs, scratch, table, operands, name):
    vmem = pl.BlockSpec(memory_space=pltpu.VMEM)
    return pl.pallas_call(
        functools.partial(kernel, width),
        out_shape=[jax.ShapeDtypeStruct(shape, jnp.float32) for shape in outs],
        in_specs=[pl.BlockSpec(memory_space=pltpu.SMEM)] + [vmem] * len(operands),
        out_specs=[vmem] * len(outs),
        scratch_shapes=[pltpu.VMEM((rows, 1, LANES), jnp.float32) for rows in scratch],
        compiler_params=pltpu.CompilerParams(vmem_limit_bytes=VMEM_LIMIT),
        name=name,
    )(table, *operands)


def around(to_prev, to_next, axis):
    devices = lax.axis_size(axis)
    up = [(i, (i + 1) % devices) for i in range(devices)]
    down = [(j, i) for i, j in up]
    return lax.ppermute(to_next, axis, up), lax.ppermute(to_prev, axis, down)


def from_behind(array, axis, by):
    devices = lax.axis_size(axis)
    pairs = [(i, i + by) for i in range(devices) if 0 <= i + by < devices]
    return lax.ppermute(array, axis, pairs)


def per_device(multipliers, coefficients, neighbours, send_list, interior, extract, lift):
    rows, count = multipliers.shape[1:]
    width = send_list.shape[0] // 2
    message = (width // 4, 1, LANES)
    links = flat_links(neighbours)
    earlier = from_behind(multipliers[0], "tm", 1)
    partial, to_prev, to_next = call(
        adjoint_local,
        width,
        [(rows, count), message, message],
        [4 * count, 4 * count + 2 * width + 8],
        links,
        (multipliers, coefficients, interior, extract, lift),
        "adjoint_local",
    )
    from_prev, from_next = around(to_prev, to_next, "space")
    combined, to_prev, to_next = call(
        join_and_pick,
        width,
        [(rows, count), message, message],
        [2 * width, 4 * count, 4 * count],
        send_list,
        (partial, earlier, from_prev, from_next, extract),
        "join_and_pick",
    )
    later = from_behind(combined, "tm", -1)
    from_prev, from_next = around(to_prev, to_next, "space")
    (forward,) = call(
        tangent_rest,
        width,
        [(rows, count)],
        [4 * count + 2 * width + 8, count],
        links,
        (combined, coefficients, from_prev, from_next, interior, extract, lift),
        "tangent_rest",
    )
    return (forward - later)[None]


def solution(mesh):
    placed = (
        P(("groups", "tm"), None, "space"),
        P(("groups", "tm"), None, "space"),
        P(None, "space"),
        P("space"),
        P(),
        P(),
        P(),
    )
    return jax.shard_map(
        per_device,
        mesh=mesh,
        in_specs=placed,
        out_specs=P(("groups", "tm"), None, "space"),
        check_vma=False,
    )
```

```python
import functools

import jax
import jax.numpy as jnp
from jax import lax
from jax.experimental import pallas as pl
from jax.experimental.pallas import tpu as pltpu
from jax.sharding import PartitionSpec as P

LANES = 128
SLOT = 32
UNROLL = 32
VMEM_LIMIT = 48 * 1024 * 1024


def halves(value):
    high = value.astype(jnp.bfloat16)
    low = (value - high.astype(jnp.float32)).astype(jnp.bfloat16)
    return high, low


def product(left, right, left_dim, right_dim):
    dims = (((left_dim,), (right_dim,)), ((), ()))
    left_high, left_low = halves(left)
    right_high, right_low = halves(right)

    def one(a, b):
        return lax.dot_general(a, b, dims, preferred_element_type=jnp.float32)

    return one(left_high, right_high) + (one(left_high, right_low) + one(left_low, right_high))


def pad_rows(value, rows):
    missing = rows - value.shape[0]
    if missing == 0:
        return value
    return jnp.concatenate([value, jnp.zeros((missing, value.shape[1]), value.dtype)], axis=0)


def pad_columns(value, columns):
    missing = columns - value.shape[1]
    if missing == 0:
        return value
    return jnp.concatenate([value, jnp.zeros((value.shape[0], missing), value.dtype)], axis=1)


def slot_of_lane(shape):
    return lax.broadcasted_iota(jnp.int32, shape, 1) // SLOT


def choose_slots(blocks):
    slot = slot_of_lane(blocks[0].shape)
    result = blocks[0]
    for q in range(1, len(blocks)):
        result = jnp.where(slot == q, blocks[q], result)
    return result


def flat(ref):
    return ref.reshape(ref.shape[0], ref.shape[2])


def repeat_slot(block, q):
    only = jnp.where(slot_of_lane(block.shape) == q, block, 0.0)
    twice = only + pltpu.roll(only, SLOT, 1)
    return twice + pltpu.roll(twice, 2 * SLOT, 1)


def for_rows(count, step):
    together = min(count, 256)

    def body(i, carry):
        for inside in range(0, together, UNROLL):
            step(i * together + inside)
        return carry

    lax.fori_loop(0, count // together, body, 0)


def flat_links(neighbours):
    count = neighbours.shape[1]
    return neighbours.reshape(4, count // LANES, LANES).transpose(1, 0, 2).reshape(-1)


def for_faces(count, step):
    def body(block, carry):
        for f in range(4):
            for inside in range(0, LANES, UNROLL):
                step(f, block * LANES + inside, block * (4 * LANES) + f * LANES + inside)
        return carry

    lax.fori_loop(0, count // LANES, body, 0)


def face_tables(transposed, extract_ref, table, count):
    for f in range(4):
        padded = pad_rows(extract_ref[f], SLOT)
        repeated = jnp.concatenate([padded] * 4, axis=0)
        table[f * count : (f + 1) * count, :] = product(transposed, repeated, 1, 1)


def packed_extract(extract_ref):
    return jnp.concatenate([pad_rows(extract_ref[f], SLOT) for f in range(4)], axis=0)


def adjoint_local(width, links, state_ref, coefs_ref, interior, extract, lift, partial, to_prev, to_next, half, sums):
    count = state_ref.shape[2]
    state = state_ref[0]
    transposed = state.T
    half_rows, sums_rows = half, sums
    half, sums = flat(half), flat(sums)
    for f in range(4):
        slot = pad_columns(0.5 * lift[f], SLOT)
        half[f * count : (f + 1) * count, :] = product(transposed, jnp.concatenate([slot] * 4, axis=1), 1, 0)
    sums[...] = jnp.zeros_like(sums)

    def scatter(f, base, first):
        rows = [half_rows[f * count + base + u] for u in range(UNROLL)]
        for u in range(UNROLL):
            sums_rows[links[first + u]] = rows[u]

    for_faces(count, scatter)
    quarter = width // 4
    for out, start in ((to_prev, 4 * count), (to_next, 4 * count + width)):
        flat(out)[...] = choose_slots([sums[start + q * quarter : start + (q + 1) * quarter, :] for q in range(4)])
    dfaces = choose_slots(
        [half[f * count : (f + 1) * count, :] + sums[f * count : (f + 1) * count, :] for f in range(4)]
    )
    back = product(packed_extract(extract).T, dfaces, 1, 1)
    partial[...] = state + coefs_ref[0] * product(interior[...].T, state, 1, 0) + back


def join_and_pick(
    width, sends, partial, earlier, from_prev, from_next, extract, combined, to_prev, to_next, received, extra, faces
):
    count = partial.shape[1]
    quarter = width // 4
    received_rows, extra_rows, faces_rows = received, extra, faces
    received, extra, faces = flat(received), flat(extra), flat(faces)
    for source, start in ((from_prev, 0), (from_next, width)):
        for q in range(4):
            received[start + q * quarter : start + (q + 1) * quarter, :] = repeat_slot(flat(source)[...], q)
    extra[...] = jnp.zeros_like(extra)

    def scatter(base):
        rows = [received_rows[base + u] for u in range(UNROLL)]
        for u in range(UNROLL):
            extra_rows[sends[base + u]] = rows[u]

    for_rows(2 * width, scatter)
    dfaces = choose_slots([extra[f * count : (f + 1) * count, :] for f in range(4)])
    total = partial[...] - earlier[...] + product(packed_extract(extract).T, dfaces, 1, 1)
    combined[...] = total
    face_tables(total.T, extract, faces, count)
    for out, start in ((to_prev, 0), (to_next, width)):
        for q in range(4):
            lanes = slice(q * SLOT, (q + 1) * SLOT)

            def pick(base):
                first = start + q * quarter + base
                rows = [faces_rows[sends[first + u], :, lanes] for u in range(UNROLL)]
                for u in range(UNROLL):
                    out[base + u, :, lanes] = rows[u]

            for_rows(quarter, pick)


def tangent_rest(
    width, links, combined, coefs_ref, from_prev, from_next, interior, extract, lift, result, pool, across
):
    count = combined.shape[1]
    quarter = width // 4
    state = combined[...]
    pool_rows, across_rows = pool, across
    pool, across = flat(pool), flat(across)
    transposed = state.T
    face_tables(transposed, extract, pool, count)
    for source, start in ((from_prev, 4 * count), (from_next, 4 * count + width)):
        for q in range(4):
            pool[start + q * quarter : start + (q + 1) * quarter, :] = repeat_slot(flat(source)[...], q)
    pool[4 * count + 2 * width :, :] = jnp.zeros((8, LANES), jnp.float32)

    def pick(f, base, first):
        lanes = slice(f * SLOT, (f + 1) * SLOT)
        rows = [pool_rows[links[first + u], :, lanes] for u in range(UNROLL)]
        for u in range(UNROLL):
            across_rows[base + u, :, lanes] = rows[u]

    for_faces(count, pick)
    faces = product(transposed, packed_extract(extract), 1, 1)
    trace = 0.5 * (faces + across[...])
    packed_lift = jnp.concatenate([pad_columns(lift[f], SLOT) for f in range(4)], axis=1)
    lifted = product(interior[...], coefs_ref[0] * state, 1, 0) + product(packed_lift, trace, 1, 1)
    result[...] = state + lifted


def call(kernel, width, outs, scratch, table, operands, name):
    vmem = pl.BlockSpec(memory_space=pltpu.VMEM)
    return pl.pallas_call(
        functools.partial(kernel, width),
        out_shape=[jax.ShapeDtypeStruct(shape, jnp.float32) for shape in outs],
        in_specs=[pl.BlockSpec(memory_space=pltpu.SMEM)] + [vmem] * len(operands),
        out_specs=[vmem] * len(outs),
        scratch_shapes=[pltpu.VMEM((rows, 1, LANES), jnp.float32) for rows in scratch],
        compiler_params=pltpu.CompilerParams(vmem_limit_bytes=VMEM_LIMIT),
        name=name,
    )(table, *operands)


def around(to_prev, to_next, axis):
    devices = lax.axis_size(axis)
    up = [(i, (i + 1) % devices) for i in range(devices)]
    down = [(j, i) for i, j in up]
    return lax.ppermute(to_next, axis, up), lax.ppermute(to_prev, axis, down)


def from_behind(array, axis, by):
    devices = lax.axis_size(axis)
    pairs = [(i, i + by) for i in range(devices) if 0 <= i + by < devices]
    return lax.ppermute(array, axis, pairs)


def per_device(multipliers, coefficients, neighbours, send_list, interior, extract, lift):
    rows, count = multipliers.shape[1:]
    width = send_list.shape[0] // 2
    message = (width // 4, 1, LANES)
    links = flat_links(neighbours)
    earlier = from_behind(multipliers[0], "tm", 1)
    partial, to_prev, to_next = call(
        adjoint_local,
        width,
        [(rows, count), message, message],
        [4 * count, 4 * count + 2 * width + 8],
        links,
        (multipliers, coefficients, interior, extract, lift),
        "adjoint_local",
    )
    from_prev, from_next = around(to_prev, to_next, "space")
    combined, to_prev, to_next = call(
        join_and_pick,
        width,
        [(rows, count), message, message],
        [2 * width, 4 * count, 4 * count],
        send_list,
        (partial, earlier, from_prev, from_next, extract),
        "join_and_pick",
    )
    later = from_behind(combined, "tm", -1)
    from_prev, from_next = around(to_prev, to_next, "space")
    (forward,) = call(
        tangent_rest,
        width,
        [(rows, count)],
        [4 * count + 2 * width + 8, count],
        links,
        (combined, coefficients, from_prev, from_next, interior, extract, lift),
        "tangent_rest",
    )
    return (forward - later)[None]


def solution(mesh):
    placed = (
        P(("groups", "tm"), None, "space"),
        P(("groups", "tm"), None, "space"),
        P(None, "space"),
        P("space"),
        P(),
        P(),
        P(),
    )
    return jax.shard_map(
        per_device,
        mesh=mesh,
        in_specs=placed,
        out_specs=P(("groups", "tm"), None, "space"),
        check_vma=False,
    )
```

```python
import functools

import jax
import jax.numpy as jnp
from jax import lax
from jax.experimental import pallas as pl
from jax.experimental.pallas import tpu as pltpu
from jax.sharding import PartitionSpec as P

LANES = 128
SLOT = 32
DEPTH = 64
UNROLL = 32
VMEM_LIMIT = 32 * 1024 * 1024


def pad_rows(value, rows):
    missing = rows - value.shape[0]
    if missing == 0:
        return value
    return jnp.concatenate([value, jnp.zeros((missing, value.shape[1]), value.dtype)], axis=0)


def pad_columns(value, columns):
    missing = columns - value.shape[1]
    if missing == 0:
        return value
    return jnp.concatenate([value, jnp.zeros((value.shape[0], missing), value.dtype)], axis=1)


def halves(value):
    high = value.astype(jnp.bfloat16)
    low = (value - high.astype(jnp.float32)).astype(jnp.bfloat16)
    return high, low


def dot(left, right, left_dim, right_dim):
    dims = (((left_dim,), (right_dim,)), ((), ()))
    return lax.dot_general(left, right, dims, preferred_element_type=jnp.float32)


def stacked_field(field):
    high, low = halves(pad_rows(field, DEPTH))
    return jnp.concatenate([high, low, high], axis=0)


def stacked_factor(matrix, axis):
    padded = pad_rows(matrix, DEPTH) if axis == 0 else pad_columns(matrix, DEPTH)
    high, low = halves(padded)
    return jnp.concatenate([high, high, low], axis=axis)


def from_rows(matrix, table):
    rows = matrix.shape[0]
    high, low = halves(pad_rows(matrix, DEPTH))
    left = jnp.concatenate(
        [jnp.concatenate([high, high], axis=1), jnp.concatenate([low, jnp.zeros_like(low)], axis=1)], axis=0
    )
    both = dot(left, jnp.concatenate(halves(table), axis=1), 1, 1)
    return (both[:DEPTH] + both[DEPTH:])[:rows]


def slot_of_lane(shape):
    return lax.broadcasted_iota(jnp.int32, shape, 1) // SLOT


def choose_slots(blocks):
    slot = slot_of_lane(blocks[0].shape)
    result = blocks[0]
    for q in range(1, len(blocks)):
        result = jnp.where(slot == q, blocks[q], result)
    return result


def repeat_slot(block, q):
    only = jnp.where(slot_of_lane(block.shape) == q, block, 0.0)
    twice = only + pltpu.roll(only, SLOT, 1)
    return twice + pltpu.roll(twice, 2 * SLOT, 1)


def flat(ref):
    return ref.reshape(ref.shape[0], ref.shape[2])


def load_field(ref, rows):
    tiles = ref.shape[0] // rows
    return jnp.concatenate([ref[pl.ds(t, rows, stride=tiles), :] for t in range(tiles)], axis=1)


def store_field(ref, field):
    rows, count = field.shape
    tiles = count // LANES
    for t in range(tiles):
        ref[pl.ds(t, rows, stride=tiles), :] = field[:, t * LANES : (t + 1) * LANES]


def for_rows(count, step):
    together = min(count, 256)

    def body(i, carry):
        for inside in range(0, together, UNROLL):
            step(i * together + inside)
        return carry

    lax.fori_loop(0, count // together, body, 0)


def flat_links(neighbours):
    count = neighbours.shape[1]
    return neighbours.reshape(4, count // LANES, LANES).transpose(1, 0, 2).reshape(-1)


def for_faces(count, step):
    def body(block, carry):
        for f in range(4):
            for inside in range(0, LANES, UNROLL):
                step(f, block * LANES + inside, block * (4 * LANES) + f * LANES + inside)
        return carry

    lax.fori_loop(0, count // LANES, body, 0)


def packed_extract(extract):
    return jnp.concatenate([pad_rows(extract[f], SLOT) for f in range(4)], axis=0)


def packed_lift(lift):
    return jnp.concatenate([pad_columns(0.5 * lift[f], SLOT) for f in range(4)], axis=1)


def adjoint_sums(width, links, multipliers, lift, half_rows, sums_rows, to_prev, to_next):
    rows = lift.shape[1]
    count = half_rows.shape[0] // 4
    quarter = width // 4
    half, sums = flat(half_rows), flat(sums_rows)
    transposed = stacked_field(load_field(multipliers, rows)).T
    for f in range(4):
        slot = pad_columns(0.5 * lift[f], SLOT)
        factor = stacked_factor(jnp.concatenate([slot] * 4, axis=1), 0)
        half[f * count : (f + 1) * count, :] = dot(transposed, factor, 1, 0)
    sums[...] = jnp.zeros(sums.shape, jnp.float32)

    def scatter(f, base, first):
        rows = [half_rows[f * count + base + u] for u in range(UNROLL)]
        for u in range(UNROLL):
            sums_rows[links[first + u]] = rows[u]

    for_faces(count, scatter)
    for out, start in ((to_prev, 4 * count), (to_next, 4 * count + width)):
        flat(out)[...] = choose_slots([sums[start + q * quarter : start + (q + 1) * quarter, :] for q in range(4)])


def adjoint_inner(multipliers, coefficients, half_rows, sums_rows, interior, extract, partial):
    rows, count = partial.shape
    half, sums = flat(half_rows), flat(sums_rows)
    state = load_field(multipliers, rows)
    coefs = load_field(coefficients, rows)
    dfaces = choose_slots(
        [half[f * count : (f + 1) * count, :] + sums[f * count : (f + 1) * count, :] for f in range(4)]
    )
    inner = dot(stacked_factor(interior[...].T, 1), stacked_field(state), 1, 0)
    partial[...] = state + coefs * inner[:rows] + from_rows(packed_extract(extract).T, dfaces)


def join_and_pick(
    width,
    sends,
    partial,
    earlier,
    from_prev,
    from_next,
    extract,
    combined,
    to_prev,
    to_next,
    pool_rows,
    received_rows,
    extra_rows,
):
    rows, count = partial.shape
    quarter = width // 4
    received, extra, pool = flat(received_rows), flat(extra_rows), flat(pool_rows)
    for source, start in ((from_prev, 0), (from_next, width)):
        for q in range(4):
            received[start + q * quarter : start + (q + 1) * quarter, :] = repeat_slot(flat(source)[...], q)
    extra[...] = jnp.zeros(extra.shape, jnp.float32)

    def scatter(base):
        rows = [received_rows[base + u] for u in range(UNROLL)]
        for u in range(UNROLL):
            extra_rows[sends[base + u]] = rows[u]

    for_rows(2 * width, scatter)
    dfaces = choose_slots([extra[f * count : (f + 1) * count, :] for f in range(4)])
    total = partial[...] - load_field(earlier, rows) + from_rows(packed_extract(extract).T, dfaces)
    store_field(combined, total)
    transposed = stacked_field(total).T
    for f in range(4):
        factor = stacked_factor(jnp.concatenate([pad_rows(extract[f], SLOT)] * 4, axis=0).T, 0)
        pool[f * count : (f + 1) * count, :] = dot(transposed, factor, 1, 0)
    pool[4 * count + 2 * width :, :] = jnp.zeros((8, LANES), jnp.float32)
    for out, start in ((to_prev, 0), (to_next, width)):
        for q in range(4):
            lanes = slice(q * SLOT, (q + 1) * SLOT)

            def pick(base):
                first = start + q * quarter + base
                rows = [pool_rows[sends[first + u], :, lanes] for u in range(UNROLL)]
                for u in range(UNROLL):
                    out[base + u, :, lanes] = rows[u]

            for_rows(quarter, pick)


def tangent_inner(combined, coefficients, interior, extract, lift, base):
    rows, count = base.shape
    state = load_field(combined, rows)
    scaled = load_field(coefficients, rows) * state
    inner = dot(stacked_factor(interior[...], 1), stacked_field(scaled), 1, 0)
    faces = dot(stacked_field(state).T, stacked_factor(packed_extract(extract).T, 0), 1, 0)
    base[...] = state + inner[:rows] + from_rows(packed_lift(lift), faces)


def tangent_across(width, links, base, pool_in, from_prev, from_next, lift, forward, pool_rows, across_rows):
    del pool_in
    count = base.shape[1]
    quarter = width // 4
    pool = flat(pool_rows)
    for source, start in ((from_prev, 4 * count), (from_next, 4 * count + width)):
        for q in range(4):
            pool[start + q * quarter : start + (q + 1) * quarter, :] = repeat_slot(flat(source)[...], q)

    def pick(f, base, first):
        lanes = slice(f * SLOT, (f + 1) * SLOT)
        rows = [pool_rows[links[first + u], :, lanes] for u in range(UNROLL)]
        for u in range(UNROLL):
            across_rows[base + u, :, lanes] = rows[u]

    for_faces(count, pick)
    store_field(forward, base[...] + from_rows(packed_lift(lift), flat(across_rows)[...]))


def call(kernel, name, outs, table, operands, scratch=(), aliases=None, flops=0):
    vmem = pl.BlockSpec(memory_space=pltpu.VMEM)
    tables = [] if table is None else [table]
    return pl.pallas_call(
        kernel,
        out_shape=[jax.ShapeDtypeStruct(shape, jnp.float32) for shape in outs],
        in_specs=[pl.BlockSpec(memory_space=pltpu.SMEM)] * len(tables) + [vmem] * len(operands),
        out_specs=[vmem] * len(outs),
        scratch_shapes=[pltpu.VMEM((rows, 1, LANES), jnp.float32) for rows in scratch],
        input_output_aliases=aliases or {},
        compiler_params=pltpu.CompilerParams(vmem_limit_bytes=VMEM_LIMIT),
        cost_estimate=pl.CostEstimate(flops=flops, bytes_accessed=0, transcendentals=0),
        name=name,
    )(*tables, *operands)


def around(to_prev, to_next, axis):
    devices = lax.axis_size(axis)
    up = [(i, (i + 1) % devices) for i in range(devices)]
    down = [(j, i) for i, j in up]
    return lax.ppermute(to_next, axis, up), lax.ppermute(to_prev, axis, down)


def from_behind(array, axis, by):
    devices = lax.axis_size(axis)
    pairs = [(i, i + by) for i in range(devices) if 0 <= i + by < devices]
    return lax.ppermute(array, axis, pairs)


def per_device(multipliers, coefficients, neighbours, send_list, interior, extract, lift):
    rows, count = multipliers.shape[1:]
    width = send_list.shape[0] // 2
    lines = (rows * count // LANES, LANES)
    message = (width // 4, 1, LANES)
    face_rows = (4 * count, 1, LANES)
    pool_rows = (4 * count + 2 * width + 8, 1, LANES)
    own = multipliers.reshape(lines)
    coefs = coefficients.reshape(lines)
    links = flat_links(neighbours)
    earlier = from_behind(own, "tm", 1)
    half, sums, to_prev, to_next = call(
        functools.partial(adjoint_sums, width),
        "adjoint_sums",
        [face_rows, pool_rows, message, message],
        links,
        (own, lift),
        flops=10**10,
    )
    from_prev, from_next = around(to_prev, to_next, "space")
    (partial,) = call(
        adjoint_inner,
        "adjoint_inner",
        [(rows, count)],
        None,
        (own, coefs, half, sums, interior, extract),
        flops=2 * 10**9,
    )
    combined, to_prev, to_next, pool = call(
        functools.partial(join_and_pick, width),
        "join_and_pick",
        [lines, message, message, pool_rows],
        send_list,
        (partial, earlier, from_prev, from_next, extract),
        scratch=(2 * width, 4 * count),
        flops=7 * 10**9,
    )
    later = from_behind(combined, "tm", -1)
    from_prev, from_next = around(to_prev, to_next, "space")
    (base,) = call(
        tangent_inner,
        "tangent_inner",
        [(rows, count)],
        None,
        (combined, coefs, interior, extract, lift),
        flops=2 * 10**9,
    )
    forward, _ = call(
        functools.partial(tangent_across, width),
        "tangent_across",
        [lines, pool_rows],
        links,
        (base, pool, from_prev, from_next, lift),
        scratch=(count,),
        aliases={2: 1},
        flops=9 * 10**9,
    )
    return (forward - later).reshape(1, rows, count)


def solution(mesh):
    placed = (
        P(("groups", "tm"), None, "space"),
        P(("groups", "tm"), None, "space"),
        P(None, "space"),
        P("space"),
        P(),
        P(),
        P(),
    )
    return jax.shard_map(
        per_device,
        mesh=mesh,
        in_specs=placed,
        out_specs=P(("groups", "tm"), None, "space"),
        check_vma=False,
    )
```

```python
import functools

import jax
import jax.numpy as jnp
from jax import lax
from jax.experimental import pallas as pl
from jax.experimental.pallas import tpu as pltpu
from jax.sharding import PartitionSpec as P

LANES = 128
SLOT = 32
DEPTH = 64
UNROLL = 32
VMEM_LIMIT = 32 * 1024 * 1024


def pad_rows(value, rows):
    missing = rows - value.shape[0]
    if missing == 0:
        return value
    return jnp.concatenate([value, jnp.zeros((missing, value.shape[1]), value.dtype)], axis=0)


def pad_columns(value, columns):
    missing = columns - value.shape[1]
    if missing == 0:
        return value
    return jnp.concatenate([value, jnp.zeros((value.shape[0], missing), value.dtype)], axis=1)


def halves(value):
    high = value.astype(jnp.bfloat16)
    low = (value - high.astype(jnp.float32)).astype(jnp.bfloat16)
    return high, low


def dot(left, right, left_dim, right_dim):
    dims = (((left_dim,), (right_dim,)), ((), ()))
    return lax.dot_general(left, right, dims, preferred_element_type=jnp.float32)


def stacked_field(field):
    high, low = halves(pad_rows(field, DEPTH))
    return jnp.concatenate([high, low, high], axis=0)


def stacked_factor(matrix, axis):
    padded = pad_rows(matrix, DEPTH) if axis == 0 else pad_columns(matrix, DEPTH)
    high, low = halves(padded)
    return jnp.concatenate([high, high, low], axis=axis)


def from_rows(matrix, table):
    rows = matrix.shape[0]
    high, low = halves(pad_rows(matrix, DEPTH))
    left = jnp.concatenate(
        [jnp.concatenate([high, high], axis=1), jnp.concatenate([low, jnp.zeros_like(low)], axis=1)], axis=0
    )
    both = dot(left, jnp.concatenate(halves(table), axis=1), 1, 1)
    return (both[:DEPTH] + both[DEPTH:])[:rows]


def slot_of_lane(shape):
    return lax.broadcasted_iota(jnp.int32, shape, 1) // SLOT


def choose_slots(blocks):
    slot = slot_of_lane(blocks[0].shape)
    result = blocks[0]
    for q in range(1, len(blocks)):
        result = jnp.where(slot == q, blocks[q], result)
    return result


def repeat_slot(block, q):
    only = jnp.where(slot_of_lane(block.shape) == q, block, 0.0)
    twice = only + pltpu.roll(only, SLOT, 1)
    return twice + pltpu.roll(twice, 2 * SLOT, 1)


def flat(ref):
    return ref.reshape(ref.shape[0], ref.shape[2])


def load_field(ref, rows):
    tiles = ref.shape[0] // rows
    return jnp.concatenate([ref[pl.ds(t, rows, stride=tiles), :] for t in range(tiles)], axis=1)


def store_field(ref, field):
    rows, count = field.shape
    tiles = count // LANES
    for t in range(tiles):
        ref[pl.ds(t, rows, stride=tiles), :] = field[:, t * LANES : (t + 1) * LANES]


def for_rows(count, step):
    together = min(count, 256)

    def body(i, carry):
        for inside in range(0, together, UNROLL):
            step(i * together + inside)
        return carry

    lax.fori_loop(0, count // together, body, 0)


def flat_links(neighbours):
    count = neighbours.shape[1]
    return neighbours.reshape(4, count // LANES, LANES).transpose(1, 0, 2).reshape(-1)


def for_faces(count, step):
    def body(block, carry):
        for f in range(4):
            for inside in range(0, LANES, UNROLL):
                step(f, block * LANES + inside, block * (4 * LANES) + f * LANES + inside)
        return carry

    lax.fori_loop(0, count // LANES, body, 0)


def packed(faces):
    return jnp.concatenate([pad_rows(faces[:, f, :], SLOT) for f in range(4)], axis=0)


def repeated(face):
    return stacked_factor(jnp.concatenate([pad_rows(face, SLOT)] * 4, axis=0).T, 0)


def stage(multipliers, copied, sums):
    copied[...] = multipliers[...]
    flat(sums)[...] = jnp.zeros((sums.shape[0], LANES), jnp.float32)


def adjoint_sums(width, links_in, multipliers, lift, sums_in, half_rows, sums_rows, to_prev, to_next, links, arrived):
    del sums_in
    fetch = pltpu.make_async_copy(links_in, links, arrived)
    fetch.start()
    rows = lift.shape[2]
    count = half_rows.shape[0] // 4
    quarter = width // 4
    half, sums = flat(half_rows), flat(sums_rows)
    transposed = stacked_field(load_field(multipliers, rows)).T
    for f in range(4):
        half[f * count : (f + 1) * count, :] = dot(transposed, repeated(0.5 * lift[:, f, :]), 1, 0)
    fetch.wait()

    def scatter(f, base, first):
        rows = [half_rows[f * count + base + u] for u in range(UNROLL)]
        for u in range(UNROLL):
            sums_rows[links[first + u]] = rows[u]

    for_faces(count, scatter)
    for out, start in ((to_prev, 4 * count), (to_next, 4 * count + width)):
        flat(out)[...] = choose_slots([sums[start + q * quarter : start + (q + 1) * quarter, :] for q in range(4)])


def adjoint_inner(multipliers, coefficients, half_rows, sums_rows, interior, extract, partial, extra_rows):
    rows, count = partial.shape
    half, sums = flat(half_rows), flat(sums_rows)
    state = load_field(multipliers, rows)
    coefs = load_field(coefficients, rows)
    dfaces = choose_slots(
        [half[f * count : (f + 1) * count, :] + sums[f * count : (f + 1) * count, :] for f in range(4)]
    )
    inner = dot(stacked_factor(interior[...].T, 1), stacked_field(state), 1, 0)
    partial[...] = state + coefs * inner[:rows] + from_rows(packed(extract).T, dfaces)
    flat(extra_rows)[...] = jnp.zeros((extra_rows.shape[0], LANES), jnp.float32)


def spread(first, width, sends, source, received_rows, extra_rows):
    quarter = width // 4
    for q in range(4):
        flat(received_rows)[q * quarter : (q + 1) * quarter, :] = repeat_slot(flat(source)[...], q)

    def scatter(base):
        rows = [received_rows[base + u] for u in range(UNROLL)]
        for u in range(UNROLL):
            extra_rows[sends[first + base + u]] = rows[u]

    for_rows(width, scatter)


def join_prev(width, sends_in, from_prev, extra_in, extra_rows, received_rows, sends, arrived):
    del extra_in
    fetch = pltpu.make_async_copy(sends_in, sends, arrived)
    fetch.start()
    fetch.wait()
    spread(0, width, sends, from_prev, received_rows, extra_rows)


def join_next(
    width,
    sends_in,
    partial,
    earlier,
    from_next,
    extra_in,
    extract,
    combined,
    to_prev,
    to_next,
    pool_rows,
    extra_rows,
    received_rows,
    sends,
    arrived,
):
    del extra_in
    fetch = pltpu.make_async_copy(sends_in, sends, arrived)
    fetch.start()
    rows, count = partial.shape
    quarter = width // 4
    extra, pool = flat(extra_rows), flat(pool_rows)
    pool[4 * count + 2 * width :, :] = jnp.zeros((8, LANES), jnp.float32)
    fetch.wait()
    spread(width, width, sends, from_next, received_rows, extra_rows)
    dfaces = choose_slots([extra[f * count : (f + 1) * count, :] for f in range(4)])
    total = partial[...] - load_field(earlier, rows) + from_rows(packed(extract).T, dfaces)
    store_field(combined, total)
    transposed = stacked_field(total).T
    for f in range(4):
        pool[f * count : (f + 1) * count, :] = dot(transposed, repeated(extract[:, f, :]), 1, 0)
    for out, start in ((to_prev, 0), (to_next, width)):
        for q in range(4):
            lanes = slice(q * SLOT, (q + 1) * SLOT)

            def pick(base):
                first = start + q * quarter + base
                rows = [pool_rows[sends[first + u], :, lanes] for u in range(UNROLL)]
                for u in range(UNROLL):
                    out[base + u, :, lanes] = rows[u]

            for_rows(quarter, pick)


def tangent_inner(combined, coefficients, interior, extract, lift, base):
    rows, count = base.shape
    state = load_field(combined, rows)
    scaled = load_field(coefficients, rows) * state
    inner = dot(stacked_factor(interior[...], 1), stacked_field(scaled), 1, 0)
    faces = dot(stacked_field(state).T, stacked_factor(packed(extract).T, 0), 1, 0)
    base[...] = state + inner[:rows] + from_rows(0.5 * packed(lift).T, faces)


def tangent_across(
    width, links_in, base, pool_in, from_prev, from_next, lift, forward, pool_rows, across_rows, links, arrived
):
    del pool_in
    fetch = pltpu.make_async_copy(links_in, links, arrived)
    fetch.start()
    count = base.shape[1]
    quarter = width // 4
    pool = flat(pool_rows)
    for source, start in ((from_prev, 4 * count), (from_next, 4 * count + width)):
        for q in range(4):
            pool[start + q * quarter : start + (q + 1) * quarter, :] = repeat_slot(flat(source)[...], q)
    fetch.wait()

    def pick(f, base, first):
        lanes = slice(f * SLOT, (f + 1) * SLOT)
        rows = [pool_rows[links[first + u], :, lanes] for u in range(UNROLL)]
        for u in range(UNROLL):
            across_rows[base + u, :, lanes] = rows[u]

    for_faces(count, pick)
    store_field(forward, base[...] + from_rows(0.5 * packed(lift).T, flat(across_rows)[...]))


def call(kernel, outs, operands, scratch=(), table=None, aliases=None, flops=0):
    outs = [out if isinstance(out, jax.ShapeDtypeStruct) else jax.ShapeDtypeStruct(out, jnp.float32) for out in outs]
    buffers = [pltpu.VMEM((rows, 1, LANES), jnp.float32) for rows in scratch]
    if table is not None:
        buffers += [pltpu.SMEM((table,), jnp.int32), pltpu.SemaphoreType.DMA]
    function = kernel.func if isinstance(kernel, functools.partial) else kernel
    return pl.pallas_call(
        kernel,
        out_shape=outs,
        in_specs=[pl.BlockSpec(memory_space=pltpu.VMEM)] * len(operands),
        out_specs=[pl.BlockSpec(memory_space=pltpu.VMEM)] * len(outs),
        scratch_shapes=buffers,
        input_output_aliases=aliases or {},
        compiler_params=pltpu.CompilerParams(vmem_limit_bytes=VMEM_LIMIT),
        cost_estimate=pl.CostEstimate(flops=flops * 10**9, bytes_accessed=0, transcendentals=0),
        name=function.__name__,
    )(*operands)


def around(to_prev, to_next, axis):
    devices = lax.axis_size(axis)
    up = [(i, (i + 1) % devices) for i in range(devices)]
    down = [(j, i) for i, j in up]
    return lax.ppermute(to_next, axis, up), lax.ppermute(to_prev, axis, down)


def from_behind(array, axis, by):
    devices = lax.axis_size(axis)
    pairs = [(i, i + by) for i in range(devices) if 0 <= i + by < devices]
    return lax.ppermute(array, axis, pairs)


def per_device(multipliers, coefficients, neighbours, send_list, interior, extract, lift):
    rows, count = multipliers.shape[1:]
    width = send_list.shape[0] // 2
    lines = (rows * count // LANES, LANES)
    message = (width // 4, 1, LANES)
    face_rows = (4 * count, 1, LANES)
    pool_rows = (4 * count + 2 * width + 8, 1, LANES)
    own = multipliers.reshape(lines)
    coefs = coefficients.reshape(lines)
    links = flat_links(neighbours)
    lift, extract = lift.transpose(2, 0, 1), extract.transpose(1, 0, 2)
    copied, sums = call(stage, [lines, pool_rows], (own,), flops=3)
    earlier = from_behind(copied, "tm", 1)
    half, sums, to_prev, to_next = call(
        functools.partial(adjoint_sums, width),
        [face_rows, pool_rows, message, message],
        (links, own, lift, sums),
        table=4 * count,
        aliases={3: 1},
        flops=9,
    )
    from_prev, from_next = around(to_prev, to_next, "space")
    partial, extra = call(
        adjoint_inner, [(rows, count), face_rows], (own, coefs, half, sums, interior, extract), flops=2
    )
    (extra,) = call(
        functools.partial(join_prev, width),
        [face_rows],
        (send_list, from_prev, extra),
        scratch=(width,),
        table=2 * width,
        aliases={2: 0},
        flops=1,
    )
    combined, to_prev, to_next, pool, _ = call(
        functools.partial(join_next, width),
        [lines, message, message, pool_rows, face_rows],
        (send_list, partial, earlier, from_next, extra, extract),
        scratch=(width,),
        table=2 * width,
        aliases={4: 4},
        flops=5,
    )
    later = from_behind(combined, "tm", -1)
    from_prev, from_next = around(to_prev, to_next, "space")
    (base,) = call(tangent_inner, [(rows, count)], (combined, coefs, interior, extract, lift), flops=2)
    forward, _ = call(
        functools.partial(tangent_across, width),
        [lines, pool_rows],
        (links, base, pool, from_prev, from_next, lift),
        scratch=(count,),
        table=4 * count,
        aliases={2: 1},
        flops=9,
    )
    return (forward - later).reshape(1, rows, count)


def solution(mesh):
    placed = (
        P(("groups", "tm"), None, "space"),
        P(("groups", "tm"), None, "space"),
        P(None, "space"),
        P("space"),
        P(),
        P(),
        P(),
    )
    return jax.shard_map(
        per_device,
        mesh=mesh,
        in_specs=placed,
        out_specs=P(("groups", "tm"), None, "space"),
        check_vma=False,
    )
```

```python
import functools

import jax
import jax.numpy as jnp
from jax import lax
from jax.experimental import pallas as pl
from jax.experimental.pallas import tpu as pltpu
from jax.sharding import PartitionSpec as P

LANES = 128
SLOT = 32
DEPTH = 64
UNROLL = 32
VMEM_LIMIT = 32 * 1024 * 1024


def pad_rows(value, rows):
    missing = rows - value.shape[0]
    if missing == 0:
        return value
    return jnp.concatenate([value, jnp.zeros((missing, value.shape[1]), value.dtype)], axis=0)


def pad_columns(value, columns):
    missing = columns - value.shape[1]
    if missing == 0:
        return value
    return jnp.concatenate([value, jnp.zeros((value.shape[0], missing), value.dtype)], axis=1)


def halves(value):
    high = value.astype(jnp.bfloat16)
    low = (value - high.astype(jnp.float32)).astype(jnp.bfloat16)
    return high, low


def dot(left, right, left_dim, right_dim):
    dims = (((left_dim,), (right_dim,)), ((), ()))
    return lax.dot_general(left, right, dims, preferred_element_type=jnp.float32)


def stacked_field(field):
    high, low = halves(pad_rows(field, DEPTH))
    return jnp.concatenate([high, low, high], axis=0)


def stacked_factor(matrix, axis):
    padded = pad_rows(matrix, DEPTH) if axis == 0 else pad_columns(matrix, DEPTH)
    high, low = halves(padded)
    return jnp.concatenate([high, high, low], axis=axis)


def from_rows(matrix, table):
    rows = matrix.shape[0]
    high, low = halves(pad_rows(matrix, DEPTH))
    left = jnp.concatenate(
        [jnp.concatenate([high, high], axis=1), jnp.concatenate([low, jnp.zeros_like(low)], axis=1)], axis=0
    )
    both = dot(left, jnp.concatenate(halves(table), axis=1), 1, 1)
    return (both[:DEPTH] + both[DEPTH:])[:rows]


def slot_of_lane(shape):
    return lax.broadcasted_iota(jnp.int32, shape, 1) // SLOT


def choose_slots(blocks):
    slot = slot_of_lane(blocks[0].shape)
    result = blocks[0]
    for q in range(1, len(blocks)):
        result = jnp.where(slot == q, blocks[q], result)
    return result


def repeat_slot(block, q):
    only = jnp.where(slot_of_lane(block.shape) == q, block, 0.0)
    twice = only + pltpu.roll(only, SLOT, 1)
    return twice + pltpu.roll(twice, 2 * SLOT, 1)


def flat(ref):
    return ref.reshape(ref.shape[0], ref.shape[2])


def load_field(ref, rows):
    tiles = ref.shape[0] // rows
    return jnp.concatenate([ref[pl.ds(t, rows, stride=tiles), :] for t in range(tiles)], axis=1)


def store_field(ref, field):
    rows, count = field.shape
    tiles = count // LANES
    for t in range(tiles):
        ref[pl.ds(t, rows, stride=tiles), :] = field[:, t * LANES : (t + 1) * LANES]


def for_rows(count, step):
    together = min(count, 256)

    def body(i, carry):
        for inside in range(0, together, UNROLL):
            step(i * together + inside)
        return carry

    lax.fori_loop(0, count // together, body, 0)


def flat_links(neighbours):
    count = neighbours.shape[1]
    return neighbours.reshape(4, count // LANES, LANES).transpose(1, 0, 2).reshape(-1)


def for_faces(count, step):
    def body(block, carry):
        for f in range(4):
            for inside in range(0, LANES, UNROLL):
                step(f, block * LANES + inside, block * (4 * LANES) + f * LANES + inside)
        return carry

    lax.fori_loop(0, count // LANES, body, 0)


def packed(faces):
    return jnp.concatenate([pad_rows(faces[:, f, :], SLOT) for f in range(4)], axis=0)


def repeated(face):
    return stacked_factor(jnp.concatenate([pad_rows(face, SLOT)] * 4, axis=0).T, 0)


def near_half(width):
    return (1 - lax.axis_index("space") % 2) * width


def unpack(source, target, first):
    quarter = source.shape[0]
    for q in range(4):
        start = pl.multiple_of(first + q * quarter, quarter)
        target[pl.ds(start, quarter), :] = repeat_slot(flat(source)[...], q)


def stage(multipliers, copied, sums):
    copied[...] = multipliers[...]
    flat(sums)[...] = jnp.zeros((sums.shape[0], LANES), jnp.float32)


def adjoint_sums(width, links_in, multipliers, lift, sums_in, half_rows, sums_rows, to_near, to_far, links, arrived):
    del sums_in
    fetch = pltpu.make_async_copy(links_in, links, arrived)
    fetch.start()
    rows = lift.shape[2]
    count = half_rows.shape[0] // 4
    quarter = width // 4
    half, sums = flat(half_rows), flat(sums_rows)
    transposed = stacked_field(load_field(multipliers, rows)).T
    for f in range(4):
        half[f * count : (f + 1) * count, :] = dot(transposed, repeated(0.5 * lift[:, f, :]), 1, 0)
    fetch.wait()

    def scatter(f, base, first):
        rows = [half_rows[f * count + base + u] for u in range(UNROLL)]
        for u in range(UNROLL):
            sums_rows[links[first + u]] = rows[u]

    for_faces(count, scatter)
    near = near_half(width)
    for out, place in ((to_near, near), (to_far, width - near)):
        starts = [pl.multiple_of(4 * count + place + q * quarter, quarter) for q in range(4)]
        flat(out)[...] = choose_slots([sums[pl.ds(start, quarter), :] for start in starts])


def adjoint_inner(multipliers, coefficients, half_rows, sums_rows, interior, extract, partial, extra_rows):
    rows, count = partial.shape
    half, sums = flat(half_rows), flat(sums_rows)
    state = load_field(multipliers, rows)
    coefs = load_field(coefficients, rows)
    dfaces = choose_slots(
        [half[f * count : (f + 1) * count, :] + sums[f * count : (f + 1) * count, :] for f in range(4)]
    )
    inner = dot(stacked_factor(interior[...].T, 1), stacked_field(state), 1, 0)
    partial[...] = state + coefs * inner[:rows] + from_rows(packed(extract).T, dfaces)
    flat(extra_rows)[...] = jnp.zeros((extra_rows.shape[0], LANES), jnp.float32)


def spread(first, width, sends, received_rows, extra_rows):
    def scatter(base):
        rows = [received_rows[base + u] for u in range(UNROLL)]
        for u in range(UNROLL):
            extra_rows[sends[first + base + u]] = rows[u]

    for_rows(width, scatter)


def join_near(width, sends_in, from_near, extra_in, extra_rows, received_rows, sends, arrived):
    del extra_in
    fetch = pltpu.make_async_copy(sends_in, sends, arrived)
    fetch.start()
    unpack(from_near, flat(received_rows), 0)
    fetch.wait()
    spread(near_half(width), width, sends, received_rows, extra_rows)


def join_far(
    width,
    sends_in,
    partial,
    earlier,
    from_far,
    extra_in,
    extract,
    combined,
    to_near,
    to_far,
    pool_rows,
    extra_rows,
    received_rows,
    sends,
    arrived,
):
    del extra_in
    fetch = pltpu.make_async_copy(sends_in, sends, arrived)
    fetch.start()
    rows, count = partial.shape
    quarter = width // 4
    extra, pool = flat(extra_rows), flat(pool_rows)
    pool[4 * count + 2 * width :, :] = jnp.zeros((8, LANES), jnp.float32)
    unpack(from_far, flat(received_rows), 0)
    near = near_half(width)
    fetch.wait()
    spread(width - near, width, sends, received_rows, extra_rows)
    dfaces = choose_slots([extra[f * count : (f + 1) * count, :] for f in range(4)])
    total = partial[...] - load_field(earlier, rows) + from_rows(packed(extract).T, dfaces)
    store_field(combined, total)
    transposed = stacked_field(total).T
    for f in range(4):
        pool[f * count : (f + 1) * count, :] = dot(transposed, repeated(extract[:, f, :]), 1, 0)
    for out, start in ((to_near, near), (to_far, width - near)):
        for q in range(4):
            lanes = slice(q * SLOT, (q + 1) * SLOT)

            def pick(base):
                first = start + q * quarter + base
                rows = [pool_rows[sends[first + u], :, lanes] for u in range(UNROLL)]
                for u in range(UNROLL):
                    out[base + u, :, lanes] = rows[u]

            for_rows(quarter, pick)


def tangent_inner(combined, coefficients, interior, extract, lift, base):
    rows, count = base.shape
    state = load_field(combined, rows)
    scaled = load_field(coefficients, rows) * state
    inner = dot(stacked_factor(interior[...], 1), stacked_field(scaled), 1, 0)
    faces = dot(stacked_field(state).T, stacked_factor(packed(extract).T, 0), 1, 0)
    base[...] = state + inner[:rows] + from_rows(0.5 * packed(lift).T, faces)


def tangent_across(
    width, links_in, base, pool_in, from_near, from_far, lift, forward, pool_rows, across_rows, links, arrived
):
    del pool_in
    fetch = pltpu.make_async_copy(links_in, links, arrived)
    fetch.start()
    count = base.shape[1]
    near = near_half(width)
    unpack(from_near, flat(pool_rows), 4 * count + near)
    unpack(from_far, flat(pool_rows), 4 * count + width - near)
    fetch.wait()

    def pick(f, base, first):
        lanes = slice(f * SLOT, (f + 1) * SLOT)
        rows = [pool_rows[links[first + u], :, lanes] for u in range(UNROLL)]
        for u in range(UNROLL):
            across_rows[base + u, :, lanes] = rows[u]

    for_faces(count, pick)
    store_field(forward, base[...] + from_rows(0.5 * packed(lift).T, flat(across_rows)[...]))


def call(kernel, outs, operands, scratch=(), table=None, aliases=None, flops=0):
    outs = [out if isinstance(out, jax.ShapeDtypeStruct) else jax.ShapeDtypeStruct(out, jnp.float32) for out in outs]
    buffers = [pltpu.VMEM((rows, 1, LANES), jnp.float32) for rows in scratch]
    if table is not None:
        buffers += [pltpu.SMEM((table,), jnp.int32), pltpu.SemaphoreType.DMA]
    function = kernel.func if isinstance(kernel, functools.partial) else kernel
    return pl.pallas_call(
        kernel,
        out_shape=outs,
        in_specs=[pl.BlockSpec(memory_space=pltpu.VMEM)] * len(operands),
        out_specs=[pl.BlockSpec(memory_space=pltpu.VMEM)] * len(outs),
        scratch_shapes=buffers,
        input_output_aliases=aliases or {},
        compiler_params=pltpu.CompilerParams(vmem_limit_bytes=VMEM_LIMIT),
        cost_estimate=pl.CostEstimate(flops=flops * 10**9, bytes_accessed=0, transcendentals=0),
        name=function.__name__,
    )(*operands)


def exchange(to_near, to_far, axis):
    devices = lax.axis_size(axis)
    near = [(i, i ^ 1) for i in range(devices)]
    far = [(i, (i + (1 if i % 2 else -1)) % devices) for i in range(devices)]
    return lax.ppermute(to_near, axis, near), lax.ppermute(to_far, axis, far)


def from_behind(array, axis, by):
    devices = lax.axis_size(axis)
    pairs = [(i, i + by) for i in range(devices) if 0 <= i + by < devices]
    return lax.ppermute(array, axis, pairs)


def per_device(multipliers, coefficients, neighbours, send_list, interior, extract, lift):
    rows, count = multipliers.shape[1:]
    width = send_list.shape[0] // 2
    lines = (rows * count // LANES, LANES)
    message = (width // 4, 1, LANES)
    face_rows = (4 * count, 1, LANES)
    pool_rows = (4 * count + 2 * width + 8, 1, LANES)
    own = multipliers.reshape(lines)
    coefs = coefficients.reshape(lines)
    links = flat_links(neighbours)
    lift, extract = lift.transpose(2, 0, 1), extract.transpose(1, 0, 2)
    copied, sums = call(stage, [lines, pool_rows], (own,), flops=3)
    earlier = from_behind(copied, "tm", 1)
    half, sums, to_near, to_far = call(
        functools.partial(adjoint_sums, width),
        [face_rows, pool_rows, message, message],
        (links, own, lift, sums),
        table=4 * count,
        aliases={3: 1},
        flops=9,
    )
    from_near, from_far = exchange(to_near, to_far, "space")
    partial, extra = call(
        adjoint_inner, [(rows, count), face_rows], (own, coefs, half, sums, interior, extract), flops=2
    )
    (extra,) = call(
        functools.partial(join_near, width),
        [face_rows],
        (send_list, from_near, extra),
        scratch=(width,),
        table=2 * width,
        aliases={2: 0},
        flops=1,
    )
    combined, to_near, to_far, pool, _ = call(
        functools.partial(join_far, width),
        [lines, message, message, pool_rows, face_rows],
        (send_list, partial, earlier, from_far, extra, extract),
        scratch=(width,),
        table=2 * width,
        aliases={4: 4},
        flops=5,
    )
    later = from_behind(combined, "tm", -1)
    from_near, from_far = exchange(to_near, to_far, "space")
    (base,) = call(tangent_inner, [(rows, count)], (combined, coefs, interior, extract, lift), flops=2)
    forward, _ = call(
        functools.partial(tangent_across, width),
        [lines, pool_rows],
        (links, base, pool, from_near, from_far, lift),
        scratch=(count,),
        table=4 * count,
        aliases={2: 1},
        flops=9,
    )
    return (forward - later).reshape(1, rows, count)


def solution(mesh):
    placed = (
        P(("groups", "tm"), None, "space"),
        P(("groups", "tm"), None, "space"),
        P(None, "space"),
        P("space"),
        P(),
        P(),
        P(),
    )
    return jax.shard_map(
        per_device,
        mesh=mesh,
        in_specs=placed,
        out_specs=P(("groups", "tm"), None, "space"),
        check_vma=False,
    )
```

```python
import functools

import jax
import jax.numpy as jnp
from jax import lax
from jax.experimental import pallas as pl
from jax.experimental.pallas import tpu as pltpu
from jax.sharding import PartitionSpec as P

LANES = 128
SLOT = 32
DEPTH = 64
UNROLL = 32
VMEM_LIMIT = 32 * 1024 * 1024


def pad_rows(value, rows):
    missing = rows - value.shape[0]
    if missing == 0:
        return value
    return jnp.concatenate([value, jnp.zeros((missing, value.shape[1]), value.dtype)], axis=0)


def pad_columns(value, columns):
    missing = columns - value.shape[1]
    if missing == 0:
        return value
    return jnp.concatenate([value, jnp.zeros((value.shape[0], missing), value.dtype)], axis=1)


def halves(value):
    high = value.astype(jnp.bfloat16)
    low = (value - high.astype(jnp.float32)).astype(jnp.bfloat16)
    return high, low


def dot(left, right, left_dim, right_dim):
    dims = (((left_dim,), (right_dim,)), ((), ()))
    return lax.dot_general(left, right, dims, preferred_element_type=jnp.float32)


def stacked_field(field):
    high, low = halves(pad_rows(field, DEPTH))
    return jnp.concatenate([high, low, high], axis=0)


def stacked_factor(matrix, axis):
    padded = pad_rows(matrix, DEPTH) if axis == 0 else pad_columns(matrix, DEPTH)
    high, low = halves(padded)
    return jnp.concatenate([high, high, low], axis=axis)


def from_rows(matrix, table):
    rows = matrix.shape[0]
    high, low = halves(pad_rows(matrix, DEPTH))
    left = jnp.concatenate(
        [jnp.concatenate([high, high], axis=1), jnp.concatenate([low, jnp.zeros_like(low)], axis=1)], axis=0
    )
    both = dot(left, jnp.concatenate(halves(table), axis=1), 1, 1)
    return (both[:DEPTH] + both[DEPTH:])[:rows]


def slot_of_lane(shape):
    return lax.broadcasted_iota(jnp.int32, shape, 1) // SLOT


def choose_slots(blocks):
    slot = slot_of_lane(blocks[0].shape)
    result = blocks[0]
    for q in range(1, len(blocks)):
        result = jnp.where(slot == q, blocks[q], result)
    return result


def repeat_slot(block, q):
    only = jnp.where(slot_of_lane(block.shape) == q, block, 0.0)
    twice = only + pltpu.roll(only, SLOT, 1)
    return twice + pltpu.roll(twice, 2 * SLOT, 1)


def flat(ref):
    return ref.reshape(ref.shape[0], ref.shape[2])


def load_field(ref, rows):
    tiles = ref.shape[0] // rows
    return jnp.concatenate([ref[pl.ds(t, rows, stride=tiles), :] for t in range(tiles)], axis=1)


def store_field(ref, field):
    rows, count = field.shape
    tiles = count // LANES
    for t in range(tiles):
        ref[pl.ds(t, rows, stride=tiles), :] = field[:, t * LANES : (t + 1) * LANES]


def for_rows(count, step):
    together = min(count, 256)

    def body(i, carry):
        step(pl.multiple_of(i * together, together), together)
        return carry

    lax.fori_loop(0, count // together, body, 0)


def move(count, load, store):
    for first in range(0, count, UNROLL):
        rows = [load(u) for u in range(first, first + UNROLL)]
        for u in range(UNROLL):
            store(first + u, rows[u])


def flat_links(neighbours):
    count = neighbours.shape[1]
    return neighbours.reshape(4, count // LANES, LANES).transpose(1, 0, 2).reshape(-1)


def for_faces(count, links, step):
    def body(block, carry):
        first = pl.multiple_of(block * LANES, LANES)
        mine = links.at[pl.ds(pl.multiple_of(block * (4 * LANES), 4 * LANES), 4 * LANES)]
        for f in range(4):
            step(f, first, lambda u, f=f: mine[f * LANES + u])
        return carry

    lax.fori_loop(0, count // LANES, body, 0)


def packed(faces):
    return jnp.concatenate([pad_rows(faces[:, f, :], SLOT) for f in range(4)], axis=0)


def repeated(face):
    return stacked_factor(jnp.concatenate([pad_rows(face, SLOT)] * 4, axis=0).T, 0)


def near_half(width):
    return (1 - lax.axis_index("space") % 2) * width


def unpack(source, target, first):
    quarter = source.shape[0]
    for q in range(4):
        start = pl.multiple_of(first + q * quarter, quarter)
        target[pl.ds(start, quarter), :] = repeat_slot(flat(source)[...], q)


def clear(sums):
    flat(sums)[...] = jnp.zeros((sums.shape[0], LANES), jnp.float32)


def adjoint_sums(width, links_in, multipliers, lift, sums_in, half_rows, sums_rows, to_near, to_far, links, arrived):
    del sums_in
    fetch = pltpu.make_async_copy(links_in, links, arrived)
    fetch.start()
    rows = lift.shape[2]
    count = half_rows.shape[0] // 4
    quarter = width // 4
    half, sums = flat(half_rows), flat(sums_rows)
    transposed = stacked_field(load_field(multipliers, rows)).T
    for f in range(4):
        half[f * count : (f + 1) * count, :] = dot(transposed, repeated(0.5 * lift[:, f, :]), 1, 0)
    fetch.wait()

    def scatter(f, first, link):
        mine = half_rows.at[pl.ds(f * count + first, LANES)]

        def store(u, row):
            sums_rows[link(u)] = row

        move(LANES, lambda u: mine[u], store)

    for_faces(count, links, scatter)
    near = near_half(width)
    for out, place in ((to_near, near), (to_far, width - near)):
        starts = [pl.multiple_of(4 * count + place + q * quarter, quarter) for q in range(4)]
        flat(out)[...] = choose_slots([sums[pl.ds(start, quarter), :] for start in starts])


def adjoint_inner(multipliers, coefficients, half_rows, sums_rows, interior, extract, partial, extra_rows):
    rows, count = partial.shape
    half, sums = flat(half_rows), flat(sums_rows)
    state = load_field(multipliers, rows)
    coefs = load_field(coefficients, rows)
    dfaces = choose_slots(
        [half[f * count : (f + 1) * count, :] + sums[f * count : (f + 1) * count, :] for f in range(4)]
    )
    inner = dot(stacked_factor(interior[...].T, 1), stacked_field(state), 1, 0)
    partial[...] = state + coefs * inner[:rows] + from_rows(packed(extract).T, dfaces)
    flat(extra_rows)[...] = jnp.zeros((extra_rows.shape[0], LANES), jnp.float32)


def spread(first, width, sends, received_rows, extra_rows):
    def scatter(base, together):
        mine = received_rows.at[pl.ds(base, together)]
        places = sends.at[pl.ds(first + base, together)]

        def store(u, row):
            extra_rows[places[u]] = row

        move(together, lambda u: mine[u], store)

    for_rows(width, scatter)


def join_near(width, sends_in, from_near, extra_in, extra_rows, received_rows, sends, arrived):
    del extra_in
    fetch = pltpu.make_async_copy(sends_in, sends, arrived)
    fetch.start()
    unpack(from_near, flat(received_rows), 0)
    fetch.wait()
    spread(near_half(width), width, sends, received_rows, extra_rows)


def join_far(
    width,
    sends_in,
    partial,
    earlier,
    from_far,
    extra_in,
    extract,
    combined,
    to_near,
    to_far,
    pool_rows,
    extra_rows,
    received_rows,
    sends,
    arrived,
):
    del extra_in
    fetch = pltpu.make_async_copy(sends_in, sends, arrived)
    fetch.start()
    rows, count = partial.shape
    quarter = width // 4
    extra, pool = flat(extra_rows), flat(pool_rows)
    pool[4 * count + 2 * width :, :] = jnp.zeros((8, LANES), jnp.float32)
    unpack(from_far, flat(received_rows), 0)
    near = near_half(width)
    fetch.wait()
    spread(width - near, width, sends, received_rows, extra_rows)
    dfaces = choose_slots([extra[f * count : (f + 1) * count, :] for f in range(4)])
    total = partial[...] - load_field(earlier, rows) + from_rows(packed(extract).T, dfaces)
    store_field(combined, total)
    transposed = stacked_field(total).T
    for f in range(4):
        pool[f * count : (f + 1) * count, :] = dot(transposed, repeated(extract[:, f, :]), 1, 0)
    for out, start in ((to_near, near), (to_far, width - near)):
        for q in range(4):
            lanes = slice(q * SLOT, (q + 1) * SLOT)

            def pick(base, together):
                places = sends.at[pl.ds(start + q * quarter + base, together)]
                mine = out.at[pl.ds(base, together)]

                def store(u, row):
                    mine[u, :, lanes] = row

                move(together, lambda u: pool_rows[places[u], :, lanes], store)

            for_rows(quarter, pick)


def tangent_inner(combined, coefficients, interior, extract, lift, base):
    rows, count = base.shape
    state = load_field(combined, rows)
    scaled = load_field(coefficients, rows) * state
    inner = dot(stacked_factor(interior[...], 1), stacked_field(scaled), 1, 0)
    faces = dot(stacked_field(state).T, stacked_factor(packed(extract).T, 0), 1, 0)
    base[...] = state + inner[:rows] + from_rows(0.5 * packed(lift).T, faces)


def tangent_across(
    width, links_in, base, pool_in, from_near, from_far, lift, forward, pool_rows, across_rows, links, arrived
):
    del pool_in
    fetch = pltpu.make_async_copy(links_in, links, arrived)
    fetch.start()
    count = base.shape[1]
    near = near_half(width)
    unpack(from_near, flat(pool_rows), 4 * count + near)
    unpack(from_far, flat(pool_rows), 4 * count + width - near)
    fetch.wait()

    def pick(f, first, link):
        lanes = slice(f * SLOT, (f + 1) * SLOT)
        mine = across_rows.at[pl.ds(first, LANES)]

        def store(u, row):
            mine[u, :, lanes] = row

        move(LANES, lambda u: pool_rows[link(u), :, lanes], store)

    for_faces(count, links, pick)
    store_field(forward, base[...] + from_rows(0.5 * packed(lift).T, flat(across_rows)[...]))


def call(kernel, outs, operands, scratch=(), table=None, aliases=None, flops=0):
    outs = [out if isinstance(out, jax.ShapeDtypeStruct) else jax.ShapeDtypeStruct(out, jnp.float32) for out in outs]
    buffers = [pltpu.VMEM((rows, 1, LANES), jnp.float32) for rows in scratch]
    if table is not None:
        buffers += [pltpu.SMEM((table,), jnp.int32), pltpu.SemaphoreType.DMA]
    function = kernel.func if isinstance(kernel, functools.partial) else kernel
    return pl.pallas_call(
        kernel,
        out_shape=outs,
        in_specs=[pl.BlockSpec(memory_space=pltpu.VMEM)] * len(operands),
        out_specs=[pl.BlockSpec(memory_space=pltpu.VMEM)] * len(outs),
        scratch_shapes=buffers,
        input_output_aliases=aliases or {},
        compiler_params=pltpu.CompilerParams(vmem_limit_bytes=VMEM_LIMIT),
        cost_estimate=pl.CostEstimate(flops=flops * 10**9, bytes_accessed=0, transcendentals=0),
        name=function.__name__,
    )(*operands)


def exchange(to_near, to_far, axis):
    devices = lax.axis_size(axis)
    near = [(i, i ^ 1) for i in range(devices)]
    far = [(i, (i + (1 if i % 2 else -1)) % devices) for i in range(devices)]
    return lax.ppermute(to_near, axis, near), lax.ppermute(to_far, axis, far)


def from_behind(array, axis, by):
    devices = lax.axis_size(axis)
    pairs = [(i, i + by) for i in range(devices) if 0 <= i + by < devices]
    return lax.ppermute(array, axis, pairs)


def per_device(multipliers, coefficients, neighbours, send_list, interior, extract, lift):
    rows, count = multipliers.shape[1:]
    width = send_list.shape[0] // 2
    lines = (rows * count // LANES, LANES)
    message = (width // 4, 1, LANES)
    face_rows = (4 * count, 1, LANES)
    pool_rows = (4 * count + 2 * width + 8, 1, LANES)
    own = multipliers.reshape(lines)
    coefs = coefficients.reshape(lines)
    links = flat_links(neighbours)
    lift, extract = lift.transpose(2, 0, 1), extract.transpose(1, 0, 2)
    earlier = from_behind(own, "tm", 1)
    (sums,) = call(clear, [pool_rows], (), flops=3)
    half, sums, to_near, to_far = call(
        functools.partial(adjoint_sums, width),
        [face_rows, pool_rows, message, message],
        (links, own, lift, sums),
        table=4 * count,
        aliases={3: 1},
        flops=9,
    )
    from_near, from_far = exchange(to_near, to_far, "space")
    partial, extra = call(
        adjoint_inner, [(rows, count), face_rows], (own, coefs, half, sums, interior, extract), flops=2
    )
    (extra,) = call(
        functools.partial(join_near, width),
        [face_rows],
        (send_list, from_near, extra),
        scratch=(width,),
        table=2 * width,
        aliases={2: 0},
        flops=1,
    )
    combined, to_near, to_far, pool, _ = call(
        functools.partial(join_far, width),
        [lines, message, message, pool_rows, face_rows],
        (send_list, partial, earlier, from_far, extra, extract),
        scratch=(width,),
        table=2 * width,
        aliases={4: 4},
        flops=5,
    )
    later = from_behind(combined, "tm", -1)
    from_near, from_far = exchange(to_near, to_far, "space")
    (base,) = call(tangent_inner, [(rows, count)], (combined, coefs, interior, extract, lift), flops=2)
    forward, _ = call(
        functools.partial(tangent_across, width),
        [lines, pool_rows],
        (links, base, pool, from_near, from_far, lift),
        scratch=(count,),
        table=4 * count,
        aliases={2: 1},
        flops=9,
    )
    return (forward - later).reshape(1, rows, count)


def solution(mesh):
    placed = (
        P(("groups", "tm"), None, "space"),
        P(("groups", "tm"), None, "space"),
        P(None, "space"),
        P("space"),
        P(),
        P(),
        P(),
    )
    return jax.shard_map(
        per_device,
        mesh=mesh,
        in_specs=placed,
        out_specs=P(("groups", "tm"), None, "space"),
        check_vma=False,
    )
```

```python
import functools

import jax
import jax.numpy as jnp
from jax import lax
from jax.experimental import pallas as pl
from jax.experimental.pallas import tpu as pltpu
from jax.sharding import PartitionSpec as P

LANES = 128
SLOT = 32
DEPTH = 64
UNROLL = 32
GROUP = 16
VMEM_LIMIT = 32 * 1024 * 1024


def pad_rows(value, rows):
    missing = rows - value.shape[0]
    if missing == 0:
        return value
    return jnp.concatenate([value, jnp.zeros((missing, value.shape[1]), value.dtype)], axis=0)


def pad_columns(value, columns):
    missing = columns - value.shape[1]
    if missing == 0:
        return value
    return jnp.concatenate([value, jnp.zeros((value.shape[0], missing), value.dtype)], axis=1)


def halves(value):
    high = value.astype(jnp.bfloat16)
    low = (value - high.astype(jnp.float32)).astype(jnp.bfloat16)
    return high, low


def dot(left, right, left_dim, right_dim):
    dims = (((left_dim,), (right_dim,)), ((), ()))
    return lax.dot_general(left, right, dims, preferred_element_type=jnp.float32)


def stacked_field(field):
    high, low = halves(pad_rows(field, DEPTH))
    return jnp.concatenate([high, low, high], axis=0)


def stacked_factor(matrix, axis):
    padded = pad_rows(matrix, DEPTH) if axis == 0 else pad_columns(matrix, DEPTH)
    high, low = halves(padded)
    return jnp.concatenate([high, high, low], axis=axis)


def from_rows(matrix, table):
    rows = matrix.shape[0]
    high, low = halves(pad_rows(matrix, DEPTH))
    left = jnp.concatenate(
        [jnp.concatenate([high, high], axis=1), jnp.concatenate([low, jnp.zeros_like(low)], axis=1)], axis=0
    )
    both = dot(left, jnp.concatenate(halves(table), axis=1), 1, 1)
    return (both[:DEPTH] + both[DEPTH:])[:rows]


def slot_of_lane(shape):
    return lax.broadcasted_iota(jnp.int32, shape, 1) // SLOT


def choose_slots(blocks):
    slot = slot_of_lane(blocks[0].shape)
    result = blocks[0]
    for q in range(1, len(blocks)):
        result = jnp.where(slot == q, blocks[q], result)
    return result


def repeat_slot(block, q):
    only = jnp.where(slot_of_lane(block.shape) == q, block, 0.0)
    twice = only + pltpu.roll(only, SLOT, 1)
    return twice + pltpu.roll(twice, 2 * SLOT, 1)


def flat(ref):
    return ref.reshape(ref.shape[0], ref.shape[2])


def load_field(ref, rows):
    tiles = ref.shape[0] // rows
    return jnp.concatenate([ref[pl.ds(t, rows, stride=tiles), :] for t in range(tiles)], axis=1)


def store_field(ref, field):
    rows, count = field.shape
    tiles = count // LANES
    for t in range(tiles):
        ref[pl.ds(t, rows, stride=tiles), :] = field[:, t * LANES : (t + 1) * LANES]


def for_rows(count, step):
    together = min(count, 256)

    def body(i, carry):
        step(pl.multiple_of(i * together, together), together)
        return carry

    lax.fori_loop(0, count // together, body, 0)


def move(count, load, store):
    for first in range(0, count, UNROLL):
        rows = [load(u) for u in range(first, first + UNROLL)]
        for u in range(UNROLL):
            store(first + u, rows[u])


def link_blocks(neighbours):
    count = neighbours.shape[1]
    return neighbours.reshape(4, count // LANES, LANES).transpose(1, 0, 2).reshape(-1, LANES)


def for_faces(count, links, step):
    def body(block, carry):
        first = pl.multiple_of(block * LANES, LANES)
        mine = links.at[pl.ds(pl.multiple_of(block * (4 * LANES), 4 * LANES), 4 * LANES)]
        for f in range(4):
            for group in range(0, LANES, GROUP):
                words = [mine[f * LANES + group + u] for u in range(GROUP)]
                step(f, first + group, [word & 0xFFFF for word in words])
                step(f, first + group + count // 2, [word >> 16 for word in words])
        return carry

    lax.fori_loop(0, count // (2 * LANES), body, 0)


def packed(faces):
    return jnp.concatenate([pad_rows(faces[:, f, :], SLOT) for f in range(4)], axis=0)


def repeated(face):
    return stacked_factor(jnp.concatenate([pad_rows(face, SLOT)] * 4, axis=0).T, 0)


def near_half(width):
    return (1 - lax.axis_index("space") % 2) * width


def unpack(source, target, first):
    quarter = source.shape[0]
    for q in range(4):
        start = pl.multiple_of(first + q * quarter, quarter)
        target[pl.ds(start, quarter), :] = repeat_slot(flat(source)[...], q)


def clear(links, packed_links, sums):
    half = links.shape[0] // 2
    packed_links[...] = links[:half, :] | (links[half:, :] << 16)
    flat(sums)[...] = jnp.zeros((sums.shape[0], LANES), jnp.float32)


def adjoint_sums(width, links_in, multipliers, lift, sums_in, half_rows, sums_rows, to_near, to_far, links, arrived):
    del sums_in
    fetch = pltpu.make_async_copy(links_in, links, arrived)
    fetch.start()
    rows = lift.shape[2]
    count = half_rows.shape[0] // 4
    quarter = width // 4
    half, sums = flat(half_rows), flat(sums_rows)
    transposed = stacked_field(load_field(multipliers, rows)).T
    for f in range(4):
        half[f * count : (f + 1) * count, :] = dot(transposed, repeated(0.5 * lift[:, f, :]), 1, 0)
    fetch.wait()

    def scatter(f, first, targets):
        mine = half_rows.at[pl.ds(f * count + first, GROUP)]
        rows = [mine[u] for u in range(GROUP)]
        for u in range(GROUP):
            sums_rows[targets[u]] = rows[u]

    for_faces(count, links, scatter)
    near = near_half(width)
    for out, place in ((to_near, near), (to_far, width - near)):
        starts = [pl.multiple_of(4 * count + place + q * quarter, quarter) for q in range(4)]
        flat(out)[...] = choose_slots([sums[pl.ds(start, quarter), :] for start in starts])


def adjoint_inner(multipliers, coefficients, half_rows, sums_rows, interior, extract, partial, extra_rows):
    rows, count = partial.shape
    half, sums = flat(half_rows), flat(sums_rows)
    state = load_field(multipliers, rows)
    coefs = load_field(coefficients, rows)
    dfaces = choose_slots(
        [half[f * count : (f + 1) * count, :] + sums[f * count : (f + 1) * count, :] for f in range(4)]
    )
    inner = dot(stacked_factor(interior[...].T, 1), stacked_field(state), 1, 0)
    partial[...] = state + coefs * inner[:rows] + from_rows(packed(extract).T, dfaces)
    flat(extra_rows)[...] = jnp.zeros((extra_rows.shape[0], LANES), jnp.float32)


def spread(first, width, sends, received_rows, extra_rows):
    def scatter(base, together):
        mine = received_rows.at[pl.ds(base, together)]
        places = sends.at[pl.ds(first + base, together)]

        def store(u, row):
            extra_rows[places[u]] = row

        move(together, lambda u: mine[u], store)

    for_rows(width, scatter)


def join_near(width, sends_in, from_near, extra_in, extra_rows, received_rows, sends, arrived):
    del extra_in
    fetch = pltpu.make_async_copy(sends_in, sends, arrived)
    fetch.start()
    unpack(from_near, flat(received_rows), 0)
    fetch.wait()
    spread(near_half(width), width, sends, received_rows, extra_rows)


def join_far(
    width,
    sends_in,
    partial,
    earlier,
    from_far,
    extra_in,
    extract,
    combined,
    to_near,
    to_far,
    pool_rows,
    extra_rows,
    received_rows,
    sends,
    arrived,
):
    del extra_in
    fetch = pltpu.make_async_copy(sends_in, sends, arrived)
    fetch.start()
    rows, count = partial.shape
    quarter = width // 4
    extra, pool = flat(extra_rows), flat(pool_rows)
    pool[4 * count + 2 * width :, :] = jnp.zeros((8, LANES), jnp.float32)
    unpack(from_far, flat(received_rows), 0)
    near = near_half(width)
    fetch.wait()
    spread(width - near, width, sends, received_rows, extra_rows)
    dfaces = choose_slots([extra[f * count : (f + 1) * count, :] for f in range(4)])
    total = partial[...] - load_field(earlier, rows) + from_rows(packed(extract).T, dfaces)
    store_field(combined, total)
    transposed = stacked_field(total).T
    for f in range(4):
        pool[f * count : (f + 1) * count, :] = dot(transposed, repeated(extract[:, f, :]), 1, 0)
    for out, start in ((to_near, near), (to_far, width - near)):
        for q in range(4):
            lanes = slice(q * SLOT, (q + 1) * SLOT)

            def pick(base, together):
                places = sends.at[pl.ds(start + q * quarter + base, together)]
                mine = out.at[pl.ds(base, together)]

                def store(u, row):
                    mine[u, :, lanes] = row

                move(together, lambda u: pool_rows[places[u], :, lanes], store)

            for_rows(quarter, pick)


def tangent_inner(combined, coefficients, interior, extract, lift, base):
    rows, count = base.shape
    state = load_field(combined, rows)
    scaled = load_field(coefficients, rows) * state
    inner = dot(stacked_factor(interior[...], 1), stacked_field(scaled), 1, 0)
    faces = dot(stacked_field(state).T, stacked_factor(packed(extract).T, 0), 1, 0)
    base[...] = state + inner[:rows] + from_rows(0.5 * packed(lift).T, faces)


def tangent_across(
    width, links_in, base, pool_in, from_near, from_far, lift, forward, pool_rows, across_rows, links, arrived
):
    del pool_in
    fetch = pltpu.make_async_copy(links_in, links, arrived)
    fetch.start()
    count = base.shape[1]
    near = near_half(width)
    unpack(from_near, flat(pool_rows), 4 * count + near)
    unpack(from_far, flat(pool_rows), 4 * count + width - near)
    fetch.wait()

    def pick(f, first, sources):
        lanes = slice(f * SLOT, (f + 1) * SLOT)
        mine = across_rows.at[pl.ds(first, GROUP)]
        rows = [pool_rows[sources[u], :, lanes] for u in range(GROUP)]
        for u in range(GROUP):
            mine[u, :, lanes] = rows[u]

    for_faces(count, links, pick)
    store_field(forward, base[...] + from_rows(0.5 * packed(lift).T, flat(across_rows)[...]))


def call(kernel, outs, operands, scratch=(), table=None, aliases=None, flops=0):
    outs = [out if isinstance(out, jax.ShapeDtypeStruct) else jax.ShapeDtypeStruct(out, jnp.float32) for out in outs]
    buffers = [pltpu.VMEM((rows, 1, LANES), jnp.float32) for rows in scratch]
    if table is not None:
        buffers += [pltpu.SMEM((table,), jnp.int32), pltpu.SemaphoreType.DMA]
    function = kernel.func if isinstance(kernel, functools.partial) else kernel
    return pl.pallas_call(
        kernel,
        out_shape=outs,
        in_specs=[pl.BlockSpec(memory_space=pltpu.VMEM)] * len(operands),
        out_specs=[pl.BlockSpec(memory_space=pltpu.VMEM)] * len(outs),
        scratch_shapes=buffers,
        input_output_aliases=aliases or {},
        compiler_params=pltpu.CompilerParams(vmem_limit_bytes=VMEM_LIMIT),
        cost_estimate=pl.CostEstimate(flops=flops * 10**9, bytes_accessed=0, transcendentals=0),
        name=function.__name__,
    )(*operands)


def exchange(to_near, to_far, axis):
    devices = lax.axis_size(axis)
    near = [(i, i ^ 1) for i in range(devices)]
    far = [(i, (i + (1 if i % 2 else -1)) % devices) for i in range(devices)]
    return lax.ppermute(to_near, axis, near), lax.ppermute(to_far, axis, far)


def from_behind(array, axis, by):
    devices = lax.axis_size(axis)
    pairs = [(i, i + by) for i in range(devices) if 0 <= i + by < devices]
    return lax.ppermute(array, axis, pairs)


def per_device(multipliers, coefficients, neighbours, send_list, interior, extract, lift):
    rows, count = multipliers.shape[1:]
    width = send_list.shape[0] // 2
    lines = (rows * count // LANES, LANES)
    message = (width // 4, 1, LANES)
    face_rows = (4 * count, 1, LANES)
    pool_rows = (4 * count + 2 * width + 8, 1, LANES)
    own = multipliers.reshape(lines)
    coefs = coefficients.reshape(lines)
    links = link_blocks(neighbours)
    lift, extract = lift.transpose(2, 0, 1), extract.transpose(1, 0, 2)
    earlier = from_behind(own, "tm", 1)
    words = jax.ShapeDtypeStruct((links.shape[0] // 2, LANES), jnp.int32)
    links, sums = call(clear, [words, pool_rows], (links,), flops=3)
    links = links.reshape(-1)
    half, sums, to_near, to_far = call(
        functools.partial(adjoint_sums, width),
        [face_rows, pool_rows, message, message],
        (links, own, lift, sums),
        table=2 * count,
        aliases={3: 1},
        flops=9,
    )
    from_near, from_far = exchange(to_near, to_far, "space")
    partial, extra = call(
        adjoint_inner, [(rows, count), face_rows], (own, coefs, half, sums, interior, extract), flops=2
    )
    (extra,) = call(
        functools.partial(join_near, width),
        [face_rows],
        (send_list, from_near, extra),
        scratch=(width,),
        table=2 * width,
        aliases={2: 0},
        flops=1,
    )
    combined, to_near, to_far, pool, _ = call(
        functools.partial(join_far, width),
        [lines, message, message, pool_rows, face_rows],
        (send_list, partial, earlier, from_far, extra, extract),
        scratch=(width,),
        table=2 * width,
        aliases={4: 4},
        flops=5,
    )
    later = from_behind(combined, "tm", -1)
    from_near, from_far = exchange(to_near, to_far, "space")
    (base,) = call(tangent_inner, [(rows, count)], (combined, coefs, interior, extract, lift), flops=2)
    forward, _ = call(
        functools.partial(tangent_across, width),
        [lines, pool_rows],
        (links, base, pool, from_near, from_far, lift),
        scratch=(count,),
        table=2 * count,
        aliases={2: 1},
        flops=9,
    )
    return (forward - later).reshape(1, rows, count)


def solution(mesh):
    placed = (
        P(("groups", "tm"), None, "space"),
        P(("groups", "tm"), None, "space"),
        P(None, "space"),
        P("space"),
        P(),
        P(),
        P(),
    )
    return jax.shard_map(
        per_device,
        mesh=mesh,
        in_specs=placed,
        out_specs=P(("groups", "tm"), None, "space"),
        check_vma=False,
    )
```

```python
import functools

import jax
import jax.numpy as jnp
from jax import lax
from jax.experimental import pallas as pl
from jax.experimental.pallas import tpu as pltpu
from jax.sharding import PartitionSpec as P

LANES = 128
SLOT = 32
DEPTH = 64
UNROLL = 32
VMEM_LIMIT = 32 * 1024 * 1024


def pad_rows(value, rows):
    missing = rows - value.shape[0]
    if missing == 0:
        return value
    return jnp.concatenate([value, jnp.zeros((missing, value.shape[1]), value.dtype)], axis=0)


def pad_columns(value, columns):
    missing = columns - value.shape[1]
    if missing == 0:
        return value
    return jnp.concatenate([value, jnp.zeros((value.shape[0], missing), value.dtype)], axis=1)


def halves(value):
    high = value.astype(jnp.bfloat16)
    low = (value - high.astype(jnp.float32)).astype(jnp.bfloat16)
    return high, low


def dot(left, right, left_dim, right_dim):
    dims = (((left_dim,), (right_dim,)), ((), ()))
    return lax.dot_general(left, right, dims, preferred_element_type=jnp.float32)


def stacked_field(field):
    high, low = halves(pad_rows(field, DEPTH))
    return jnp.concatenate([high, low, high], axis=0)


def stacked_factor(matrix, axis):
    padded = pad_rows(matrix, DEPTH) if axis == 0 else pad_columns(matrix, DEPTH)
    high, low = halves(padded)
    return jnp.concatenate([high, high, low], axis=axis)


def from_rows(matrix, table):
    rows = matrix.shape[0]
    high, low = halves(pad_rows(matrix, DEPTH))
    left = jnp.concatenate(
        [jnp.concatenate([high, high], axis=1), jnp.concatenate([low, jnp.zeros_like(low)], axis=1)], axis=0
    )
    both = dot(left, jnp.concatenate(halves(table), axis=1), 1, 1)
    return (both[:DEPTH] + both[DEPTH:])[:rows]


def slot_of_lane(shape):
    return lax.broadcasted_iota(jnp.int32, shape, 1) // SLOT


def choose_slots(blocks):
    slot = slot_of_lane(blocks[0].shape)
    result = blocks[0]
    for q in range(1, len(blocks)):
        result = jnp.where(slot == q, blocks[q], result)
    return result


def repeat_slot(block, q):
    only = jnp.where(slot_of_lane(block.shape) == q, block, 0.0)
    twice = only + pltpu.roll(only, SLOT, 1)
    return twice + pltpu.roll(twice, 2 * SLOT, 1)


def flat(ref):
    return ref.reshape(ref.shape[0], ref.shape[2])


def load_field(ref, rows):
    tiles = ref.shape[0] // rows
    return jnp.concatenate([ref[pl.ds(t, rows, stride=tiles), :] for t in range(tiles)], axis=1)


def store_field(ref, field):
    rows, count = field.shape
    tiles = count // LANES
    for t in range(tiles):
        ref[pl.ds(t, rows, stride=tiles), :] = field[:, t * LANES : (t + 1) * LANES]


def for_rows(count, step):
    together = min(count, 256)

    def body(i, carry):
        step(pl.multiple_of(i * together, together), together)
        return carry

    lax.fori_loop(0, count // together, body, 0)


def move(count, load, store):
    for first in range(0, count, UNROLL):
        rows = [load(u) for u in range(first, first + UNROLL)]
        for u in range(UNROLL):
            store(first + u, rows[u])


def flat_links(neighbours):
    count = neighbours.shape[1]
    return neighbours.reshape(4, count // LANES, LANES).transpose(1, 0, 2).reshape(-1)


def for_faces(count, links, step):
    def body(block, carry):
        first = pl.multiple_of(block * LANES, LANES)
        mine = links.at[pl.ds(pl.multiple_of(block * (4 * LANES), 4 * LANES), 4 * LANES)]
        for f in range(4):
            step(f, first, lambda u, f=f: mine[f * LANES + u])
        return carry

    lax.fori_loop(0, count // LANES, body, 0)


def gather_blocks(count, links, source, target):
    line = lax.broadcasted_iota(jnp.int32, (8, LANES), 0)
    slot = slot_of_lane((8, LANES))

    def body(block, carry):
        first = pl.multiple_of(block * LANES, LANES)
        mine = links.at[pl.ds(pl.multiple_of(block * (4 * LANES), 4 * LANES), 4 * LANES)]
        for group in range(0, LANES, 8):
            faces = []
            for f in range(4):
                together = jnp.broadcast_to(source[pl.ds(mine[f * LANES + group], 1), :], (8, LANES))
                for u in range(1, 8):
                    row = jnp.broadcast_to(source[pl.ds(mine[f * LANES + group + u], 1), :], (8, LANES))
                    together = jnp.where(line == u, row, together)
                faces.append(together)
            result = faces[0]
            for f in range(1, 4):
                result = jnp.where(slot == f, faces[f], result)
            target[pl.ds(pl.multiple_of(first + group, 8), 8), :] = result
        return carry

    lax.fori_loop(0, count // LANES, body, 0)


def packed(faces):
    return jnp.concatenate([pad_rows(faces[:, f, :], SLOT) for f in range(4)], axis=0)


def repeated(face):
    return stacked_factor(jnp.concatenate([pad_rows(face, SLOT)] * 4, axis=0).T, 0)


def near_half(width):
    return (1 - lax.axis_index("space") % 2) * width


def unpack(source, target, first):
    quarter = source.shape[0]
    for q in range(4):
        start = pl.multiple_of(first + q * quarter, quarter)
        target[pl.ds(start, quarter), :] = repeat_slot(flat(source)[...], q)


def clear(sums):
    flat(sums)[...] = jnp.zeros((sums.shape[0], LANES), jnp.float32)


def adjoint_sums(width, links_in, multipliers, lift, sums_in, half_rows, sums_rows, to_near, to_far, links, arrived):
    del sums_in
    fetch = pltpu.make_async_copy(links_in, links, arrived)
    fetch.start()
    rows = lift.shape[2]
    count = half_rows.shape[0] // 4
    quarter = width // 4
    half, sums = flat(half_rows), flat(sums_rows)
    transposed = stacked_field(load_field(multipliers, rows)).T
    for f in range(4):
        half[f * count : (f + 1) * count, :] = dot(transposed, repeated(0.5 * lift[:, f, :]), 1, 0)
    fetch.wait()

    def scatter(f, first, link):
        for group in range(0, LANES, 8):
            block = half[pl.ds(pl.multiple_of(f * count + first + group, 8), 8), :]
            for u in range(8):
                sums[pl.ds(link(group + u), 1), :] = block[u : u + 1, :]

    for_faces(count, links, scatter)
    near = near_half(width)
    for out, place in ((to_near, near), (to_far, width - near)):
        starts = [pl.multiple_of(4 * count + place + q * quarter, quarter) for q in range(4)]
        flat(out)[...] = choose_slots([sums[pl.ds(start, quarter), :] for start in starts])


def adjoint_inner(multipliers, coefficients, half_rows, sums_rows, interior, extract, partial, extra_rows):
    rows, count = partial.shape
    half, sums = flat(half_rows), flat(sums_rows)
    state = load_field(multipliers, rows)
    coefs = load_field(coefficients, rows)
    dfaces = choose_slots(
        [half[f * count : (f + 1) * count, :] + sums[f * count : (f + 1) * count, :] for f in range(4)]
    )
    inner = dot(stacked_factor(interior[...].T, 1), stacked_field(state), 1, 0)
    partial[...] = state + coefs * inner[:rows] + from_rows(packed(extract).T, dfaces)
    flat(extra_rows)[...] = jnp.zeros((extra_rows.shape[0], LANES), jnp.float32)


def spread(first, width, sends, received_rows, extra_rows):
    def scatter(base, together):
        mine = received_rows.at[pl.ds(base, together)]
        places = sends.at[pl.ds(first + base, together)]

        def store(u, row):
            extra_rows[places[u]] = row

        move(together, lambda u: mine[u], store)

    for_rows(width, scatter)


def join_near(width, sends_in, from_near, extra_in, extra_rows, received_rows, sends, arrived):
    del extra_in
    fetch = pltpu.make_async_copy(sends_in, sends, arrived)
    fetch.start()
    unpack(from_near, flat(received_rows), 0)
    fetch.wait()
    spread(near_half(width), width, sends, received_rows, extra_rows)


def join_far(
    width,
    sends_in,
    partial,
    earlier,
    from_far,
    extra_in,
    extract,
    combined,
    to_near,
    to_far,
    pool_rows,
    extra_rows,
    received_rows,
    sends,
    arrived,
):
    del extra_in
    fetch = pltpu.make_async_copy(sends_in, sends, arrived)
    fetch.start()
    rows, count = partial.shape
    quarter = width // 4
    extra, pool = flat(extra_rows), flat(pool_rows)
    pool[4 * count + 2 * width :, :] = jnp.zeros((8, LANES), jnp.float32)
    unpack(from_far, flat(received_rows), 0)
    near = near_half(width)
    fetch.wait()
    spread(width - near, width, sends, received_rows, extra_rows)
    dfaces = choose_slots([extra[f * count : (f + 1) * count, :] for f in range(4)])
    total = partial[...] - load_field(earlier, rows) + from_rows(packed(extract).T, dfaces)
    store_field(combined, total)
    transposed = stacked_field(total).T
    for f in range(4):
        pool[f * count : (f + 1) * count, :] = dot(transposed, repeated(extract[:, f, :]), 1, 0)
    for out, start in ((to_near, near), (to_far, width - near)):
        for q in range(4):
            lanes = slice(q * SLOT, (q + 1) * SLOT)

            def pick(base, together):
                places = sends.at[pl.ds(start + q * quarter + base, together)]
                mine = out.at[pl.ds(base, together)]

                def store(u, row):
                    mine[u, :, lanes] = row

                move(together, lambda u: pool_rows[places[u], :, lanes], store)

            for_rows(quarter, pick)


def tangent_inner(combined, coefficients, interior, extract, lift, base):
    rows, count = base.shape
    state = load_field(combined, rows)
    scaled = load_field(coefficients, rows) * state
    inner = dot(stacked_factor(interior[...], 1), stacked_field(scaled), 1, 0)
    faces = dot(stacked_field(state).T, stacked_factor(packed(extract).T, 0), 1, 0)
    base[...] = state + inner[:rows] + from_rows(0.5 * packed(lift).T, faces)


def tangent_across(
    width, links_in, base, pool_in, from_near, from_far, lift, forward, pool_rows, across_rows, links, arrived
):
    del pool_in
    fetch = pltpu.make_async_copy(links_in, links, arrived)
    fetch.start()
    count = base.shape[1]
    near = near_half(width)
    unpack(from_near, flat(pool_rows), 4 * count + near)
    unpack(from_far, flat(pool_rows), 4 * count + width - near)
    fetch.wait()

    gather_blocks(count, links, flat(pool_rows), flat(across_rows))
    store_field(forward, base[...] + from_rows(0.5 * packed(lift).T, flat(across_rows)[...]))


def call(kernel, outs, operands, scratch=(), table=None, aliases=None, flops=0):
    outs = [out if isinstance(out, jax.ShapeDtypeStruct) else jax.ShapeDtypeStruct(out, jnp.float32) for out in outs]
    buffers = [pltpu.VMEM((rows, 1, LANES), jnp.float32) for rows in scratch]
    if table is not None:
        buffers += [pltpu.SMEM((table,), jnp.int32), pltpu.SemaphoreType.DMA]
    function = kernel.func if isinstance(kernel, functools.partial) else kernel
    return pl.pallas_call(
        kernel,
        out_shape=outs,
        in_specs=[pl.BlockSpec(memory_space=pltpu.VMEM)] * len(operands),
        out_specs=[pl.BlockSpec(memory_space=pltpu.VMEM)] * len(outs),
        scratch_shapes=buffers,
        input_output_aliases=aliases or {},
        compiler_params=pltpu.CompilerParams(vmem_limit_bytes=VMEM_LIMIT),
        cost_estimate=pl.CostEstimate(flops=flops * 10**9, bytes_accessed=0, transcendentals=0),
        name=function.__name__,
    )(*operands)


def exchange(to_near, to_far, axis):
    devices = lax.axis_size(axis)
    near = [(i, i ^ 1) for i in range(devices)]
    far = [(i, (i + (1 if i % 2 else -1)) % devices) for i in range(devices)]
    return lax.ppermute(to_near, axis, near), lax.ppermute(to_far, axis, far)


def from_behind(array, axis, by):
    devices = lax.axis_size(axis)
    pairs = [(i, i + by) for i in range(devices) if 0 <= i + by < devices]
    return lax.ppermute(array, axis, pairs)


def per_device(multipliers, coefficients, neighbours, send_list, interior, extract, lift):
    rows, count = multipliers.shape[1:]
    width = send_list.shape[0] // 2
    lines = (rows * count // LANES, LANES)
    message = (width // 4, 1, LANES)
    face_rows = (4 * count, 1, LANES)
    pool_rows = (4 * count + 2 * width + 8, 1, LANES)
    own = multipliers.reshape(lines)
    coefs = coefficients.reshape(lines)
    links = flat_links(neighbours)
    lift, extract = lift.transpose(2, 0, 1), extract.transpose(1, 0, 2)
    earlier = from_behind(own, "tm", 1)
    (sums,) = call(clear, [pool_rows], (), flops=3)
    half, sums, to_near, to_far = call(
        functools.partial(adjoint_sums, width),
        [face_rows, pool_rows, message, message],
        (links, own, lift, sums),
        table=4 * count,
        aliases={3: 1},
        flops=9,
    )
    from_near, from_far = exchange(to_near, to_far, "space")
    partial, extra = call(
        adjoint_inner, [(rows, count), face_rows], (own, coefs, half, sums, interior, extract), flops=2
    )
    (extra,) = call(
        functools.partial(join_near, width),
        [face_rows],
        (send_list, from_near, extra),
        scratch=(width,),
        table=2 * width,
        aliases={2: 0},
        flops=1,
    )
    combined, to_near, to_far, pool, _ = call(
        functools.partial(join_far, width),
        [lines, message, message, pool_rows, face_rows],
        (send_list, partial, earlier, from_far, extra, extract),
        scratch=(width,),
        table=2 * width,
        aliases={4: 4},
        flops=5,
    )
    later = from_behind(combined, "tm", -1)
    from_near, from_far = exchange(to_near, to_far, "space")
    (base,) = call(tangent_inner, [(rows, count)], (combined, coefs, interior, extract, lift), flops=2)
    forward, _ = call(
        functools.partial(tangent_across, width),
        [lines, pool_rows],
        (links, base, pool, from_near, from_far, lift),
        scratch=(count,),
        table=4 * count,
        aliases={2: 1},
        flops=9,
    )
    return (forward - later).reshape(1, rows, count)


def solution(mesh):
    placed = (
        P(("groups", "tm"), None, "space"),
        P(("groups", "tm"), None, "space"),
        P(None, "space"),
        P("space"),
        P(),
        P(),
        P(),
    )
    return jax.shard_map(
        per_device,
        mesh=mesh,
        in_specs=placed,
        out_specs=P(("groups", "tm"), None, "space"),
        check_vma=False,
    )
```

```python
import functools

import jax
import jax.numpy as jnp
from jax import lax
from jax.experimental import pallas as pl
from jax.experimental.pallas import tpu as pltpu
from jax.sharding import PartitionSpec as P

LANES = 128
SLOT = 32
DEPTH = 64
UNROLL = 32
TILE = 256
DENSE = 1
VMEM_LIMIT = 32 * 1024 * 1024


def pad_rows(value, rows):
    missing = rows - value.shape[0]
    if missing == 0:
        return value
    return jnp.concatenate([value, jnp.zeros((missing, value.shape[1]), value.dtype)], axis=0)


def pad_columns(value, columns):
    missing = columns - value.shape[1]
    if missing == 0:
        return value
    return jnp.concatenate([value, jnp.zeros((value.shape[0], missing), value.dtype)], axis=1)


def halves(value):
    high = value.astype(jnp.bfloat16)
    low = (value - high.astype(jnp.float32)).astype(jnp.bfloat16)
    return high, low


def dot(left, right, left_dim, right_dim):
    dims = (((left_dim,), (right_dim,)), ((), ()))
    return lax.dot_general(left, right, dims, preferred_element_type=jnp.float32)


def stacked_field(field):
    high, low = halves(pad_rows(field, DEPTH))
    return jnp.concatenate([high, low, high], axis=0)


def stacked_factor(matrix, axis):
    padded = pad_rows(matrix, DEPTH) if axis == 0 else pad_columns(matrix, DEPTH)
    high, low = halves(padded)
    return jnp.concatenate([high, high, low], axis=axis)


def from_rows(matrix, table):
    rows = matrix.shape[0]
    high, low = halves(pad_rows(matrix, DEPTH))
    left = jnp.concatenate(
        [jnp.concatenate([high, high], axis=1), jnp.concatenate([low, jnp.zeros_like(low)], axis=1)], axis=0
    )
    both = dot(left, jnp.concatenate(halves(table), axis=1), 1, 1)
    return (both[:DEPTH] + both[DEPTH:])[:rows]


def from_columns(matrix, table):
    rows = matrix.shape[0]
    high, low = halves(pad_rows(matrix, DEPTH))
    left = jnp.concatenate(
        [jnp.concatenate([high, high], axis=1), jnp.concatenate([low, jnp.zeros_like(low)], axis=1)], axis=0
    )
    both = dot(left, jnp.concatenate(halves(table), axis=0), 1, 0)
    return (both[:DEPTH] + both[DEPTH:])[:rows]


def slot_of_lane(shape):
    return lax.broadcasted_iota(jnp.int32, shape, 1) // SLOT


def choose_slots(blocks):
    slot = slot_of_lane(blocks[0].shape)
    result = blocks[0]
    for q in range(1, len(blocks)):
        result = jnp.where(slot == q, blocks[q], result)
    return result


def repeat_slot(block, q):
    only = jnp.where(slot_of_lane(block.shape) == q, block, 0.0)
    twice = only + pltpu.roll(only, SLOT, 1)
    return twice + pltpu.roll(twice, 2 * SLOT, 1)


def flat(ref):
    return ref.reshape(ref.shape[0], ref.shape[2])


def load_field(ref, rows):
    tiles = ref.shape[0] // rows
    return jnp.concatenate([ref[pl.ds(t, rows, stride=tiles), :] for t in range(tiles)], axis=1)


def store_field(ref, field):
    rows, count = field.shape
    tiles = count // LANES
    for t in range(tiles):
        ref[pl.ds(t, rows, stride=tiles), :] = field[:, t * LANES : (t + 1) * LANES]


def for_rows(count, step):
    together = min(count, 256)

    def body(i, carry):
        step(pl.multiple_of(i * together, together), together)
        return carry

    lax.fori_loop(0, count // together, body, 0)


def move(count, load, store):
    for first in range(0, count, UNROLL):
        rows = [load(u) for u in range(first, first + UNROLL)]
        for u in range(UNROLL):
            store(first + u, rows[u])


def link_blocks(neighbours):
    count = neighbours.shape[1]
    return neighbours.reshape(4, count // LANES, LANES).transpose(1, 0, 2).reshape(-1, LANES)


def gather_blocks(count, links, source, target):
    line = lax.broadcasted_iota(jnp.int32, (8, LANES), 0)
    slot = slot_of_lane((8, LANES))

    def body(block, carry):
        first = pl.multiple_of(block * LANES, LANES)
        mine = links.at[pl.ds(pl.multiple_of(block * (4 * LANES), 4 * LANES), 4 * LANES)]
        for group in range(0, LANES, 8):
            faces = []
            for f in range(4):
                together = jnp.broadcast_to(source[pl.ds(mine[f * LANES + group], 1), :], (8, LANES))
                for u in range(1, 8):
                    row = jnp.broadcast_to(source[pl.ds(mine[f * LANES + group + u], 1), :], (8, LANES))
                    together = jnp.where(line == u, row, together)
                faces.append(together)
            result = faces[0]
            for f in range(1, 4):
                result = jnp.where(slot == f, faces[f], result)
            target[pl.ds(pl.multiple_of(first + group, 8), 8), :] = result
        return carry

    lax.fori_loop(0, count // LANES, body, 0)


def packed(faces):
    return jnp.concatenate([pad_rows(faces[:, f, :], SLOT) for f in range(4)], axis=0)


def repeated(face):
    return stacked_factor(jnp.concatenate([pad_rows(face, SLOT)] * 4, axis=0).T, 0)


def near_half(width):
    return (1 - lax.axis_index("space") % 2) * width


def unpack(source, target, first):
    quarter = source.shape[0]
    for q in range(4):
        start = pl.multiple_of(first + q * quarter, quarter)
        target[pl.ds(start, quarter), :] = repeat_slot(flat(source)[...], q)


def clear(sums):
    flat(sums)[...] = jnp.zeros((sums.shape[0], LANES), jnp.float32)


def dense_sums(block, links, faces, parts_ref, acc):
    lines = TILE // LANES
    first = pl.multiple_of(block * TILE, TILE)
    places, parts = [], []
    for i, f in enumerate(faces):
        for line in range(lines):
            places.append(links[pl.ds((block * lines + line) * 4 + f, 1), :])
        parts.append(parts_ref[i, :, pl.ds(first, TILE)])
    places, parts = jnp.concatenate(places, axis=1), jnp.concatenate(parts, axis=1)
    width = places.shape[1]
    lane = lax.broadcasted_iota(jnp.int32, (TILE, width), 0)
    one = jnp.where((places & (TILE - 1)) == lane, 1.0, 0.0).astype(jnp.bfloat16)
    high = places // TILE
    count = acc.shape[0] // parts.shape[0]
    masked = [jnp.where(high == h, parts, 0.0).astype(jnp.bfloat16) for h in range(count)]
    acc[...] += dot(jnp.concatenate(masked, axis=0), one, 1, 1)


def adjoint_sums(
    width,
    links_in,
    link_lines,
    multipliers,
    lift,
    sums_in,
    sums_rows,
    dense,
    to_near,
    to_far,
    half_rows,
    parts,
    acc,
    links,
    arrived,
):
    del sums_in
    fetch = pltpu.make_async_copy(links_in, links, arrived)
    fetch.start()
    rows = lift.shape[2]
    count = dense.shape[1]
    quarter = width // 4
    half, sums = flat(half_rows), flat(sums_rows)
    field = stacked_field(load_field(multipliers, rows))
    transposed = field.T
    by_row, by_product = range(4 - DENSE), range(4 - DENSE, 4)
    for f in by_row:
        half[f * count : (f + 1) * count, :] = dot(transposed, repeated(0.5 * lift[:, f, :]), 1, 0)
    for i, f in enumerate(by_product):
        face = dot(stacked_factor(pad_rows(0.5 * lift[:, f, :], SLOT), 1), field, 1, 0)
        high, low = halves(face)
        parts[i] = jnp.concatenate([high.astype(jnp.float32), low.astype(jnp.float32)], axis=0)
    acc[...] = jnp.zeros(acc.shape, jnp.float32)
    fetch.wait()

    def body(block, carry):
        dense_sums(block, link_lines, by_product, parts, acc)
        for line in range(TILE // LANES):
            first = block * TILE + line * LANES
            mine = links.at[pl.ds(pl.multiple_of((block * TILE + line * LANES) * 4, 4 * LANES), 4 * LANES)]
            for f in by_row:
                for group in range(0, LANES, 8):
                    rows = half[pl.ds(pl.multiple_of(f * count + first + group, 8), 8), :]
                    for u in range(8):
                        sums[pl.ds(mine[f * LANES + group + u], 1), :] = rows[u : u + 1, :]
        return carry

    lax.fori_loop(0, count // TILE, body, 0)

    def place(h):
        start = pl.multiple_of(h * 2 * SLOT, 2 * SLOT)
        return acc[pl.ds(start, SLOT), :] + acc[pl.ds(pl.multiple_of(start + SLOT, SLOT), SLOT), :]

    near = near_half(width)
    for out, start in ((to_near, near), (to_far, width - near)):
        starts = [pl.multiple_of(4 * count + start + q * quarter, quarter) for q in range(4)]
        added = jnp.concatenate([place((4 * count + start) // TILE + q) for q in range(4)], axis=0).T
        flat(out)[...] = choose_slots([sums[pl.ds(start, quarter), :] for start in starts]) + added
    per_face = count // TILE
    for f in range(4):
        for t in range(per_face):
            dense[f * SLOT : (f + 1) * SLOT, t * TILE : (t + 1) * TILE] = place(f * per_face + t)


def adjoint_inner(multipliers, coefficients, sums_rows, dense, interior, lift, extract, partial, extra_rows):
    rows, count = partial.shape
    sums = flat(sums_rows)
    state = load_field(multipliers, rows)
    coefs = load_field(coefficients, rows)
    field = stacked_field(state)
    inner = dot(stacked_factor(interior[...].T, 1), field, 1, 0)
    own = dot(stacked_factor(0.5 * packed(lift), 1), field, 1, 0) + dense[...]
    moved = choose_slots([sums[f * count : (f + 1) * count, :] for f in range(4)])
    back = packed(extract).T
    partial[...] = state + coefs * inner[:rows] + from_columns(back, own) + from_rows(back, moved)
    flat(extra_rows)[...] = jnp.zeros((extra_rows.shape[0], LANES), jnp.float32)


def spread(first, width, sends, received_rows, extra_rows):
    def scatter(base, together):
        mine = received_rows.at[pl.ds(base, together)]
        places = sends.at[pl.ds(first + base, together)]

        def store(u, row):
            extra_rows[places[u]] = row

        move(together, lambda u: mine[u], store)

    for_rows(width, scatter)


def join_near(width, sends_in, from_near, extra_in, extra_rows, received_rows, sends, arrived):
    del extra_in
    fetch = pltpu.make_async_copy(sends_in, sends, arrived)
    fetch.start()
    unpack(from_near, flat(received_rows), 0)
    fetch.wait()
    spread(near_half(width), width, sends, received_rows, extra_rows)


def join_far(
    width,
    sends_in,
    partial,
    earlier,
    from_far,
    extra_in,
    extract,
    combined,
    to_near,
    to_far,
    pool_rows,
    extra_rows,
    received_rows,
    sends,
    arrived,
):
    del extra_in
    fetch = pltpu.make_async_copy(sends_in, sends, arrived)
    fetch.start()
    rows, count = partial.shape
    quarter = width // 4
    extra, pool = flat(extra_rows), flat(pool_rows)
    pool[4 * count + 2 * width :, :] = jnp.zeros((8, LANES), jnp.float32)
    unpack(from_far, flat(received_rows), 0)
    near = near_half(width)
    fetch.wait()
    spread(width - near, width, sends, received_rows, extra_rows)
    dfaces = choose_slots([extra[f * count : (f + 1) * count, :] for f in range(4)])
    total = partial[...] - load_field(earlier, rows) + from_rows(packed(extract).T, dfaces)
    store_field(combined, total)
    transposed = stacked_field(total).T
    for f in range(4):
        pool[f * count : (f + 1) * count, :] = dot(transposed, repeated(extract[:, f, :]), 1, 0)
    for out, start in ((to_near, near), (to_far, width - near)):
        for q in range(4):
            lanes = slice(q * SLOT, (q + 1) * SLOT)

            def pick(base, together):
                places = sends.at[pl.ds(start + q * quarter + base, together)]
                mine = out.at[pl.ds(base, together)]

                def store(u, row):
                    mine[u, :, lanes] = row

                move(together, lambda u: pool_rows[places[u], :, lanes], store)

            for_rows(quarter, pick)


def tangent_inner(combined, coefficients, interior, extract, lift, base):
    rows, count = base.shape
    state = load_field(combined, rows)
    scaled = load_field(coefficients, rows) * state
    inner = dot(stacked_factor(interior[...], 1), stacked_field(scaled), 1, 0)
    faces = dot(stacked_field(state).T, stacked_factor(packed(extract).T, 0), 1, 0)
    base[...] = state + inner[:rows] + from_rows(0.5 * packed(lift).T, faces)


def tangent_across(
    width, links_in, base, pool_in, from_near, from_far, lift, forward, pool_rows, across_rows, links, arrived
):
    del pool_in
    fetch = pltpu.make_async_copy(links_in, links, arrived)
    fetch.start()
    count = base.shape[1]
    near = near_half(width)
    unpack(from_near, flat(pool_rows), 4 * count + near)
    unpack(from_far, flat(pool_rows), 4 * count + width - near)
    fetch.wait()

    gather_blocks(count, links, flat(pool_rows), flat(across_rows))
    store_field(forward, base[...] + from_rows(0.5 * packed(lift).T, flat(across_rows)[...]))


def call(kernel, outs, operands, scratch=(), table=None, aliases=None, flops=0, buffers=()):
    outs = [out if isinstance(out, jax.ShapeDtypeStruct) else jax.ShapeDtypeStruct(out, jnp.float32) for out in outs]
    buffers = [pltpu.VMEM((rows, 1, LANES), jnp.float32) for rows in scratch] + list(buffers)
    if table is not None:
        buffers += [pltpu.SMEM((table,), jnp.int32), pltpu.SemaphoreType.DMA]
    function = kernel.func if isinstance(kernel, functools.partial) else kernel
    return pl.pallas_call(
        kernel,
        out_shape=outs,
        in_specs=[pl.BlockSpec(memory_space=pltpu.VMEM)] * len(operands),
        out_specs=[pl.BlockSpec(memory_space=pltpu.VMEM)] * len(outs),
        scratch_shapes=buffers,
        input_output_aliases=aliases or {},
        compiler_params=pltpu.CompilerParams(vmem_limit_bytes=VMEM_LIMIT),
        cost_estimate=pl.CostEstimate(flops=flops * 10**9, bytes_accessed=0, transcendentals=0),
        name=function.__name__,
    )(*operands)


def exchange(to_near, to_far, axis):
    devices = lax.axis_size(axis)
    near = [(i, i ^ 1) for i in range(devices)]
    far = [(i, (i + (1 if i % 2 else -1)) % devices) for i in range(devices)]
    return lax.ppermute(to_near, axis, near), lax.ppermute(to_far, axis, far)


def from_behind(array, axis, by):
    devices = lax.axis_size(axis)
    pairs = [(i, i + by) for i in range(devices) if 0 <= i + by < devices]
    return lax.ppermute(array, axis, pairs)


def per_device(multipliers, coefficients, neighbours, send_list, interior, extract, lift):
    rows, count = multipliers.shape[1:]
    width = send_list.shape[0] // 2
    lines = (rows * count // LANES, LANES)
    message = (width // 4, 1, LANES)
    face_rows = (4 * count, 1, LANES)
    pool_rows = (4 * count + 2 * width + 8, 1, LANES)
    own = multipliers.reshape(lines)
    coefs = coefficients.reshape(lines)
    link_lines = link_blocks(neighbours)
    links = link_lines.reshape(-1)
    lift, extract = lift.transpose(2, 0, 1), extract.transpose(1, 0, 2)
    earlier = from_behind(own, "tm", 1)
    (sums,) = call(clear, [pool_rows], (), flops=3)
    sums, dense, to_near, to_far = call(
        functools.partial(adjoint_sums, width),
        [pool_rows, (LANES, count), message, message],
        (links, link_lines, own, lift, sums),
        scratch=((4 - DENSE) * count,),
        buffers=(
            pltpu.VMEM((DENSE, 2 * SLOT, count), jnp.float32),
            pltpu.VMEM(((4 * count + 2 * width) // TILE * 2 * SLOT, TILE), jnp.float32),
        ),
        table=4 * count,
        aliases={4: 0},
        flops=9,
    )
    from_near, from_far = exchange(to_near, to_far, "space")
    partial, extra = call(
        adjoint_inner, [(rows, count), face_rows], (own, coefs, sums, dense, interior, lift, extract), flops=2
    )
    (extra,) = call(
        functools.partial(join_near, width),
        [face_rows],
        (send_list, from_near, extra),
        scratch=(width,),
        table=2 * width,
        aliases={2: 0},
        flops=1,
    )
    combined, to_near, to_far, pool, _ = call(
        functools.partial(join_far, width),
        [lines, message, message, pool_rows, face_rows],
        (send_list, partial, earlier, from_far, extra, extract),
        scratch=(width,),
        table=2 * width,
        aliases={4: 4},
        flops=5,
    )
    later = from_behind(combined, "tm", -1)
    from_near, from_far = exchange(to_near, to_far, "space")
    (base,) = call(tangent_inner, [(rows, count)], (combined, coefs, interior, extract, lift), flops=2)
    forward, _ = call(
        functools.partial(tangent_across, width),
        [lines, pool_rows],
        (links, base, pool, from_near, from_far, lift),
        scratch=(count,),
        table=4 * count,
        aliases={2: 1},
        flops=9,
    )
    return (forward - later).reshape(1, rows, count)


def solution(mesh):
    placed = (
        P(("groups", "tm"), None, "space"),
        P(("groups", "tm"), None, "space"),
        P(None, "space"),
        P("space"),
        P(),
        P(),
        P(),
    )
    return jax.shard_map(
        per_device,
        mesh=mesh,
        in_specs=placed,
        out_specs=P(("groups", "tm"), None, "space"),
        check_vma=False,
    )
```

```python
import functools

import jax
import jax.numpy as jnp
from jax import lax
from jax.experimental import pallas as pl
from jax.experimental.pallas import tpu as pltpu
from jax.sharding import PartitionSpec as P

LANES = 128
SLOT = 32
DEPTH = 64
UNROLL = 32
TILE = 256
DENSE = 2
VMEM_LIMIT = 32 * 1024 * 1024


def pad_rows(value, rows):
    missing = rows - value.shape[0]
    if missing == 0:
        return value
    return jnp.concatenate([value, jnp.zeros((missing, value.shape[1]), value.dtype)], axis=0)


def pad_columns(value, columns):
    missing = columns - value.shape[1]
    if missing == 0:
        return value
    return jnp.concatenate([value, jnp.zeros((value.shape[0], missing), value.dtype)], axis=1)


def halves(value):
    high = value.astype(jnp.bfloat16)
    low = (value - high.astype(jnp.float32)).astype(jnp.bfloat16)
    return high, low


def dot(left, right, left_dim, right_dim):
    dims = (((left_dim,), (right_dim,)), ((), ()))
    return lax.dot_general(left, right, dims, preferred_element_type=jnp.float32)


def stacked_field(field):
    high, low = halves(pad_rows(field, DEPTH))
    return jnp.concatenate([high, low, high], axis=0)


def stacked_factor(matrix, axis):
    padded = pad_rows(matrix, DEPTH) if axis == 0 else pad_columns(matrix, DEPTH)
    high, low = halves(padded)
    return jnp.concatenate([high, high, low], axis=axis)


def from_rows(matrix, table):
    rows = matrix.shape[0]
    high, low = halves(pad_rows(matrix, DEPTH))
    left = jnp.concatenate(
        [jnp.concatenate([high, high], axis=1), jnp.concatenate([low, jnp.zeros_like(low)], axis=1)], axis=0
    )
    both = dot(left, jnp.concatenate(halves(table), axis=1), 1, 1)
    return (both[:DEPTH] + both[DEPTH:])[:rows]


def from_columns(matrix, table):
    rows = matrix.shape[0]
    high, low = halves(pad_rows(matrix, DEPTH))
    left = jnp.concatenate(
        [jnp.concatenate([high, high], axis=1), jnp.concatenate([low, jnp.zeros_like(low)], axis=1)], axis=0
    )
    both = dot(left, jnp.concatenate(halves(table), axis=0), 1, 0)
    return (both[:DEPTH] + both[DEPTH:])[:rows]


def slot_of_lane(shape):
    return lax.broadcasted_iota(jnp.int32, shape, 1) // SLOT


def choose_slots(blocks):
    slot = slot_of_lane(blocks[0].shape)
    result = blocks[0]
    for q in range(1, len(blocks)):
        result = jnp.where(slot == q, blocks[q], result)
    return result


def repeat_slot(block, q):
    only = jnp.where(slot_of_lane(block.shape) == q, block, 0.0)
    twice = only + pltpu.roll(only, SLOT, 1)
    return twice + pltpu.roll(twice, 2 * SLOT, 1)


def flat(ref):
    return ref.reshape(ref.shape[0], ref.shape[2])


def load_field(ref, rows):
    tiles = ref.shape[0] // rows
    return jnp.concatenate([ref[pl.ds(t, rows, stride=tiles), :] for t in range(tiles)], axis=1)


def store_field(ref, field):
    rows, count = field.shape
    tiles = count // LANES
    for t in range(tiles):
        ref[pl.ds(t, rows, stride=tiles), :] = field[:, t * LANES : (t + 1) * LANES]


def for_rows(count, step):
    together = min(count, 256)

    def body(i, carry):
        step(pl.multiple_of(i * together, together), together)
        return carry

    lax.fori_loop(0, count // together, body, 0)


def move(count, load, store):
    for first in range(0, count, UNROLL):
        rows = [load(u) for u in range(first, first + UNROLL)]
        for u in range(UNROLL):
            store(first + u, rows[u])


def link_blocks(neighbours):
    count = neighbours.shape[1]
    return neighbours.reshape(4, count // LANES, LANES).transpose(1, 0, 2).reshape(-1, LANES)


def gather_blocks(count, links, source, target):
    line = lax.broadcasted_iota(jnp.int32, (8, LANES), 0)
    slot = slot_of_lane((8, LANES))

    def body(block, carry):
        first = pl.multiple_of(block * LANES, LANES)
        mine = links.at[pl.ds(pl.multiple_of(block * (4 * LANES), 4 * LANES), 4 * LANES)]
        for group in range(0, LANES, 8):
            faces = []
            for f in range(4):
                together = jnp.broadcast_to(source[pl.ds(mine[f * LANES + group], 1), :], (8, LANES))
                for u in range(1, 8):
                    row = jnp.broadcast_to(source[pl.ds(mine[f * LANES + group + u], 1), :], (8, LANES))
                    together = jnp.where(line == u, row, together)
                faces.append(together)
            result = faces[0]
            for f in range(1, 4):
                result = jnp.where(slot == f, faces[f], result)
            target[pl.ds(pl.multiple_of(first + group, 8), 8), :] = result
        return carry

    lax.fori_loop(0, count // LANES, body, 0)


def packed(faces):
    return jnp.concatenate([pad_rows(faces[:, f, :], SLOT) for f in range(4)], axis=0)


def repeated(face):
    return stacked_factor(jnp.concatenate([pad_rows(face, SLOT)] * 4, axis=0).T, 0)


def near_half(width):
    return (1 - lax.axis_index("space") % 2) * width


def unpack(source, target, first):
    quarter = source.shape[0]
    for q in range(4):
        start = pl.multiple_of(first + q * quarter, quarter)
        target[pl.ds(start, quarter), :] = repeat_slot(flat(source)[...], q)


def clear(sums):
    flat(sums)[...] = jnp.zeros((sums.shape[0], LANES), jnp.float32)


def dense_sums(block, links, faces, parts_ref, acc):
    lines = TILE // LANES
    first = pl.multiple_of(block * TILE, TILE)
    places, parts = [], []
    for i, f in enumerate(faces):
        for line in range(lines):
            places.append(links[pl.ds((block * lines + line) * 4 + f, 1), :])
        parts.append(parts_ref[i, :, pl.ds(first, TILE)])
    places, parts = jnp.concatenate(places, axis=1), jnp.concatenate(parts, axis=1)
    width = places.shape[1]
    lane = lax.broadcasted_iota(jnp.int32, (TILE, width), 0)
    one = jnp.where((places & (TILE - 1)) == lane, 1.0, 0.0).astype(jnp.bfloat16)
    high = places // TILE
    count = acc.shape[0] // parts.shape[0]
    masked = [jnp.where(high == h, parts, 0.0).astype(jnp.bfloat16) for h in range(count)]
    acc[...] += dot(jnp.concatenate(masked, axis=0), one, 1, 1)


def adjoint_sums(
    width,
    links_in,
    link_lines,
    multipliers,
    lift,
    sums_in,
    sums_rows,
    dense,
    to_near,
    to_far,
    half_rows,
    parts,
    acc,
    links,
    arrived,
):
    del sums_in
    fetch = pltpu.make_async_copy(links_in, links, arrived)
    fetch.start()
    rows = lift.shape[2]
    count = dense.shape[1]
    quarter = width // 4
    half, sums = flat(half_rows), flat(sums_rows)
    field = stacked_field(load_field(multipliers, rows))
    transposed = field.T
    by_row, by_product = range(4 - DENSE), range(4 - DENSE, 4)
    for f in by_row:
        half[f * count : (f + 1) * count, :] = dot(transposed, repeated(0.5 * lift[:, f, :]), 1, 0)
    for i, f in enumerate(by_product):
        face = dot(stacked_factor(pad_rows(0.5 * lift[:, f, :], SLOT), 1), field, 1, 0)
        high, low = halves(face)
        parts[i] = jnp.concatenate([high.astype(jnp.float32), low.astype(jnp.float32)], axis=0)
    acc[...] = jnp.zeros(acc.shape, jnp.float32)
    fetch.wait()

    def body(block, carry):
        dense_sums(block, link_lines, by_product, parts, acc)
        for line in range(TILE // LANES):
            first = block * TILE + line * LANES
            mine = links.at[pl.ds(pl.multiple_of((block * TILE + line * LANES) * 4, 4 * LANES), 4 * LANES)]
            for f in by_row:
                for group in range(0, LANES, 8):
                    rows = half[pl.ds(pl.multiple_of(f * count + first + group, 8), 8), :]
                    for u in range(8):
                        sums[pl.ds(mine[f * LANES + group + u], 1), :] = rows[u : u + 1, :]
        return carry

    lax.fori_loop(0, count // TILE, body, 0)

    def place(h):
        start = pl.multiple_of(h * 2 * SLOT, 2 * SLOT)
        return acc[pl.ds(start, SLOT), :] + acc[pl.ds(pl.multiple_of(start + SLOT, SLOT), SLOT), :]

    near = near_half(width)
    for out, start in ((to_near, near), (to_far, width - near)):
        starts = [pl.multiple_of(4 * count + start + q * quarter, quarter) for q in range(4)]
        added = jnp.concatenate([place((4 * count + start) // TILE + q) for q in range(4)], axis=0).T
        flat(out)[...] = choose_slots([sums[pl.ds(start, quarter), :] for start in starts]) + added
    per_face = count // TILE
    for f in range(4):
        for t in range(per_face):
            dense[f * SLOT : (f + 1) * SLOT, t * TILE : (t + 1) * TILE] = place(f * per_face + t)


def adjoint_inner(multipliers, coefficients, sums_rows, dense, interior, lift, extract, partial, extra_rows):
    rows, count = partial.shape
    sums = flat(sums_rows)
    state = load_field(multipliers, rows)
    coefs = load_field(coefficients, rows)
    field = stacked_field(state)
    inner = dot(stacked_factor(interior[...].T, 1), field, 1, 0)
    own = dot(stacked_factor(0.5 * packed(lift), 1), field, 1, 0) + dense[...]
    moved = choose_slots([sums[f * count : (f + 1) * count, :] for f in range(4)])
    back = packed(extract).T
    partial[...] = state + coefs * inner[:rows] + from_columns(back, own) + from_rows(back, moved)
    flat(extra_rows)[...] = jnp.zeros((extra_rows.shape[0], LANES), jnp.float32)


def spread(first, width, sends, received_rows, extra_rows):
    def scatter(base, together):
        mine = received_rows.at[pl.ds(base, together)]
        places = sends.at[pl.ds(first + base, together)]

        def store(u, row):
            extra_rows[places[u]] = row

        move(together, lambda u: mine[u], store)

    for_rows(width, scatter)


def join_near(width, sends_in, from_near, extra_in, extra_rows, received_rows, sends, arrived):
    del extra_in
    fetch = pltpu.make_async_copy(sends_in, sends, arrived)
    fetch.start()
    unpack(from_near, flat(received_rows), 0)
    fetch.wait()
    spread(near_half(width), width, sends, received_rows, extra_rows)


def join_far(
    width,
    sends_in,
    partial,
    earlier,
    from_far,
    extra_in,
    extract,
    combined,
    to_near,
    to_far,
    pool_rows,
    extra_rows,
    received_rows,
    sends,
    arrived,
):
    del extra_in
    fetch = pltpu.make_async_copy(sends_in, sends, arrived)
    fetch.start()
    rows, count = partial.shape
    quarter = width // 4
    extra, pool = flat(extra_rows), flat(pool_rows)
    pool[4 * count + 2 * width :, :] = jnp.zeros((8, LANES), jnp.float32)
    unpack(from_far, flat(received_rows), 0)
    near = near_half(width)
    fetch.wait()
    spread(width - near, width, sends, received_rows, extra_rows)
    dfaces = choose_slots([extra[f * count : (f + 1) * count, :] for f in range(4)])
    total = partial[...] - load_field(earlier, rows) + from_rows(packed(extract).T, dfaces)
    store_field(combined, total)
    transposed = stacked_field(total).T
    for f in range(4):
        pool[f * count : (f + 1) * count, :] = dot(transposed, repeated(extract[:, f, :]), 1, 0)
    for out, start in ((to_near, near), (to_far, width - near)):
        for q in range(4):
            lanes = slice(q * SLOT, (q + 1) * SLOT)

            def pick(base, together):
                places = sends.at[pl.ds(start + q * quarter + base, together)]
                mine = out.at[pl.ds(base, together)]

                def store(u, row):
                    mine[u, :, lanes] = row

                move(together, lambda u: pool_rows[places[u], :, lanes], store)

            for_rows(quarter, pick)


def tangent_inner(combined, coefficients, interior, extract, lift, base):
    rows, count = base.shape
    state = load_field(combined, rows)
    scaled = load_field(coefficients, rows) * state
    inner = dot(stacked_factor(interior[...], 1), stacked_field(scaled), 1, 0)
    faces = dot(stacked_field(state).T, stacked_factor(packed(extract).T, 0), 1, 0)
    base[...] = state + inner[:rows] + from_rows(0.5 * packed(lift).T, faces)


def tangent_across(
    width, links_in, base, pool_in, from_near, from_far, lift, forward, pool_rows, across_rows, links, arrived
):
    del pool_in
    fetch = pltpu.make_async_copy(links_in, links, arrived)
    fetch.start()
    count = base.shape[1]
    near = near_half(width)
    unpack(from_near, flat(pool_rows), 4 * count + near)
    unpack(from_far, flat(pool_rows), 4 * count + width - near)
    fetch.wait()

    gather_blocks(count, links, flat(pool_rows), flat(across_rows))
    store_field(forward, base[...] + from_rows(0.5 * packed(lift).T, flat(across_rows)[...]))


def call(kernel, outs, operands, scratch=(), table=None, aliases=None, flops=0, buffers=()):
    outs = [out if isinstance(out, jax.ShapeDtypeStruct) else jax.ShapeDtypeStruct(out, jnp.float32) for out in outs]
    buffers = [pltpu.VMEM((rows, 1, LANES), jnp.float32) for rows in scratch] + list(buffers)
    if table is not None:
        buffers += [pltpu.SMEM((table,), jnp.int32), pltpu.SemaphoreType.DMA]
    function = kernel.func if isinstance(kernel, functools.partial) else kernel
    return pl.pallas_call(
        kernel,
        out_shape=outs,
        in_specs=[pl.BlockSpec(memory_space=pltpu.VMEM)] * len(operands),
        out_specs=[pl.BlockSpec(memory_space=pltpu.VMEM)] * len(outs),
        scratch_shapes=buffers,
        input_output_aliases=aliases or {},
        compiler_params=pltpu.CompilerParams(vmem_limit_bytes=VMEM_LIMIT),
        cost_estimate=pl.CostEstimate(flops=flops * 10**9, bytes_accessed=0, transcendentals=0),
        name=function.__name__,
    )(*operands)


def exchange(to_near, to_far, axis):
    devices = lax.axis_size(axis)
    near = [(i, i ^ 1) for i in range(devices)]
    far = [(i, (i + (1 if i % 2 else -1)) % devices) for i in range(devices)]
    return lax.ppermute(to_near, axis, near), lax.ppermute(to_far, axis, far)


def from_behind(array, axis, by):
    devices = lax.axis_size(axis)
    pairs = [(i, i + by) for i in range(devices) if 0 <= i + by < devices]
    return lax.ppermute(array, axis, pairs)


def per_device(multipliers, coefficients, neighbours, send_list, interior, extract, lift):
    rows, count = multipliers.shape[1:]
    width = send_list.shape[0] // 2
    lines = (rows * count // LANES, LANES)
    message = (width // 4, 1, LANES)
    face_rows = (4 * count, 1, LANES)
    pool_rows = (4 * count + 2 * width + 8, 1, LANES)
    own = multipliers.reshape(lines)
    coefs = coefficients.reshape(lines)
    link_lines = link_blocks(neighbours)
    links = link_lines.reshape(-1)
    lift, extract = lift.transpose(2, 0, 1), extract.transpose(1, 0, 2)
    earlier = from_behind(own, "tm", 1)
    (sums,) = call(clear, [pool_rows], (), flops=3)
    sums, dense, to_near, to_far = call(
        functools.partial(adjoint_sums, width),
        [pool_rows, (LANES, count), message, message],
        (links, link_lines, own, lift, sums),
        scratch=((4 - DENSE) * count,),
        buffers=(
            pltpu.VMEM((DENSE, 2 * SLOT, count), jnp.float32),
            pltpu.VMEM(((4 * count + 2 * width) // TILE * 2 * SLOT, TILE), jnp.float32),
        ),
        table=4 * count,
        aliases={4: 0},
        flops=9,
    )
    from_near, from_far = exchange(to_near, to_far, "space")
    partial, extra = call(
        adjoint_inner, [(rows, count), face_rows], (own, coefs, sums, dense, interior, lift, extract), flops=2
    )
    (extra,) = call(
        functools.partial(join_near, width),
        [face_rows],
        (send_list, from_near, extra),
        scratch=(width,),
        table=2 * width,
        aliases={2: 0},
        flops=1,
    )
    combined, to_near, to_far, pool, _ = call(
        functools.partial(join_far, width),
        [lines, message, message, pool_rows, face_rows],
        (send_list, partial, earlier, from_far, extra, extract),
        scratch=(width,),
        table=2 * width,
        aliases={4: 4},
        flops=5,
    )
    later = from_behind(combined, "tm", -1)
    from_near, from_far = exchange(to_near, to_far, "space")
    (base,) = call(tangent_inner, [(rows, count)], (combined, coefs, interior, extract, lift), flops=2)
    forward, _ = call(
        functools.partial(tangent_across, width),
        [lines, pool_rows],
        (links, base, pool, from_near, from_far, lift),
        scratch=(count,),
        table=4 * count,
        aliases={2: 1},
        flops=9,
    )
    return (forward - later).reshape(1, rows, count)


def solution(mesh):
    placed = (
        P(("groups", "tm"), None, "space"),
        P(("groups", "tm"), None, "space"),
        P(None, "space"),
        P("space"),
        P(),
        P(),
        P(),
    )
    return jax.shard_map(
        per_device,
        mesh=mesh,
        in_specs=placed,
        out_specs=P(("groups", "tm"), None, "space"),
        check_vma=False,
    )
```

```python
import functools

import jax
import jax.numpy as jnp
from jax import lax
from jax.experimental import pallas as pl
from jax.experimental.pallas import tpu as pltpu
from jax.sharding import PartitionSpec as P

LANES = 128
SLOT = 32
DEPTH = 64
UNROLL = 32
TILE = 256
DENSE = 1
PULLED = 2
VMEM_LIMIT = 32 * 1024 * 1024


def pad_rows(value, rows):
    missing = rows - value.shape[0]
    if missing == 0:
        return value
    return jnp.concatenate([value, jnp.zeros((missing, value.shape[1]), value.dtype)], axis=0)


def pad_columns(value, columns):
    missing = columns - value.shape[1]
    if missing == 0:
        return value
    return jnp.concatenate([value, jnp.zeros((value.shape[0], missing), value.dtype)], axis=1)


def halves(value):
    high = value.astype(jnp.bfloat16)
    low = (value - high.astype(jnp.float32)).astype(jnp.bfloat16)
    return high, low


def dot(left, right, left_dim, right_dim):
    dims = (((left_dim,), (right_dim,)), ((), ()))
    return lax.dot_general(left, right, dims, preferred_element_type=jnp.float32)


def stacked_field(field):
    high, low = halves(pad_rows(field, DEPTH))
    return jnp.concatenate([high, low, high], axis=0)


def stacked_factor(matrix, axis):
    padded = pad_rows(matrix, DEPTH) if axis == 0 else pad_columns(matrix, DEPTH)
    high, low = halves(padded)
    return jnp.concatenate([high, high, low], axis=axis)


def from_rows(matrix, table):
    rows = matrix.shape[0]
    high, low = halves(pad_rows(matrix, DEPTH))
    left = jnp.concatenate(
        [jnp.concatenate([high, high], axis=1), jnp.concatenate([low, jnp.zeros_like(low)], axis=1)], axis=0
    )
    both = dot(left, jnp.concatenate(halves(table), axis=1), 1, 1)
    return (both[:DEPTH] + both[DEPTH:])[:rows]


def from_columns(matrix, table):
    rows = matrix.shape[0]
    high, low = halves(pad_rows(matrix, DEPTH))
    left = jnp.concatenate(
        [jnp.concatenate([high, high], axis=1), jnp.concatenate([low, jnp.zeros_like(low)], axis=1)], axis=0
    )
    both = dot(left, jnp.concatenate(halves(table), axis=0), 1, 0)
    return (both[:DEPTH] + both[DEPTH:])[:rows]


def slot_of_lane(shape):
    return lax.broadcasted_iota(jnp.int32, shape, 1) // SLOT


def choose_slots(blocks):
    slot = slot_of_lane(blocks[0].shape)
    result = blocks[0]
    for q in range(1, len(blocks)):
        result = jnp.where(slot == q, blocks[q], result)
    return result


def repeat_slot(block, q):
    only = jnp.where(slot_of_lane(block.shape) == q, block, 0.0)
    twice = only + pltpu.roll(only, SLOT, 1)
    return twice + pltpu.roll(twice, 2 * SLOT, 1)


def flat(ref):
    return ref.reshape(ref.shape[0], ref.shape[2])


def load_field(ref, rows):
    tiles = ref.shape[0] // rows
    return jnp.concatenate([ref[pl.ds(t, rows, stride=tiles), :] for t in range(tiles)], axis=1)


def store_field(ref, field):
    rows, count = field.shape
    tiles = count // LANES
    for t in range(tiles):
        ref[pl.ds(t, rows, stride=tiles), :] = field[:, t * LANES : (t + 1) * LANES]


def for_rows(count, step):
    together = min(count, 256)

    def body(i, carry):
        step(pl.multiple_of(i * together, together), together)
        return carry

    lax.fori_loop(0, count // together, body, 0)


def move(count, load, store):
    for first in range(0, count, UNROLL):
        rows = [load(u) for u in range(first, first + UNROLL)]
        for u in range(UNROLL):
            store(first + u, rows[u])


def link_blocks(neighbours):
    count = neighbours.shape[1]
    return neighbours.reshape(4, count // LANES, LANES).transpose(1, 0, 2).reshape(-1, LANES)


def high_and_low(columns):
    return jnp.concatenate(halves(columns), axis=0)


def gather_rows(first, mine, faces, source, target):
    line = lax.broadcasted_iota(jnp.int32, (8, LANES), 0)
    slot = slot_of_lane((8, LANES))
    for group in range(0, LANES, 8):
        result = jnp.zeros((8, LANES), jnp.float32)
        for f in faces:
            together = jnp.broadcast_to(source[pl.ds(mine[f * LANES + group], 1), :], (8, LANES))
            for u in range(1, 8):
                row = jnp.broadcast_to(source[pl.ds(mine[f * LANES + group + u], 1), :], (8, LANES))
                together = jnp.where(line == u, row, together)
            result = jnp.where(slot == f, together, result)
        target[pl.ds(pl.multiple_of(first + group, 8), 8), :] = result


def gather_product(places, tables):
    lane = lax.broadcasted_iota(jnp.int32, (TILE, TILE), 0)
    one = jnp.where((places & (TILE - 1)) == lane, 1.0, 0.0).astype(jnp.bfloat16)
    tile = places // TILE
    result = jnp.zeros((2 * SLOT, TILE), jnp.float32)
    for lines, tiles in tables:
        columns = dot(lines, one, 1, 0)
        for i, at in enumerate(tiles):
            result = jnp.where(tile == at, columns[i * 2 * SLOT : (i + 1) * 2 * SLOT], result)
    return result[:SLOT] + result[SLOT:]


def packed(faces):
    return jnp.concatenate([pad_rows(faces[:, f, :], SLOT) for f in range(4)], axis=0)


def repeated(face):
    return stacked_factor(jnp.concatenate([pad_rows(face, SLOT)] * 4, axis=0).T, 0)


def near_half(width):
    return (1 - lax.axis_index("space") % 2) * width


def unpack(source, target, first):
    quarter = source.shape[0]
    for q in range(4):
        start = pl.multiple_of(first + q * quarter, quarter)
        target[pl.ds(start, quarter), :] = repeat_slot(flat(source)[...], q)


def clear(sums):
    flat(sums)[...] = jnp.zeros((sums.shape[0], LANES), jnp.float32)


def dense_sums(block, links, faces, parts_ref, acc):
    lines = TILE // LANES
    first = pl.multiple_of(block * TILE, TILE)
    places, parts = [], []
    for i, f in enumerate(faces):
        for line in range(lines):
            places.append(links[pl.ds((block * lines + line) * 4 + f, 1), :])
        parts.append(parts_ref[i, :, pl.ds(first, TILE)])
    places, parts = jnp.concatenate(places, axis=1), jnp.concatenate(parts, axis=1)
    width = places.shape[1]
    lane = lax.broadcasted_iota(jnp.int32, (TILE, width), 0)
    one = jnp.where((places & (TILE - 1)) == lane, 1.0, 0.0).astype(jnp.bfloat16)
    high = places // TILE
    count = acc.shape[0] // parts.shape[0]
    masked = [jnp.where(high == h, parts, 0.0).astype(jnp.bfloat16) for h in range(count)]
    acc[...] += dot(jnp.concatenate(masked, axis=0), one, 1, 1)


def adjoint_sums(
    width,
    links_in,
    link_lines,
    multipliers,
    lift,
    sums_in,
    sums_rows,
    dense,
    to_near,
    to_far,
    half_rows,
    parts,
    acc,
    links,
    arrived,
):
    del sums_in
    fetch = pltpu.make_async_copy(links_in, links, arrived)
    fetch.start()
    rows = lift.shape[2]
    count = dense.shape[1]
    quarter = width // 4
    half, sums = flat(half_rows), flat(sums_rows)
    field = stacked_field(load_field(multipliers, rows))
    transposed = field.T
    by_row, by_product = range(4 - DENSE), range(4 - DENSE, 4)
    for f in by_row:
        half[f * count : (f + 1) * count, :] = dot(transposed, repeated(0.5 * lift[:, f, :]), 1, 0)
    for i, f in enumerate(by_product):
        face = dot(stacked_factor(pad_rows(0.5 * lift[:, f, :], SLOT), 1), field, 1, 0)
        high, low = halves(face)
        parts[i] = jnp.concatenate([high.astype(jnp.float32), low.astype(jnp.float32)], axis=0)
    acc[...] = jnp.zeros(acc.shape, jnp.float32)
    fetch.wait()

    def body(block, carry):
        dense_sums(block, link_lines, by_product, parts, acc)
        for line in range(TILE // LANES):
            first = block * TILE + line * LANES
            mine = links.at[pl.ds(pl.multiple_of((block * TILE + line * LANES) * 4, 4 * LANES), 4 * LANES)]
            for f in by_row:
                for group in range(0, LANES, 8):
                    rows = half[pl.ds(pl.multiple_of(f * count + first + group, 8), 8), :]
                    for u in range(8):
                        sums[pl.ds(mine[f * LANES + group + u], 1), :] = rows[u : u + 1, :]
        return carry

    lax.fori_loop(0, count // TILE, body, 0)

    def place(h):
        start = pl.multiple_of(h * 2 * SLOT, 2 * SLOT)
        return acc[pl.ds(start, SLOT), :] + acc[pl.ds(pl.multiple_of(start + SLOT, SLOT), SLOT), :]

    near = near_half(width)
    for out, start in ((to_near, near), (to_far, width - near)):
        starts = [pl.multiple_of(4 * count + start + q * quarter, quarter) for q in range(4)]
        added = jnp.concatenate([place((4 * count + start) // TILE + q) for q in range(4)], axis=0).T
        flat(out)[...] = choose_slots([sums[pl.ds(start, quarter), :] for start in starts]) + added
    per_face = count // TILE
    for f in range(4):
        for t in range(per_face):
            dense[f * SLOT : (f + 1) * SLOT, t * TILE : (t + 1) * TILE] = place(f * per_face + t)


def adjoint_inner(multipliers, coefficients, sums_rows, dense, interior, lift, extract, partial, extra_rows):
    rows, count = partial.shape
    sums = flat(sums_rows)
    state = load_field(multipliers, rows)
    coefs = load_field(coefficients, rows)
    field = stacked_field(state)
    inner = dot(stacked_factor(interior[...].T, 1), field, 1, 0)
    own = dot(stacked_factor(0.5 * packed(lift), 1), field, 1, 0) + dense[...]
    moved = choose_slots([sums[f * count : (f + 1) * count, :] for f in range(4)])
    back = packed(extract).T
    partial[...] = state + coefs * inner[:rows] + from_columns(back, own) + from_rows(back, moved)
    flat(extra_rows)[...] = jnp.zeros((extra_rows.shape[0], LANES), jnp.float32)


def spread(first, width, sends, received_rows, extra_rows):
    def scatter(base, together):
        mine = received_rows.at[pl.ds(base, together)]
        places = sends.at[pl.ds(first + base, together)]

        def store(u, row):
            extra_rows[places[u]] = row

        move(together, lambda u: mine[u], store)

    for_rows(width, scatter)


def join_near(width, sends_in, from_near, extra_in, extra_rows, received_rows, sends, arrived):
    del extra_in
    fetch = pltpu.make_async_copy(sends_in, sends, arrived)
    fetch.start()
    unpack(from_near, flat(received_rows), 0)
    fetch.wait()
    spread(near_half(width), width, sends, received_rows, extra_rows)


def join_far(
    width,
    sends_in,
    partial,
    earlier,
    from_far,
    extra_in,
    extract,
    combined,
    to_near,
    to_far,
    pool_rows,
    extra_rows,
    received_rows,
    sends,
    arrived,
):
    del extra_in
    fetch = pltpu.make_async_copy(sends_in, sends, arrived)
    fetch.start()
    rows, count = partial.shape
    quarter = width // 4
    extra, pool = flat(extra_rows), flat(pool_rows)
    pool[4 * count + 2 * width :, :] = jnp.zeros((8, LANES), jnp.float32)
    unpack(from_far, flat(received_rows), 0)
    near = near_half(width)
    fetch.wait()
    spread(width - near, width, sends, received_rows, extra_rows)
    dfaces = choose_slots([extra[f * count : (f + 1) * count, :] for f in range(4)])
    total = partial[...] - load_field(earlier, rows) + from_rows(packed(extract).T, dfaces)
    store_field(combined, total)
    transposed = stacked_field(total).T
    for f in range(4):
        pool[f * count : (f + 1) * count, :] = dot(transposed, repeated(extract[:, f, :]), 1, 0)
    for out, start in ((to_near, near), (to_far, width - near)):
        for q in range(4):
            lanes = slice(q * SLOT, (q + 1) * SLOT)

            def pick(base, together):
                places = sends.at[pl.ds(start + q * quarter + base, together)]
                mine = out.at[pl.ds(base, together)]

                def store(u, row):
                    mine[u, :, lanes] = row

                move(together, lambda u: pool_rows[places[u], :, lanes], store)

            for_rows(quarter, pick)


def tangent_inner(combined, coefficients, interior, extract, lift, base, columns):
    rows, count = base.shape
    state = load_field(combined, rows)
    scaled = load_field(coefficients, rows) * state
    inner = dot(stacked_factor(interior[...], 1), stacked_field(scaled), 1, 0)
    faces = dot(stacked_factor(packed(extract), 1), stacked_field(state), 1, 0)
    base[...] = state + inner[:rows] + from_columns(0.5 * packed(lift).T, faces)
    per_face = count // TILE
    for f in range(4):
        for t in range(per_face):
            start = (f * per_face + t) * 2 * SLOT
            tile = faces[f * SLOT : (f + 1) * SLOT, t * TILE : (t + 1) * TILE]
            columns[start : start + 2 * SLOT, :] = high_and_low(tile)


def tangent_across(
    width,
    links_in,
    link_lines,
    base,
    pool_in,
    columns,
    from_near,
    from_far,
    lift,
    forward,
    pool_rows,
    across_rows,
    pulled,
    halo,
    links,
    arrived,
):
    del pool_in
    fetch = pltpu.make_async_copy(links_in, links, arrived)
    fetch.start()
    count = base.shape[1]
    pool, across = flat(pool_rows), flat(across_rows)
    near = near_half(width)
    unpack(from_near, pool, 4 * count + near)
    unpack(from_far, pool, 4 * count + width - near)
    halo_tiles = []
    for message, start in ((from_near, near), (from_far, width - near)):
        turned = flat(message)[...].T
        for q in range(4):
            at = len(halo_tiles) * 2 * SLOT
            halo[at : at + 2 * SLOT, :] = high_and_low(turned[q * SLOT : (q + 1) * SLOT, :])
            halo_tiles.append((4 * count + start) // TILE + q)
    own_tiles = list(range(4 * count // TILE))
    by_row, by_product = range(4 - PULLED), range(4 - PULLED, 4)
    fetch.wait()

    def body(block, carry):
        lines = TILE // LANES
        for i, f in enumerate(by_product):
            parts = [link_lines[pl.ds((block * lines + line) * 4 + f, 1), :] for line in range(lines)]
            found = gather_product(
                jnp.concatenate(parts, axis=1), ((columns[...], own_tiles), (halo[...], halo_tiles))
            )
            pulled[i * SLOT : (i + 1) * SLOT, pl.ds(pl.multiple_of(block * TILE, TILE), TILE)] = found
        for line in range(lines):
            first = block * TILE + line * LANES
            gather_rows(first, links.at[pl.ds(pl.multiple_of(first * 4, 4 * LANES), 4 * LANES)], by_row, pool, across)
        return carry

    lax.fori_loop(0, count // TILE, body, 0)
    factor = 0.5 * packed(lift).T
    done = base[...] + from_rows(factor, across[...])
    store_field(forward, done + from_columns(factor[:, (4 - PULLED) * SLOT :], pulled[...]))


def call(kernel, outs, operands, scratch=(), table=None, aliases=None, flops=0, buffers=()):
    outs = [out if isinstance(out, jax.ShapeDtypeStruct) else jax.ShapeDtypeStruct(out, jnp.float32) for out in outs]
    buffers = [pltpu.VMEM((rows, 1, LANES), jnp.float32) for rows in scratch] + list(buffers)
    if table is not None:
        buffers += [pltpu.SMEM((table,), jnp.int32), pltpu.SemaphoreType.DMA]
    function = kernel.func if isinstance(kernel, functools.partial) else kernel
    return pl.pallas_call(
        kernel,
        out_shape=outs,
        in_specs=[pl.BlockSpec(memory_space=pltpu.VMEM)] * len(operands),
        out_specs=[pl.BlockSpec(memory_space=pltpu.VMEM)] * len(outs),
        scratch_shapes=buffers,
        input_output_aliases=aliases or {},
        compiler_params=pltpu.CompilerParams(vmem_limit_bytes=VMEM_LIMIT),
        cost_estimate=pl.CostEstimate(flops=flops * 10**9, bytes_accessed=0, transcendentals=0),
        name=function.__name__,
    )(*operands)


def exchange(to_near, to_far, axis):
    devices = lax.axis_size(axis)
    near = [(i, i ^ 1) for i in range(devices)]
    far = [(i, (i + (1 if i % 2 else -1)) % devices) for i in range(devices)]
    return lax.ppermute(to_near, axis, near), lax.ppermute(to_far, axis, far)


def from_behind(array, axis, by):
    devices = lax.axis_size(axis)
    pairs = [(i, i + by) for i in range(devices) if 0 <= i + by < devices]
    return lax.ppermute(array, axis, pairs)


def per_device(multipliers, coefficients, neighbours, send_list, interior, extract, lift):
    rows, count = multipliers.shape[1:]
    width = send_list.shape[0] // 2
    lines = (rows * count // LANES, LANES)
    message = (width // 4, 1, LANES)
    face_rows = (4 * count, 1, LANES)
    pool_rows = (4 * count + 2 * width + 8, 1, LANES)
    own = multipliers.reshape(lines)
    coefs = coefficients.reshape(lines)
    link_lines = link_blocks(neighbours)
    links = link_lines.reshape(-1)
    lift, extract = lift.transpose(2, 0, 1), extract.transpose(1, 0, 2)
    earlier = from_behind(own, "tm", 1)
    (sums,) = call(clear, [pool_rows], (), flops=3)
    sums, dense, to_near, to_far = call(
        functools.partial(adjoint_sums, width),
        [pool_rows, (LANES, count), message, message],
        (links, link_lines, own, lift, sums),
        scratch=((4 - DENSE) * count,),
        buffers=(
            pltpu.VMEM((DENSE, 2 * SLOT, count), jnp.float32),
            pltpu.VMEM(((4 * count + 2 * width) // TILE * 2 * SLOT, TILE), jnp.float32),
        ),
        table=4 * count,
        aliases={4: 0},
        flops=9,
    )
    from_near, from_far = exchange(to_near, to_far, "space")
    partial, extra = call(
        adjoint_inner, [(rows, count), face_rows], (own, coefs, sums, dense, interior, lift, extract), flops=2
    )
    (extra,) = call(
        functools.partial(join_near, width),
        [face_rows],
        (send_list, from_near, extra),
        scratch=(width,),
        table=2 * width,
        aliases={2: 0},
        flops=1,
    )
    combined, to_near, to_far, pool, _ = call(
        functools.partial(join_far, width),
        [lines, message, message, pool_rows, face_rows],
        (send_list, partial, earlier, from_far, extra, extract),
        scratch=(width,),
        table=2 * width,
        aliases={4: 4},
        flops=5,
    )
    later = from_behind(combined, "tm", -1)
    from_near, from_far = exchange(to_near, to_far, "space")
    tiles = 4 * count // TILE
    base, columns = call(
        tangent_inner,
        [(rows, count), jax.ShapeDtypeStruct((tiles * 2 * SLOT, TILE), jnp.bfloat16)],
        (combined, coefs, interior, extract, lift),
        flops=2,
    )
    forward, _ = call(
        functools.partial(tangent_across, width),
        [lines, pool_rows],
        (links, link_lines, base, pool, columns, from_near, from_far, lift),
        scratch=(count,),
        buffers=(
            pltpu.VMEM((PULLED * SLOT, count), jnp.float32),
            pltpu.VMEM((2 * width // TILE * 2 * SLOT, TILE), jnp.bfloat16),
        ),
        table=4 * count,
        aliases={3: 1},
        flops=0,
    )
    return (forward - later).reshape(1, rows, count)


def solution(mesh):
    placed = (
        P(("groups", "tm"), None, "space"),
        P(("groups", "tm"), None, "space"),
        P(None, "space"),
        P("space"),
        P(),
        P(),
        P(),
    )
    return jax.shard_map(
        per_device,
        mesh=mesh,
        in_specs=placed,
        out_specs=P(("groups", "tm"), None, "space"),
        check_vma=False,
    )
```

```python
import functools

import jax
import jax.numpy as jnp
from jax import lax
from jax.experimental import pallas as pl
from jax.experimental.pallas import tpu as pltpu
from jax.sharding import PartitionSpec as P

LANES = 128
SLOT = 32
DEPTH = 64
UNROLL = 32
TILE = 256
WIDE = 512
DENSE = 2
PULLED = 2
VMEM_LIMIT = 32 * 1024 * 1024


def pad_rows(value, rows):
    missing = rows - value.shape[0]
    if missing == 0:
        return value
    return jnp.concatenate([value, jnp.zeros((missing, value.shape[1]), value.dtype)], axis=0)


def pad_columns(value, columns):
    missing = columns - value.shape[1]
    if missing == 0:
        return value
    return jnp.concatenate([value, jnp.zeros((value.shape[0], missing), value.dtype)], axis=1)


def halves(value):
    high = value.astype(jnp.bfloat16)
    low = (value - high.astype(jnp.float32)).astype(jnp.bfloat16)
    return high, low


def dot(left, right, left_dim, right_dim):
    dims = (((left_dim,), (right_dim,)), ((), ()))
    return lax.dot_general(left, right, dims, preferred_element_type=jnp.float32)


def stacked_field(field):
    high, low = halves(pad_rows(field, DEPTH))
    return jnp.concatenate([high, low, high], axis=0)


def stacked_factor(matrix, axis):
    padded = pad_rows(matrix, DEPTH) if axis == 0 else pad_columns(matrix, DEPTH)
    high, low = halves(padded)
    return jnp.concatenate([high, high, low], axis=axis)


def from_rows(matrix, table):
    rows = matrix.shape[0]
    high, low = halves(pad_rows(matrix, DEPTH))
    left = jnp.concatenate(
        [jnp.concatenate([high, high], axis=1), jnp.concatenate([low, jnp.zeros_like(low)], axis=1)], axis=0
    )
    both = dot(left, jnp.concatenate(halves(table), axis=1), 1, 1)
    return (both[:DEPTH] + both[DEPTH:])[:rows]


def from_columns(matrix, table):
    rows = matrix.shape[0]
    high, low = halves(pad_rows(matrix, DEPTH))
    left = jnp.concatenate(
        [jnp.concatenate([high, high], axis=1), jnp.concatenate([low, jnp.zeros_like(low)], axis=1)], axis=0
    )
    both = dot(left, jnp.concatenate(halves(table), axis=0), 1, 0)
    return (both[:DEPTH] + both[DEPTH:])[:rows]


def slot_of_lane(shape):
    return lax.broadcasted_iota(jnp.int32, shape, 1) // SLOT


def choose_slots(blocks):
    slot = slot_of_lane(blocks[0].shape)
    result = blocks[0]
    for q in range(1, len(blocks)):
        result = jnp.where(slot == q, blocks[q], result)
    return result


def repeat_slot(block, q):
    only = jnp.where(slot_of_lane(block.shape) == q, block, 0.0)
    twice = only + pltpu.roll(only, SLOT, 1)
    return twice + pltpu.roll(twice, 2 * SLOT, 1)


def flat(ref):
    return ref.reshape(ref.shape[0], ref.shape[2])


def load_field(ref, rows):
    tiles = ref.shape[0] // rows
    return jnp.concatenate([ref[pl.ds(t, rows, stride=tiles), :] for t in range(tiles)], axis=1)


def store_field(ref, field):
    rows, count = field.shape
    tiles = count // LANES
    for t in range(tiles):
        ref[pl.ds(t, rows, stride=tiles), :] = field[:, t * LANES : (t + 1) * LANES]


def for_rows(count, step):
    together = min(count, 256)

    def body(i, carry):
        step(pl.multiple_of(i * together, together), together)
        return carry

    lax.fori_loop(0, count // together, body, 0)


def move(count, load, store):
    for first in range(0, count, UNROLL):
        rows = [load(u) for u in range(first, first + UNROLL)]
        for u in range(UNROLL):
            store(first + u, rows[u])


def link_blocks(neighbours):
    count = neighbours.shape[1]
    return neighbours.reshape(4, count // LANES, LANES).transpose(1, 0, 2).reshape(-1, LANES)


def high_and_low(columns):
    return jnp.concatenate(halves(columns), axis=0)


def gather_rows(first, mine, faces, source, target):
    line = lax.broadcasted_iota(jnp.int32, (8, LANES), 0)
    slot = slot_of_lane((8, LANES))
    for group in range(0, LANES, 8):
        result = jnp.zeros((8, LANES), jnp.float32)
        for f in faces:
            together = jnp.broadcast_to(source[pl.ds(mine[f * LANES + group], 1), :], (8, LANES))
            for u in range(1, 8):
                row = jnp.broadcast_to(source[pl.ds(mine[f * LANES + group + u], 1), :], (8, LANES))
                together = jnp.where(line == u, row, together)
            result = jnp.where(slot == f, together, result)
        target[pl.ds(pl.multiple_of(first + group, 8), 8), :] = result


def gather_product(places, tables):
    count = places.shape[1]
    lane = lax.broadcasted_iota(jnp.int32, (TILE, count), 0)
    one = jnp.where((places & (TILE - 1)) == lane, 1.0, 0.0).astype(jnp.bfloat16)
    tile = places // TILE
    result = jnp.zeros((2 * SLOT, count), jnp.float32)
    for lines, tiles in tables:
        columns = dot(lines, one, 1, 0)
        for i, at in enumerate(tiles):
            result = jnp.where(tile == at, columns[i * 2 * SLOT : (i + 1) * 2 * SLOT], result)
    return result[:SLOT] + result[SLOT:]


def packed(faces):
    return jnp.concatenate([pad_rows(faces[:, f, :], SLOT) for f in range(4)], axis=0)


def repeated(face):
    return stacked_factor(jnp.concatenate([pad_rows(face, SLOT)] * 4, axis=0).T, 0)


def near_half(width):
    return (1 - lax.axis_index("space") % 2) * width


def unpack(source, target, first):
    quarter = source.shape[0]
    for q in range(4):
        start = pl.multiple_of(first + q * quarter, quarter)
        target[pl.ds(start, quarter), :] = repeat_slot(flat(source)[...], q)


def clear(sums):
    flat(sums)[...] = jnp.zeros((sums.shape[0], LANES), jnp.float32)


def dense_sums(block, links, faces, parts_ref, acc):
    lines = TILE // LANES
    first = pl.multiple_of(block * TILE, TILE)
    places, parts = [], []
    for i, f in enumerate(faces):
        for line in range(lines):
            places.append(links[pl.ds((block * lines + line) * 4 + f, 1), :])
        parts.append(parts_ref[i, :, pl.ds(first, TILE)])
    places, parts = jnp.concatenate(places, axis=1), jnp.concatenate(parts, axis=1)
    lane = lax.broadcasted_iota(jnp.int32, (WIDE, places.shape[1]), 0)
    one = jnp.where((places & (WIDE - 1)) == lane, 1.0, 0.0).astype(jnp.bfloat16)
    high = places // WIDE
    count = acc.shape[0] // parts.shape[0]
    masked = [jnp.where(high == h, parts, 0.0).astype(jnp.bfloat16) for h in range(count)]
    acc[...] += dot(jnp.concatenate(masked, axis=0), one, 1, 1)


def adjoint_sums(
    width,
    links_in,
    link_lines,
    multipliers,
    lift,
    sums_in,
    sums_rows,
    dense,
    to_near,
    to_far,
    half_rows,
    parts,
    acc,
    links,
    arrived,
):
    del sums_in
    fetch = pltpu.make_async_copy(links_in, links, arrived)
    fetch.start()
    rows = lift.shape[2]
    count = dense.shape[1]
    quarter = width // 4
    half, sums = flat(half_rows), flat(sums_rows)
    field = stacked_field(load_field(multipliers, rows))
    transposed = field.T
    by_row, by_product = range(4 - DENSE), range(4 - DENSE, 4)
    for f in by_row:
        half[f * count : (f + 1) * count, :] = dot(transposed, repeated(0.5 * lift[:, f, :]), 1, 0)
    for i, f in enumerate(by_product):
        face = dot(stacked_factor(pad_rows(0.5 * lift[:, f, :], SLOT), 1), field, 1, 0)
        high, low = halves(face)
        parts[i] = jnp.concatenate([high.astype(jnp.float32), low.astype(jnp.float32)], axis=0)
    acc[...] = jnp.zeros(acc.shape, jnp.float32)
    fetch.wait()

    def body(block, carry):
        dense_sums(block, link_lines, by_product, parts, acc)
        for line in range(TILE // LANES):
            first = block * TILE + line * LANES
            mine = links.at[pl.ds(pl.multiple_of((block * TILE + line * LANES) * 4, 4 * LANES), 4 * LANES)]
            for f in by_row:
                for group in range(0, LANES, 8):
                    rows = half[pl.ds(pl.multiple_of(f * count + first + group, 8), 8), :]
                    for u in range(8):
                        sums[pl.ds(mine[f * LANES + group + u], 1), :] = rows[u : u + 1, :]
        return carry

    lax.fori_loop(0, count // TILE, body, 0)

    def place(tile, part):
        start = pl.multiple_of(tile * 2 * SLOT, 2 * SLOT)
        lanes = slice(part * TILE, (part + 1) * TILE)
        return acc[pl.ds(start, SLOT), lanes] + acc[pl.ds(pl.multiple_of(start + SLOT, SLOT), SLOT), lanes]

    near = near_half(width)
    parts_of = WIDE // TILE
    for out, start in ((to_near, near), (to_far, width - near)):
        starts = [pl.multiple_of(4 * count + start + q * quarter, quarter) for q in range(4)]
        tile = (4 * count + start) // WIDE
        added = jnp.concatenate([place(tile + q // parts_of, q % parts_of) for q in range(4)], axis=0).T
        flat(out)[...] = choose_slots([sums[pl.ds(start, quarter), :] for start in starts]) + added
    per_face = count // TILE
    for f in range(4):
        for t in range(per_face):
            tile, part = divmod(f * per_face + t, parts_of)
            dense[f * SLOT : (f + 1) * SLOT, t * TILE : (t + 1) * TILE] = place(tile, part)


def adjoint_inner(multipliers, coefficients, sums_rows, dense, interior, lift, extract, partial, extra_rows):
    rows, count = partial.shape
    sums = flat(sums_rows)
    state = load_field(multipliers, rows)
    coefs = load_field(coefficients, rows)
    field = stacked_field(state)
    inner = dot(stacked_factor(interior[...].T, 1), field, 1, 0)
    own = dot(stacked_factor(0.5 * packed(lift), 1), field, 1, 0) + dense[...]
    moved = choose_slots([sums[f * count : (f + 1) * count, :] for f in range(4)])
    back = packed(extract).T
    partial[...] = state + coefs * inner[:rows] + from_columns(back, own) + from_rows(back, moved)
    flat(extra_rows)[...] = jnp.zeros((extra_rows.shape[0], LANES), jnp.float32)


def spread(first, width, sends, received_rows, extra_rows):
    def scatter(base, together):
        mine = received_rows.at[pl.ds(base, together)]
        places = sends.at[pl.ds(first + base, together)]

        def store(u, row):
            extra_rows[places[u]] = row

        move(together, lambda u: mine[u], store)

    for_rows(width, scatter)


def join_near(width, sends_in, from_near, extra_in, extra_rows, received_rows, sends, arrived):
    del extra_in
    fetch = pltpu.make_async_copy(sends_in, sends, arrived)
    fetch.start()
    unpack(from_near, flat(received_rows), 0)
    fetch.wait()
    spread(near_half(width), width, sends, received_rows, extra_rows)


def join_far(
    width,
    sends_in,
    partial,
    earlier,
    from_far,
    extra_in,
    extract,
    combined,
    to_near,
    to_far,
    pool_rows,
    extra_rows,
    received_rows,
    sends,
    arrived,
):
    del extra_in
    fetch = pltpu.make_async_copy(sends_in, sends, arrived)
    fetch.start()
    rows, count = partial.shape
    quarter = width // 4
    extra, pool = flat(extra_rows), flat(pool_rows)
    pool[4 * count + 2 * width :, :] = jnp.zeros((8, LANES), jnp.float32)
    unpack(from_far, flat(received_rows), 0)
    near = near_half(width)
    fetch.wait()
    spread(width - near, width, sends, received_rows, extra_rows)
    dfaces = choose_slots([extra[f * count : (f + 1) * count, :] for f in range(4)])
    total = partial[...] - load_field(earlier, rows) + from_rows(packed(extract).T, dfaces)
    store_field(combined, total)
    transposed = stacked_field(total).T
    for f in range(4):
        pool[f * count : (f + 1) * count, :] = dot(transposed, repeated(extract[:, f, :]), 1, 0)
    for out, start in ((to_near, near), (to_far, width - near)):
        for q in range(4):
            lanes = slice(q * SLOT, (q + 1) * SLOT)

            def pick(base, together):
                places = sends.at[pl.ds(start + q * quarter + base, together)]
                mine = out.at[pl.ds(base, together)]

                def store(u, row):
                    mine[u, :, lanes] = row

                move(together, lambda u: pool_rows[places[u], :, lanes], store)

            for_rows(quarter, pick)


def tangent_inner(combined, coefficients, interior, extract, lift, base, columns):
    rows, count = base.shape
    state = load_field(combined, rows)
    scaled = load_field(coefficients, rows) * state
    inner = dot(stacked_factor(interior[...], 1), stacked_field(scaled), 1, 0)
    faces = dot(stacked_factor(packed(extract), 1), stacked_field(state), 1, 0)
    base[...] = state + inner[:rows] + from_columns(0.5 * packed(lift).T, faces)
    per_face = count // TILE
    for f in range(4):
        for t in range(per_face):
            start = (f * per_face + t) * 2 * SLOT
            tile = faces[f * SLOT : (f + 1) * SLOT, t * TILE : (t + 1) * TILE]
            columns[start : start + 2 * SLOT, :] = high_and_low(tile)


def tangent_across(
    width,
    links_in,
    link_lines,
    base,
    pool_in,
    columns,
    from_near,
    from_far,
    lift,
    forward,
    pool_rows,
    across_rows,
    pulled,
    halo,
    links,
    arrived,
):
    del pool_in
    fetch = pltpu.make_async_copy(links_in, links, arrived)
    fetch.start()
    count = base.shape[1]
    pool, across = flat(pool_rows), flat(across_rows)
    near = near_half(width)
    unpack(from_near, pool, 4 * count + near)
    unpack(from_far, pool, 4 * count + width - near)
    halo_tiles = []
    for message, start in ((from_near, near), (from_far, width - near)):
        turned = flat(message)[...].T
        for q in range(4):
            at = len(halo_tiles) * 2 * SLOT
            halo[at : at + 2 * SLOT, :] = high_and_low(turned[q * SLOT : (q + 1) * SLOT, :])
            halo_tiles.append((4 * count + start) // TILE + q)
    own_tiles = list(range(4 * count // TILE))
    by_row, by_product = range(4 - PULLED), range(4 - PULLED, 4)
    fetch.wait()

    def body(block, carry):
        lines = WIDE // LANES
        for i, f in enumerate(by_product):
            parts = [link_lines[pl.ds((block * lines + line) * 4 + f, 1), :] for line in range(lines)]
            found = gather_product(
                jnp.concatenate(parts, axis=1), ((columns[...], own_tiles), (halo[...], halo_tiles))
            )
            pulled[i * SLOT : (i + 1) * SLOT, pl.ds(pl.multiple_of(block * WIDE, WIDE), WIDE)] = found
        for line in range(lines):
            first = block * WIDE + line * LANES
            gather_rows(first, links.at[pl.ds(pl.multiple_of(first * 4, 4 * LANES), 4 * LANES)], by_row, pool, across)
        return carry

    lax.fori_loop(0, count // WIDE, body, 0)
    factor = 0.5 * packed(lift).T
    done = base[...] + from_rows(factor, across[...])
    store_field(forward, done + from_columns(factor[:, (4 - PULLED) * SLOT :], pulled[...]))


def call(kernel, outs, operands, scratch=(), table=None, aliases=None, flops=0, buffers=()):
    outs = [out if isinstance(out, jax.ShapeDtypeStruct) else jax.ShapeDtypeStruct(out, jnp.float32) for out in outs]
    buffers = [pltpu.VMEM((rows, 1, LANES), jnp.float32) for rows in scratch] + list(buffers)
    if table is not None:
        buffers += [pltpu.SMEM((table,), jnp.int32), pltpu.SemaphoreType.DMA]
    function = kernel.func if isinstance(kernel, functools.partial) else kernel
    return pl.pallas_call(
        kernel,
        out_shape=outs,
        in_specs=[pl.BlockSpec(memory_space=pltpu.VMEM)] * len(operands),
        out_specs=[pl.BlockSpec(memory_space=pltpu.VMEM)] * len(outs),
        scratch_shapes=buffers,
        input_output_aliases=aliases or {},
        compiler_params=pltpu.CompilerParams(vmem_limit_bytes=VMEM_LIMIT),
        cost_estimate=pl.CostEstimate(flops=flops * 10**9, bytes_accessed=0, transcendentals=0),
        name=function.__name__,
    )(*operands)


def exchange(to_near, to_far, axis):
    devices = lax.axis_size(axis)
    near = [(i, i ^ 1) for i in range(devices)]
    far = [(i, (i + (1 if i % 2 else -1)) % devices) for i in range(devices)]
    return lax.ppermute(to_near, axis, near), lax.ppermute(to_far, axis, far)


def from_behind(array, axis, by):
    devices = lax.axis_size(axis)
    pairs = [(i, i + by) for i in range(devices) if 0 <= i + by < devices]
    return lax.ppermute(array, axis, pairs)


def per_device(multipliers, coefficients, neighbours, send_list, interior, extract, lift):
    rows, count = multipliers.shape[1:]
    width = send_list.shape[0] // 2
    lines = (rows * count // LANES, LANES)
    message = (width // 4, 1, LANES)
    face_rows = (4 * count, 1, LANES)
    pool_rows = (4 * count + 2 * width + 8, 1, LANES)
    own = multipliers.reshape(lines)
    coefs = coefficients.reshape(lines)
    link_lines = link_blocks(neighbours)
    links = link_lines.reshape(-1)
    lift, extract = lift.transpose(2, 0, 1), extract.transpose(1, 0, 2)
    earlier = from_behind(own, "tm", 1)
    (sums,) = call(clear, [pool_rows], (), flops=3)
    sums, dense, to_near, to_far = call(
        functools.partial(adjoint_sums, width),
        [pool_rows, (LANES, count), message, message],
        (links, link_lines, own, lift, sums),
        scratch=((4 - DENSE) * count,),
        buffers=(
            pltpu.VMEM((DENSE, 2 * SLOT, count), jnp.float32),
            pltpu.VMEM(((4 * count + 2 * width) // WIDE * 2 * SLOT, WIDE), jnp.float32),
        ),
        table=4 * count,
        aliases={4: 0},
        flops=9,
    )
    from_near, from_far = exchange(to_near, to_far, "space")
    partial, extra = call(
        adjoint_inner, [(rows, count), face_rows], (own, coefs, sums, dense, interior, lift, extract), flops=2
    )
    (extra,) = call(
        functools.partial(join_near, width),
        [face_rows],
        (send_list, from_near, extra),
        scratch=(width,),
        table=2 * width,
        aliases={2: 0},
        flops=1,
    )
    combined, to_near, to_far, pool, _ = call(
        functools.partial(join_far, width),
        [lines, message, message, pool_rows, face_rows],
        (send_list, partial, earlier, from_far, extra, extract),
        scratch=(width,),
        table=2 * width,
        aliases={4: 4},
        flops=5,
    )
    later = from_behind(combined, "tm", -1)
    from_near, from_far = exchange(to_near, to_far, "space")
    tiles = 4 * count // TILE
    base, columns = call(
        tangent_inner,
        [(rows, count), jax.ShapeDtypeStruct((tiles * 2 * SLOT, TILE), jnp.bfloat16)],
        (combined, coefs, interior, extract, lift),
        flops=2,
    )
    forward, _ = call(
        functools.partial(tangent_across, width),
        [lines, pool_rows],
        (links, link_lines, base, pool, columns, from_near, from_far, lift),
        scratch=(count,),
        buffers=(
            pltpu.VMEM((PULLED * SLOT, count), jnp.float32),
            pltpu.VMEM((2 * width // TILE * 2 * SLOT, TILE), jnp.bfloat16),
        ),
        table=4 * count,
        aliases={3: 1},
        flops=0,
    )
    return (forward - later).reshape(1, rows, count)


def solution(mesh):
    placed = (
        P(("groups", "tm"), None, "space"),
        P(("groups", "tm"), None, "space"),
        P(None, "space"),
        P("space"),
        P(),
        P(),
        P(),
    )
    return jax.shard_map(
        per_device,
        mesh=mesh,
        in_specs=placed,
        out_specs=P(("groups", "tm"), None, "space"),
        check_vma=False,
    )
```

```python
import functools

import jax
import jax.numpy as jnp
from jax import lax
from jax.experimental import pallas as pl
from jax.experimental.pallas import tpu as pltpu
from jax.sharding import PartitionSpec as P

LANES = 128
SLOT = 32
DEPTH = 64
UNROLL = 32
TILE = 256
WIDE = 512
DENSE = 1
PULLED = 1
VMEM_LIMIT = 32 * 1024 * 1024


def pad_rows(value, rows):
    missing = rows - value.shape[0]
    if missing == 0:
        return value
    return jnp.concatenate([value, jnp.zeros((missing, value.shape[1]), value.dtype)], axis=0)


def pad_columns(value, columns):
    missing = columns - value.shape[1]
    if missing == 0:
        return value
    return jnp.concatenate([value, jnp.zeros((value.shape[0], missing), value.dtype)], axis=1)


def halves(value):
    high = value.astype(jnp.bfloat16)
    low = (value - high.astype(jnp.float32)).astype(jnp.bfloat16)
    return high, low


def dot(left, right, left_dim, right_dim):
    dims = (((left_dim,), (right_dim,)), ((), ()))
    return lax.dot_general(left, right, dims, preferred_element_type=jnp.float32)


def stacked_field(field):
    high, low = halves(pad_rows(field, DEPTH))
    return jnp.concatenate([high, low, high], axis=0)


def stacked_factor(matrix, axis):
    padded = pad_rows(matrix, DEPTH) if axis == 0 else pad_columns(matrix, DEPTH)
    high, low = halves(padded)
    return jnp.concatenate([high, high, low], axis=axis)


def from_rows(matrix, table):
    rows = matrix.shape[0]
    high, low = halves(pad_rows(matrix, DEPTH))
    left = jnp.concatenate(
        [jnp.concatenate([high, high], axis=1), jnp.concatenate([low, jnp.zeros_like(low)], axis=1)], axis=0
    )
    both = dot(left, jnp.concatenate(halves(table), axis=1), 1, 1)
    return (both[:DEPTH] + both[DEPTH:])[:rows]


def from_columns(matrix, table):
    rows = matrix.shape[0]
    high, low = halves(pad_rows(matrix, DEPTH))
    left = jnp.concatenate(
        [jnp.concatenate([high, high], axis=1), jnp.concatenate([low, jnp.zeros_like(low)], axis=1)], axis=0
    )
    both = dot(left, jnp.concatenate(halves(table), axis=0), 1, 0)
    return (both[:DEPTH] + both[DEPTH:])[:rows]


def slot_of_lane(shape):
    return lax.broadcasted_iota(jnp.int32, shape, 1) // SLOT


def choose_slots(blocks):
    slot = slot_of_lane(blocks[0].shape)
    result = blocks[0]
    for q in range(1, len(blocks)):
        result = jnp.where(slot == q, blocks[q], result)
    return result


def repeat_slot(block, q):
    only = jnp.where(slot_of_lane(block.shape) == q, block, 0.0)
    twice = only + pltpu.roll(only, SLOT, 1)
    return twice + pltpu.roll(twice, 2 * SLOT, 1)


def flat(ref):
    return ref.reshape(ref.shape[0], ref.shape[2])


def load_field(ref, rows):
    tiles = ref.shape[0] // rows
    return jnp.concatenate([ref[pl.ds(t, rows, stride=tiles), :] for t in range(tiles)], axis=1)


def store_field(ref, field):
    rows, count = field.shape
    tiles = count // LANES
    for t in range(tiles):
        ref[pl.ds(t, rows, stride=tiles), :] = field[:, t * LANES : (t + 1) * LANES]


def for_rows(count, step):
    together = min(count, 256)

    def body(i, carry):
        step(pl.multiple_of(i * together, together), together)
        return carry

    lax.fori_loop(0, count // together, body, 0)


def move(count, load, store):
    for first in range(0, count, UNROLL):
        rows = [load(u) for u in range(first, first + UNROLL)]
        for u in range(UNROLL):
            store(first + u, rows[u])


def link_blocks(neighbours):
    count = neighbours.shape[1]
    return neighbours.reshape(4, count // LANES, LANES).transpose(1, 0, 2).reshape(-1, LANES)


def high_and_low(columns):
    return jnp.concatenate(halves(columns), axis=0)


def gather_rows(first, mine, faces, source, target):
    line = lax.broadcasted_iota(jnp.int32, (8, LANES), 0)
    slot = slot_of_lane((8, LANES))
    for group in range(0, LANES, 8):
        result = jnp.zeros((8, LANES), jnp.float32)
        for f in faces:
            together = jnp.broadcast_to(source[pl.ds(mine[f * LANES + group], 1), :], (8, LANES))
            for u in range(1, 8):
                row = jnp.broadcast_to(source[pl.ds(mine[f * LANES + group + u], 1), :], (8, LANES))
                together = jnp.where(line == u, row, together)
            result = jnp.where(slot == f, together, result)
        target[pl.ds(pl.multiple_of(first + group, 8), 8), :] = result


def gather_product(places, tables):
    count = places.shape[1]
    lane = lax.broadcasted_iota(jnp.int32, (TILE, count), 0)
    one = jnp.where((places & (TILE - 1)) == lane, 1.0, 0.0).astype(jnp.bfloat16)
    tile = places // TILE
    result = jnp.zeros((2 * SLOT, count), jnp.float32)
    for lines, tiles in tables:
        columns = dot(lines, one, 1, 0)
        for i, at in enumerate(tiles):
            result = jnp.where(tile == at, columns[i * 2 * SLOT : (i + 1) * 2 * SLOT], result)
    return result[:SLOT] + result[SLOT:]


def packed(faces):
    return jnp.concatenate([pad_rows(faces[:, f, :], SLOT) for f in range(4)], axis=0)


def repeated(face):
    return stacked_factor(jnp.concatenate([pad_rows(face, SLOT)] * 4, axis=0).T, 0)


def near_half(width):
    return (1 - lax.axis_index("space") % 2) * width


def unpack(source, target, first):
    quarter = source.shape[0]
    for q in range(4):
        start = pl.multiple_of(first + q * quarter, quarter)
        target[pl.ds(start, quarter), :] = repeat_slot(flat(source)[...], q)


def clear(sums):
    flat(sums)[...] = jnp.zeros((sums.shape[0], LANES), jnp.float32)


def dense_sums(block, links, faces, parts_ref, acc):
    lines = TILE // LANES
    first = pl.multiple_of(block * TILE, TILE)
    places, parts = [], []
    for i, f in enumerate(faces):
        for line in range(lines):
            places.append(links[pl.ds((block * lines + line) * 4 + f, 1), :])
        parts.append(parts_ref[i, :, pl.ds(first, TILE)])
    places, parts = jnp.concatenate(places, axis=1), jnp.concatenate(parts, axis=1)
    width = places.shape[1]
    lane = lax.broadcasted_iota(jnp.int32, (TILE, width), 0)
    one = jnp.where((places & (TILE - 1)) == lane, 1.0, 0.0).astype(jnp.bfloat16)
    high = places // TILE
    count = acc.shape[0] // parts.shape[0]
    masked = [jnp.where(high == h, parts, 0.0).astype(jnp.bfloat16) for h in range(count)]
    acc[...] += dot(jnp.concatenate(masked, axis=0), one, 1, 1)


def adjoint_sums(
    width,
    links_in,
    link_lines,
    multipliers,
    lift,
    sums_in,
    sums_rows,
    dense,
    to_near,
    to_far,
    half_rows,
    parts,
    acc,
    links,
    arrived,
):
    del sums_in
    fetch = pltpu.make_async_copy(links_in, links, arrived)
    fetch.start()
    rows = lift.shape[2]
    count = dense.shape[1]
    quarter = width // 4
    half, sums = flat(half_rows), flat(sums_rows)
    field = stacked_field(load_field(multipliers, rows))
    transposed = field.T
    by_row, by_product = range(4 - DENSE), range(4 - DENSE, 4)
    for f in by_row:
        half[f * count : (f + 1) * count, :] = dot(transposed, repeated(0.5 * lift[:, f, :]), 1, 0)
    for i, f in enumerate(by_product):
        face = dot(stacked_factor(pad_rows(0.5 * lift[:, f, :], SLOT), 1), field, 1, 0)
        high, low = halves(face)
        parts[i] = jnp.concatenate([high.astype(jnp.float32), low.astype(jnp.float32)], axis=0)
    acc[...] = jnp.zeros(acc.shape, jnp.float32)
    fetch.wait()

    def body(block, carry):
        dense_sums(block, link_lines, by_product, parts, acc)
        for line in range(TILE // LANES):
            first = block * TILE + line * LANES
            mine = links.at[pl.ds(pl.multiple_of((block * TILE + line * LANES) * 4, 4 * LANES), 4 * LANES)]
            for f in by_row:
                for group in range(0, LANES, 8):
                    rows = half[pl.ds(pl.multiple_of(f * count + first + group, 8), 8), :]
                    for u in range(8):
                        sums[pl.ds(mine[f * LANES + group + u], 1), :] = rows[u : u + 1, :]
        return carry

    lax.fori_loop(0, count // TILE, body, 0)

    def place(h):
        start = pl.multiple_of(h * 2 * SLOT, 2 * SLOT)
        return acc[pl.ds(start, SLOT), :] + acc[pl.ds(pl.multiple_of(start + SLOT, SLOT), SLOT), :]

    near = near_half(width)
    for out, start in ((to_near, near), (to_far, width - near)):
        starts = [pl.multiple_of(4 * count + start + q * quarter, quarter) for q in range(4)]
        added = jnp.concatenate([place((4 * count + start) // TILE + q) for q in range(4)], axis=0).T
        flat(out)[...] = choose_slots([sums[pl.ds(start, quarter), :] for start in starts]) + added
    per_face = count // TILE
    for f in range(4):
        for t in range(per_face):
            dense[f * SLOT : (f + 1) * SLOT, t * TILE : (t + 1) * TILE] = place(f * per_face + t)


def adjoint_inner(multipliers, coefficients, sums_rows, dense, interior, lift, extract, partial, extra_rows):
    rows, count = partial.shape
    sums = flat(sums_rows)
    state = load_field(multipliers, rows)
    coefs = load_field(coefficients, rows)
    field = stacked_field(state)
    inner = dot(stacked_factor(interior[...].T, 1), field, 1, 0)
    own = dot(stacked_factor(0.5 * packed(lift), 1), field, 1, 0) + dense[...]
    moved = choose_slots([sums[f * count : (f + 1) * count, :] for f in range(4)])
    back = packed(extract).T
    partial[...] = state + coefs * inner[:rows] + from_columns(back, own) + from_rows(back, moved)
    flat(extra_rows)[...] = jnp.zeros((extra_rows.shape[0], LANES), jnp.float32)


def spread(first, width, sends, received_rows, extra_rows):
    def scatter(base, together):
        mine = received_rows.at[pl.ds(base, together)]
        places = sends.at[pl.ds(first + base, together)]

        def store(u, row):
            extra_rows[places[u]] = row

        move(together, lambda u: mine[u], store)

    for_rows(width, scatter)


def join_near(width, sends_in, from_near, extra_in, extra_rows, received_rows, sends, arrived):
    del extra_in
    fetch = pltpu.make_async_copy(sends_in, sends, arrived)
    fetch.start()
    unpack(from_near, flat(received_rows), 0)
    fetch.wait()
    spread(near_half(width), width, sends, received_rows, extra_rows)


def pick(first, width, sends, pool_rows, out):
    quarter = width // 4
    for q in range(4):
        lanes = slice(q * SLOT, (q + 1) * SLOT)

        def group(base, together):
            places = sends.at[pl.ds(first + q * quarter + base, together)]
            mine = out.at[pl.ds(base, together)]

            def store(u, row):
                mine[u, :, lanes] = row

            move(together, lambda u: pool_rows[places[u], :, lanes], store)

        for_rows(quarter, group)


def join_far(
    width,
    sends_in,
    partial,
    earlier,
    from_far,
    extra_in,
    extract,
    combined,
    to_far,
    pool_rows,
    extra_rows,
    received_rows,
    sends,
    arrived,
):
    del extra_in
    fetch = pltpu.make_async_copy(sends_in, sends, arrived)
    fetch.start()
    rows, count = partial.shape
    extra, pool = flat(extra_rows), flat(pool_rows)
    pool[4 * count + 2 * width :, :] = jnp.zeros((8, LANES), jnp.float32)
    unpack(from_far, flat(received_rows), 0)
    far = width - near_half(width)
    fetch.wait()
    spread(far, width, sends, received_rows, extra_rows)
    dfaces = choose_slots([extra[f * count : (f + 1) * count, :] for f in range(4)])
    total = partial[...] - load_field(earlier, rows) + from_rows(packed(extract).T, dfaces)
    store_field(combined, total)
    transposed = stacked_field(total).T
    for f in range(4):
        pool[f * count : (f + 1) * count, :] = dot(transposed, repeated(extract[:, f, :]), 1, 0)
    pick(far, width, sends, pool_rows, to_far)


def pick_near(width, sends_in, pool_rows, to_near, sends, arrived):
    fetch = pltpu.make_async_copy(sends_in, sends, arrived)
    fetch.start()
    fetch.wait()
    pick(near_half(width), width, sends, pool_rows, to_near)


def take(message, start, pool, halo):
    unpack(message, pool, start)
    turned = flat(message)[...].T
    for q in range(4):
        halo[q * 2 * SLOT : (q + 1) * 2 * SLOT, :] = high_and_low(turned[q * SLOT : (q + 1) * SLOT, :])


def tangent_inner(
    width,
    combined,
    coefficients,
    interior,
    extract,
    lift,
    pool_in,
    from_far,
    base,
    columns,
    pool_rows,
    far_halo,
):
    del pool_in
    rows, count = base.shape
    take(from_far, 4 * count + width - near_half(width), flat(pool_rows), far_halo)
    state = load_field(combined, rows)
    scaled = load_field(coefficients, rows) * state
    inner = dot(stacked_factor(interior[...], 1), stacked_field(scaled), 1, 0)
    faces = dot(stacked_factor(packed(extract), 1), stacked_field(state), 1, 0)
    base[...] = state + inner[:rows] + from_columns(0.5 * packed(lift).T, faces)
    per_face = count // TILE
    for f in range(4):
        for t in range(per_face):
            start = (f * per_face + t) * 2 * SLOT
            tile = faces[f * SLOT : (f + 1) * SLOT, t * TILE : (t + 1) * TILE]
            columns[start : start + 2 * SLOT, :] = high_and_low(tile)


def tangent_across(
    width,
    links_in,
    link_lines,
    base,
    pool_in,
    columns,
    far_halo,
    from_near,
    lift,
    forward,
    pool_rows,
    across_rows,
    pulled,
    near_halo,
    links,
    arrived,
):
    del pool_in
    fetch = pltpu.make_async_copy(links_in, links, arrived)
    fetch.start()
    count = base.shape[1]
    pool, across = flat(pool_rows), flat(across_rows)
    near = near_half(width)
    take(from_near, 4 * count + near, pool, near_halo)
    near_tiles = [(4 * count + near) // TILE + q for q in range(4)]
    far_tiles = [(4 * count + width - near) // TILE + q for q in range(4)]
    own_tiles = list(range(4 * count // TILE))
    by_row, by_product = range(4 - PULLED), range(4 - PULLED, 4)
    fetch.wait()

    def body(block, carry):
        lines = WIDE // LANES
        for i, f in enumerate(by_product):
            parts = [link_lines[pl.ds((block * lines + line) * 4 + f, 1), :] for line in range(lines)]
            tables = ((columns[...], own_tiles), (near_halo[...], near_tiles), (far_halo[...], far_tiles))
            found = gather_product(jnp.concatenate(parts, axis=1), tables)
            pulled[i * SLOT : (i + 1) * SLOT, pl.ds(pl.multiple_of(block * WIDE, WIDE), WIDE)] = found
        for line in range(lines):
            first = block * WIDE + line * LANES
            gather_rows(first, links.at[pl.ds(pl.multiple_of(first * 4, 4 * LANES), 4 * LANES)], by_row, pool, across)
        return carry

    lax.fori_loop(0, count // WIDE, body, 0)
    factor = 0.5 * packed(lift).T
    done = base[...] + from_rows(factor, across[...])
    store_field(forward, done + from_columns(factor[:, (4 - PULLED) * SLOT :], pulled[...]))


def call(kernel, outs, operands, scratch=(), table=None, aliases=None, flops=0, buffers=()):
    outs = [out if isinstance(out, jax.ShapeDtypeStruct) else jax.ShapeDtypeStruct(out, jnp.float32) for out in outs]
    buffers = [pltpu.VMEM((rows, 1, LANES), jnp.float32) for rows in scratch] + list(buffers)
    if table is not None:
        buffers += [pltpu.SMEM((table,), jnp.int32), pltpu.SemaphoreType.DMA]
    function = kernel.func if isinstance(kernel, functools.partial) else kernel
    return pl.pallas_call(
        kernel,
        out_shape=outs,
        in_specs=[pl.BlockSpec(memory_space=pltpu.VMEM)] * len(operands),
        out_specs=[pl.BlockSpec(memory_space=pltpu.VMEM)] * len(outs),
        scratch_shapes=buffers,
        input_output_aliases=aliases or {},
        compiler_params=pltpu.CompilerParams(vmem_limit_bytes=VMEM_LIMIT),
        cost_estimate=pl.CostEstimate(flops=flops * 10**9, bytes_accessed=0, transcendentals=0),
        name=function.__name__,
    )(*operands)


def exchange(to_near, to_far, axis):
    devices = lax.axis_size(axis)
    near = [(i, i ^ 1) for i in range(devices)]
    far = [(i, (i + (1 if i % 2 else -1)) % devices) for i in range(devices)]
    return lax.ppermute(to_near, axis, near), lax.ppermute(to_far, axis, far)


def from_behind(array, axis, by):
    devices = lax.axis_size(axis)
    pairs = [(i, i + by) for i in range(devices) if 0 <= i + by < devices]
    return lax.ppermute(array, axis, pairs)


def per_device(multipliers, coefficients, neighbours, send_list, interior, extract, lift):
    rows, count = multipliers.shape[1:]
    width = send_list.shape[0] // 2
    lines = (rows * count // LANES, LANES)
    message = (width // 4, 1, LANES)
    face_rows = (4 * count, 1, LANES)
    pool_rows = (4 * count + 2 * width + 8, 1, LANES)
    own = multipliers.reshape(lines)
    coefs = coefficients.reshape(lines)
    link_lines = link_blocks(neighbours)
    links = link_lines.reshape(-1)
    lift, extract = lift.transpose(2, 0, 1), extract.transpose(1, 0, 2)
    earlier = from_behind(own, "tm", 1)
    (sums,) = call(clear, [pool_rows], (), flops=3)
    sums, dense, to_near, to_far = call(
        functools.partial(adjoint_sums, width),
        [pool_rows, (LANES, count), message, message],
        (links, link_lines, own, lift, sums),
        scratch=((4 - DENSE) * count,),
        buffers=(
            pltpu.VMEM((DENSE, 2 * SLOT, count), jnp.float32),
            pltpu.VMEM(((4 * count + 2 * width) // TILE * 2 * SLOT, TILE), jnp.float32),
        ),
        table=4 * count,
        aliases={4: 0},
        flops=9,
    )
    from_near, from_far = exchange(to_near, to_far, "space")
    partial, extra = call(
        adjoint_inner, [(rows, count), face_rows], (own, coefs, sums, dense, interior, lift, extract), flops=2
    )
    (extra,) = call(
        functools.partial(join_near, width),
        [face_rows],
        (send_list, from_near, extra),
        scratch=(width,),
        table=2 * width,
        aliases={2: 0},
        flops=1,
    )
    combined, to_far, pool, _ = call(
        functools.partial(join_far, width),
        [lines, message, pool_rows, face_rows],
        (send_list, partial, earlier, from_far, extra, extract),
        scratch=(width,),
        table=2 * width,
        aliases={4: 3},
        flops=5,
    )
    (to_near,) = call(
        functools.partial(pick_near, width), [message], (send_list, pool), table=2 * width, flops=2
    )
    later = from_behind(combined, "tm", -1)
    from_near, from_far = exchange(to_near, to_far, "space")
    tiles = 4 * count // TILE
    half_halo = jax.ShapeDtypeStruct((width // TILE * 2 * SLOT, TILE), jnp.bfloat16)
    base, columns, pool, far_halo = call(
        functools.partial(tangent_inner, width),
        [
            (rows, count),
            jax.ShapeDtypeStruct((tiles * 2 * SLOT, TILE), jnp.bfloat16),
            pool_rows,
            half_halo,
        ],
        (combined, coefs, interior, extract, lift, pool, from_far),
        aliases={5: 2},
        flops=4,
    )
    forward, _ = call(
        functools.partial(tangent_across, width),
        [lines, pool_rows],
        (links, link_lines, base, pool, columns, far_halo, from_near, lift),
        scratch=(count,),
        buffers=(
            pltpu.VMEM((PULLED * SLOT, count), jnp.float32),
            pltpu.VMEM(half_halo.shape, half_halo.dtype),
        ),
        table=4 * count,
        aliases={3: 1},
        flops=0,
    )
    return (forward - later).reshape(1, rows, count)


def solution(mesh):
    placed = (
        P(("groups", "tm"), None, "space"),
        P(("groups", "tm"), None, "space"),
        P(None, "space"),
        P("space"),
        P(),
        P(),
        P(),
    )
    return jax.shard_map(
        per_device,
        mesh=mesh,
        in_specs=placed,
        out_specs=P(("groups", "tm"), None, "space"),
        check_vma=False,
    )
```

```python
import functools

import jax
import jax.numpy as jnp
from jax import lax
from jax.experimental import pallas as pl
from jax.experimental.pallas import tpu as pltpu
from jax.sharding import PartitionSpec as P

LANES = 128
SLOT = 32
DEPTH = 64
UNROLL = 32
TILE = 256
DENSE = 1
PULLED = 1
VMEM_LIMIT = 32 * 1024 * 1024


def pad_rows(value, rows):
    missing = rows - value.shape[0]
    if missing == 0:
        return value
    return jnp.concatenate([value, jnp.zeros((missing, value.shape[1]), value.dtype)], axis=0)


def pad_columns(value, columns):
    missing = columns - value.shape[1]
    if missing == 0:
        return value
    return jnp.concatenate([value, jnp.zeros((value.shape[0], missing), value.dtype)], axis=1)


def halves(value):
    high = value.astype(jnp.bfloat16)
    low = (value - high.astype(jnp.float32)).astype(jnp.bfloat16)
    return high, low


def dot(left, right, left_dim, right_dim):
    dims = (((left_dim,), (right_dim,)), ((), ()))
    return lax.dot_general(left, right, dims, preferred_element_type=jnp.float32)


def stacked_field(field):
    high, low = halves(pad_rows(field, DEPTH))
    return jnp.concatenate([high, low, high], axis=0)


def stacked_factor(matrix, axis):
    padded = pad_rows(matrix, DEPTH) if axis == 0 else pad_columns(matrix, DEPTH)
    high, low = halves(padded)
    return jnp.concatenate([high, high, low], axis=axis)


def from_rows(matrix, table):
    rows = matrix.shape[0]
    high, low = halves(pad_rows(matrix, DEPTH))
    left = jnp.concatenate(
        [jnp.concatenate([high, high], axis=1), jnp.concatenate([low, jnp.zeros_like(low)], axis=1)], axis=0
    )
    both = dot(left, jnp.concatenate(halves(table), axis=1), 1, 1)
    return (both[:DEPTH] + both[DEPTH:])[:rows]


def from_columns(matrix, table):
    rows = matrix.shape[0]
    high, low = halves(pad_rows(matrix, DEPTH))
    left = jnp.concatenate(
        [jnp.concatenate([high, high], axis=1), jnp.concatenate([low, jnp.zeros_like(low)], axis=1)], axis=0
    )
    both = dot(left, jnp.concatenate(halves(table), axis=0), 1, 0)
    return (both[:DEPTH] + both[DEPTH:])[:rows]


def slot_of_lane(shape):
    return lax.broadcasted_iota(jnp.int32, shape, 1) // SLOT


def choose_slots(blocks):
    slot = slot_of_lane(blocks[0].shape)
    result = blocks[0]
    for q in range(1, len(blocks)):
        result = jnp.where(slot == q, blocks[q], result)
    return result


def repeat_slot(block, q):
    only = jnp.where(slot_of_lane(block.shape) == q, block, 0.0)
    twice = only + pltpu.roll(only, SLOT, 1)
    return twice + pltpu.roll(twice, 2 * SLOT, 1)


def flat(ref):
    return ref.reshape(ref.shape[0], ref.shape[2])


def load_field(ref, rows):
    tiles = ref.shape[0] // rows
    return jnp.concatenate([ref[pl.ds(t, rows, stride=tiles), :] for t in range(tiles)], axis=1)


def store_field(ref, field):
    rows, count = field.shape
    tiles = count // LANES
    for t in range(tiles):
        ref[pl.ds(t, rows, stride=tiles), :] = field[:, t * LANES : (t + 1) * LANES]


def for_rows(count, step):
    together = min(count, 256)

    def body(i, carry):
        step(pl.multiple_of(i * together, together), together)
        return carry

    lax.fori_loop(0, count // together, body, 0)


def move(count, load, store):
    for first in range(0, count, UNROLL):
        rows = [load(u) for u in range(first, first + UNROLL)]
        for u in range(UNROLL):
            store(first + u, rows[u])


def link_blocks(neighbours):
    count = neighbours.shape[1]
    return neighbours.reshape(4, count // LANES, LANES).transpose(1, 0, 2).reshape(-1, LANES)


def high_and_low(columns):
    return jnp.concatenate(halves(columns), axis=0)


def gather_rows(first, mine, faces, source, target):
    to = target.at[pl.ds(first, LANES)]
    for f in faces:
        lanes = slice(f * SLOT, (f + 1) * SLOT)

        def store(u, row, lanes=lanes):
            to[u, :, lanes] = row

        move(LANES, lambda u, f=f, lanes=lanes: source[mine[f * LANES + u], :, lanes], store)


def gather_product(places, tables):
    count = places.shape[1]
    lane = lax.broadcasted_iota(jnp.int32, (TILE, count), 0)
    one = jnp.where((places & (TILE - 1)) == lane, 1.0, 0.0).astype(jnp.bfloat16)
    tile = places // TILE
    result = jnp.zeros((2 * SLOT, count), jnp.float32)
    for lines, tiles in tables:
        columns = dot(lines, one, 1, 0)
        for i, at in enumerate(tiles):
            result = jnp.where(tile == at, columns[i * 2 * SLOT : (i + 1) * 2 * SLOT], result)
    return result[:SLOT] + result[SLOT:]


def packed(faces):
    return jnp.concatenate([pad_rows(faces[:, f, :], SLOT) for f in range(4)], axis=0)


def repeated(face):
    return stacked_factor(jnp.concatenate([pad_rows(face, SLOT)] * 4, axis=0).T, 0)


def near_half(width):
    return (1 - lax.axis_index("space") % 2) * width


def unpack(source, target, first):
    quarter = source.shape[0]
    for q in range(4):
        start = pl.multiple_of(first + q * quarter, quarter)
        target[pl.ds(start, quarter), :] = repeat_slot(flat(source)[...], q)


def clear(sums):
    flat(sums)[...] = jnp.zeros((sums.shape[0], LANES), jnp.float32)


def dense_sums(block, links, faces, parts_ref, acc):
    lines = TILE // LANES
    first = pl.multiple_of(block * TILE, TILE)
    places, parts = [], []
    for i, f in enumerate(faces):
        for line in range(lines):
            places.append(links[pl.ds((block * lines + line) * 4 + f, 1), :])
        parts.append(parts_ref[i, :, pl.ds(first, TILE)])
    places, parts = jnp.concatenate(places, axis=1), jnp.concatenate(parts, axis=1)
    width = places.shape[1]
    lane = lax.broadcasted_iota(jnp.int32, (TILE, width), 0)
    one = jnp.where((places & (TILE - 1)) == lane, 1.0, 0.0).astype(jnp.bfloat16)
    high = places // TILE
    count = acc.shape[0] // parts.shape[0]
    masked = [jnp.where(high == h, parts, 0.0).astype(jnp.bfloat16) for h in range(count)]
    acc[...] += dot(jnp.concatenate(masked, axis=0), one, 1, 1)


def adjoint_sums(
    width,
    links_in,
    link_lines,
    multipliers,
    lift,
    sums_in,
    sums_rows,
    dense,
    to_near,
    to_far,
    half_rows,
    parts,
    acc,
    links,
    arrived,
):
    del sums_in
    fetch = pltpu.make_async_copy(links_in, links, arrived)
    fetch.start()
    rows = lift.shape[2]
    count = dense.shape[1]
    quarter = width // 4
    half, sums = flat(half_rows), flat(sums_rows)
    field = stacked_field(load_field(multipliers, rows))
    transposed = field.T
    by_row, by_product = range(4 - DENSE), range(4 - DENSE, 4)
    for f in by_row:
        half[f * count : (f + 1) * count, :] = dot(transposed, repeated(0.5 * lift[:, f, :]), 1, 0)
    for i, f in enumerate(by_product):
        face = dot(stacked_factor(pad_rows(0.5 * lift[:, f, :], SLOT), 1), field, 1, 0)
        high, low = halves(face)
        parts[i] = jnp.concatenate([high.astype(jnp.float32), low.astype(jnp.float32)], axis=0)
    acc[...] = jnp.zeros(acc.shape, jnp.float32)
    fetch.wait()

    def body(block, carry):
        dense_sums(block, link_lines, by_product, parts, acc)
        for line in range(TILE // LANES):
            first = block * TILE + line * LANES
            mine = links.at[pl.ds(pl.multiple_of((block * TILE + line * LANES) * 4, 4 * LANES), 4 * LANES)]
            for f in by_row:
                for group in range(0, LANES, 8):
                    rows = half[pl.ds(pl.multiple_of(f * count + first + group, 8), 8), :]
                    for u in range(8):
                        sums[pl.ds(mine[f * LANES + group + u], 1), :] = rows[u : u + 1, :]
        return carry

    lax.fori_loop(0, count // TILE, body, 0)

    def place(h):
        start = pl.multiple_of(h * 2 * SLOT, 2 * SLOT)
        return acc[pl.ds(start, SLOT), :] + acc[pl.ds(pl.multiple_of(start + SLOT, SLOT), SLOT), :]

    near = near_half(width)
    for out, start in ((to_near, near), (to_far, width - near)):
        starts = [pl.multiple_of(4 * count + start + q * quarter, quarter) for q in range(4)]
        added = jnp.concatenate([place((4 * count + start) // TILE + q) for q in range(4)], axis=0).T
        flat(out)[...] = choose_slots([sums[pl.ds(start, quarter), :] for start in starts]) + added
    per_face = count // TILE
    for f in range(4):
        for t in range(per_face):
            dense[f * SLOT : (f + 1) * SLOT, t * TILE : (t + 1) * TILE] = place(f * per_face + t)


def adjoint_inner(multipliers, coefficients, sums_rows, dense, interior, lift, extract, partial, extra_rows):
    rows, count = partial.shape
    sums = flat(sums_rows)
    state = load_field(multipliers, rows)
    coefs = load_field(coefficients, rows)
    field = stacked_field(state)
    inner = dot(stacked_factor(interior[...].T, 1), field, 1, 0)
    own = dot(stacked_factor(0.5 * packed(lift), 1), field, 1, 0) + dense[...]
    moved = choose_slots([sums[f * count : (f + 1) * count, :] for f in range(4)])
    back = packed(extract).T
    partial[...] = state + coefs * inner[:rows] + from_columns(back, own) + from_rows(back, moved)
    flat(extra_rows)[...] = jnp.zeros((extra_rows.shape[0], LANES), jnp.float32)


def spread(first, width, sends, received_rows, extra_rows):
    def scatter(base, together):
        mine = received_rows.at[pl.ds(base, together)]
        places = sends.at[pl.ds(first + base, together)]

        def store(u, row):
            extra_rows[places[u]] = row

        move(together, lambda u: mine[u], store)

    for_rows(width, scatter)


def join_near(width, sends_in, from_near, extra_in, extra_rows, received_rows, sends, arrived):
    del extra_in
    fetch = pltpu.make_async_copy(sends_in, sends, arrived)
    fetch.start()
    unpack(from_near, flat(received_rows), 0)
    fetch.wait()
    spread(near_half(width), width, sends, received_rows, extra_rows)


def pick(first, width, sends, pool_rows, out):
    quarter = width // 4
    for q in range(4):
        lanes = slice(q * SLOT, (q + 1) * SLOT)

        def group(base, together):
            places = sends.at[pl.ds(first + q * quarter + base, together)]
            mine = out.at[pl.ds(base, together)]

            def store(u, row):
                mine[u, :, lanes] = row

            move(together, lambda u: pool_rows[places[u], :, lanes], store)

        for_rows(quarter, group)


def join_far(
    width,
    sends_in,
    partial,
    earlier,
    from_far,
    extra_in,
    extract,
    combined,
    to_far,
    pool_rows,
    extra_rows,
    received_rows,
    sends,
    arrived,
):
    del extra_in
    fetch = pltpu.make_async_copy(sends_in, sends, arrived)
    fetch.start()
    rows, count = partial.shape
    extra, pool = flat(extra_rows), flat(pool_rows)
    pool[4 * count + 2 * width :, :] = jnp.zeros((8, LANES), jnp.float32)
    unpack(from_far, flat(received_rows), 0)
    far = width - near_half(width)
    fetch.wait()
    spread(far, width, sends, received_rows, extra_rows)
    dfaces = choose_slots([extra[f * count : (f + 1) * count, :] for f in range(4)])
    total = partial[...] - load_field(earlier, rows) + from_rows(packed(extract).T, dfaces)
    store_field(combined, total)
    transposed = stacked_field(total).T
    for f in range(4):
        pool[f * count : (f + 1) * count, :] = dot(transposed, repeated(extract[:, f, :]), 1, 0)
    pick(far, width, sends, pool_rows, to_far)


def pick_near(width, sends_in, pool_rows, to_near, sends, arrived):
    fetch = pltpu.make_async_copy(sends_in, sends, arrived)
    fetch.start()
    fetch.wait()
    pick(near_half(width), width, sends, pool_rows, to_near)


def take(message, start, pool, halo):
    unpack(message, pool, start)
    turned = flat(message)[...].T
    for q in range(4):
        halo[q * 2 * SLOT : (q + 1) * 2 * SLOT, :] = high_and_low(turned[q * SLOT : (q + 1) * SLOT, :])


def tangent_inner(
    width,
    combined,
    coefficients,
    interior,
    extract,
    lift,
    pool_in,
    from_far,
    base,
    columns,
    pool_rows,
    far_halo,
):
    del pool_in
    rows, count = base.shape
    take(from_far, 4 * count + width - near_half(width), flat(pool_rows), far_halo)
    state = load_field(combined, rows)
    scaled = load_field(coefficients, rows) * state
    inner = dot(stacked_factor(interior[...], 1), stacked_field(scaled), 1, 0)
    faces = dot(stacked_factor(packed(extract), 1), stacked_field(state), 1, 0)
    base[...] = state + inner[:rows] + from_columns(0.5 * packed(lift).T, faces)
    per_face = count // TILE
    for f in range(4):
        for t in range(per_face):
            start = (f * per_face + t) * 2 * SLOT
            tile = faces[f * SLOT : (f + 1) * SLOT, t * TILE : (t + 1) * TILE]
            columns[start : start + 2 * SLOT, :] = high_and_low(tile)


def tangent_across(
    width,
    links_in,
    link_lines,
    base,
    pool_in,
    columns,
    far_halo,
    from_near,
    lift,
    forward,
    pool_rows,
    across_rows,
    pulled,
    near_halo,
    links,
    arrived,
):
    del pool_in
    fetch = pltpu.make_async_copy(links_in, links, arrived)
    fetch.start()
    count = base.shape[1]
    pool, across = flat(pool_rows), flat(across_rows)
    near = near_half(width)
    take(from_near, 4 * count + near, pool, near_halo)
    near_tiles = [(4 * count + near) // TILE + q for q in range(4)]
    far_tiles = [(4 * count + width - near) // TILE + q for q in range(4)]
    own_tiles = list(range(4 * count // TILE))
    by_row, by_product = range(4 - PULLED), range(4 - PULLED, 4)
    fetch.wait()

    across[...] = jnp.zeros(across.shape, jnp.float32)

    def body(block, carry):
        lines = TILE // LANES
        for i, f in enumerate(by_product):
            parts = [link_lines[pl.ds((block * lines + line) * 4 + f, 1), :] for line in range(lines)]
            tables = ((columns[...], own_tiles), (near_halo[...], near_tiles), (far_halo[...], far_tiles))
            found = gather_product(jnp.concatenate(parts, axis=1), tables)
            pulled[i * SLOT : (i + 1) * SLOT, pl.ds(pl.multiple_of(block * TILE, TILE), TILE)] = found
        for line in range(lines):
            first = pl.multiple_of(block * TILE + line * LANES, LANES)
            mine = links.at[pl.ds(pl.multiple_of(first * 4, 4 * LANES), 4 * LANES)]
            gather_rows(first, mine, by_row, pool_rows, across_rows)
        return carry

    lax.fori_loop(0, count // TILE, body, 0)
    factor = 0.5 * packed(lift).T
    done = base[...] + from_rows(factor, across[...])
    store_field(forward, done + from_columns(factor[:, (4 - PULLED) * SLOT :], pulled[...]))


def call(kernel, outs, operands, scratch=(), table=None, aliases=None, flops=0, buffers=()):
    outs = [out if isinstance(out, jax.ShapeDtypeStruct) else jax.ShapeDtypeStruct(out, jnp.float32) for out in outs]
    buffers = [pltpu.VMEM((rows, 1, LANES), jnp.float32) for rows in scratch] + list(buffers)
    if table is not None:
        buffers += [pltpu.SMEM((table,), jnp.int32), pltpu.SemaphoreType.DMA]
    function = kernel.func if isinstance(kernel, functools.partial) else kernel
    return pl.pallas_call(
        kernel,
        out_shape=outs,
        in_specs=[pl.BlockSpec(memory_space=pltpu.VMEM)] * len(operands),
        out_specs=[pl.BlockSpec(memory_space=pltpu.VMEM)] * len(outs),
        scratch_shapes=buffers,
        input_output_aliases=aliases or {},
        compiler_params=pltpu.CompilerParams(vmem_limit_bytes=VMEM_LIMIT),
        cost_estimate=pl.CostEstimate(flops=flops * 10**9, bytes_accessed=0, transcendentals=0),
        name=function.__name__,
    )(*operands)


def exchange(to_near, to_far, axis):
    devices = lax.axis_size(axis)
    near = [(i, i ^ 1) for i in range(devices)]
    far = [(i, (i + (1 if i % 2 else -1)) % devices) for i in range(devices)]
    return lax.ppermute(to_near, axis, near), lax.ppermute(to_far, axis, far)


def from_behind(array, axis, by):
    devices = lax.axis_size(axis)
    pairs = [(i, i + by) for i in range(devices) if 0 <= i + by < devices]
    return lax.ppermute(array, axis, pairs)


def per_device(multipliers, coefficients, neighbours, send_list, interior, extract, lift):
    rows, count = multipliers.shape[1:]
    width = send_list.shape[0] // 2
    lines = (rows * count // LANES, LANES)
    message = (width // 4, 1, LANES)
    face_rows = (4 * count, 1, LANES)
    pool_rows = (4 * count + 2 * width + 8, 1, LANES)
    own = multipliers.reshape(lines)
    coefs = coefficients.reshape(lines)
    link_lines = link_blocks(neighbours)
    links = link_lines.reshape(-1)
    lift, extract = lift.transpose(2, 0, 1), extract.transpose(1, 0, 2)
    earlier = from_behind(own, "tm", 1)
    (sums,) = call(clear, [pool_rows], (), flops=3)
    sums, dense, to_near, to_far = call(
        functools.partial(adjoint_sums, width),
        [pool_rows, (LANES, count), message, message],
        (links, link_lines, own, lift, sums),
        scratch=((4 - DENSE) * count,),
        buffers=(
            pltpu.VMEM((DENSE, 2 * SLOT, count), jnp.float32),
            pltpu.VMEM(((4 * count + 2 * width) // TILE * 2 * SLOT, TILE), jnp.float32),
        ),
        table=4 * count,
        aliases={4: 0},
        flops=9,
    )
    from_near, from_far = exchange(to_near, to_far, "space")
    partial, extra = call(
        adjoint_inner, [(rows, count), face_rows], (own, coefs, sums, dense, interior, lift, extract), flops=2
    )
    (extra,) = call(
        functools.partial(join_near, width),
        [face_rows],
        (send_list, from_near, extra),
        scratch=(width,),
        table=2 * width,
        aliases={2: 0},
        flops=1,
    )
    combined, to_far, pool, _ = call(
        functools.partial(join_far, width),
        [lines, message, pool_rows, face_rows],
        (send_list, partial, earlier, from_far, extra, extract),
        scratch=(width,),
        table=2 * width,
        aliases={4: 3},
        flops=5,
    )
    (to_near,) = call(
        functools.partial(pick_near, width), [message], (send_list, pool), table=2 * width, flops=2
    )
    later = from_behind(combined, "tm", -1)
    from_near, from_far = exchange(to_near, to_far, "space")
    tiles = 4 * count // TILE
    half_halo = jax.ShapeDtypeStruct((width // TILE * 2 * SLOT, TILE), jnp.bfloat16)
    base, columns, pool, far_halo = call(
        functools.partial(tangent_inner, width),
        [
            (rows, count),
            jax.ShapeDtypeStruct((tiles * 2 * SLOT, TILE), jnp.bfloat16),
            pool_rows,
            half_halo,
        ],
        (combined, coefs, interior, extract, lift, pool, from_far),
        aliases={5: 2},
        flops=4,
    )
    forward, _ = call(
        functools.partial(tangent_across, width),
        [lines, pool_rows],
        (links, link_lines, base, pool, columns, far_halo, from_near, lift),
        scratch=(count,),
        buffers=(
            pltpu.VMEM((PULLED * SLOT, count), jnp.float32),
            pltpu.VMEM(half_halo.shape, half_halo.dtype),
        ),
        table=4 * count,
        aliases={3: 1},
        flops=0,
    )
    return (forward - later).reshape(1, rows, count)


def solution(mesh):
    placed = (
        P(("groups", "tm"), None, "space"),
        P(("groups", "tm"), None, "space"),
        P(None, "space"),
        P("space"),
        P(),
        P(),
        P(),
    )
    return jax.shard_map(
        per_device,
        mesh=mesh,
        in_specs=placed,
        out_specs=P(("groups", "tm"), None, "space"),
        check_vma=False,
    )
```

```python
import functools

import jax
import jax.numpy as jnp
from jax import lax
from jax.experimental import pallas as pl
from jax.experimental.pallas import tpu as pltpu
from jax.sharding import PartitionSpec as P

LANES = 128
SLOT = 32
DEPTH = 64
UNROLL = 32
TILE = 256
DENSE = 1
VMEM_LIMIT = 32 * 1024 * 1024


def pad_rows(value, rows):
    missing = rows - value.shape[0]
    if missing == 0:
        return value
    return jnp.concatenate([value, jnp.zeros((missing, value.shape[1]), value.dtype)], axis=0)


def pad_columns(value, columns):
    missing = columns - value.shape[1]
    if missing == 0:
        return value
    return jnp.concatenate([value, jnp.zeros((value.shape[0], missing), value.dtype)], axis=1)


def halves(value):
    high = value.astype(jnp.bfloat16)
    low = (value - high.astype(jnp.float32)).astype(jnp.bfloat16)
    return high, low


def dot(left, right, left_dim, right_dim):
    dims = (((left_dim,), (right_dim,)), ((), ()))
    return lax.dot_general(left, right, dims, preferred_element_type=jnp.float32)


def stacked_field(field):
    high, low = halves(pad_rows(field, DEPTH))
    return jnp.concatenate([high, low, high], axis=0)


def stacked_factor(matrix, axis):
    padded = pad_rows(matrix, DEPTH) if axis == 0 else pad_columns(matrix, DEPTH)
    high, low = halves(padded)
    return jnp.concatenate([high, high, low], axis=axis)


def from_rows(matrix, table):
    rows = matrix.shape[0]
    high, low = halves(pad_rows(matrix, DEPTH))
    left = jnp.concatenate(
        [jnp.concatenate([high, high], axis=1), jnp.concatenate([low, jnp.zeros_like(low)], axis=1)], axis=0
    )
    both = dot(left, jnp.concatenate(halves(table), axis=1), 1, 1)
    return (both[:DEPTH] + both[DEPTH:])[:rows]


def from_columns(matrix, table):
    rows = matrix.shape[0]
    high, low = halves(pad_rows(matrix, DEPTH))
    left = jnp.concatenate(
        [jnp.concatenate([high, high], axis=1), jnp.concatenate([low, jnp.zeros_like(low)], axis=1)], axis=0
    )
    both = dot(left, jnp.concatenate(halves(table), axis=0), 1, 0)
    return (both[:DEPTH] + both[DEPTH:])[:rows]


def slot_of_lane(shape):
    return lax.broadcasted_iota(jnp.int32, shape, 1) // SLOT


def choose_slots(blocks):
    slot = slot_of_lane(blocks[0].shape)
    result = blocks[0]
    for q in range(1, len(blocks)):
        result = jnp.where(slot == q, blocks[q], result)
    return result


def repeat_slot(block, q):
    only = jnp.where(slot_of_lane(block.shape) == q, block, 0.0)
    twice = only + pltpu.roll(only, SLOT, 1)
    return twice + pltpu.roll(twice, 2 * SLOT, 1)


def flat(ref):
    return ref.reshape(ref.shape[0], ref.shape[2])


def load_field(ref, rows):
    tiles = ref.shape[0] // rows
    return jnp.concatenate([ref[pl.ds(t, rows, stride=tiles), :] for t in range(tiles)], axis=1)


def store_field(ref, field):
    rows, count = field.shape
    tiles = count // LANES
    for t in range(tiles):
        ref[pl.ds(t, rows, stride=tiles), :] = field[:, t * LANES : (t + 1) * LANES]


def for_rows(count, step):
    together = min(count, 256)

    def body(i, carry):
        step(pl.multiple_of(i * together, together), together)
        return carry

    lax.fori_loop(0, count // together, body, 0)


def move(count, load, store):
    for first in range(0, count, UNROLL):
        rows = [load(u) for u in range(first, first + UNROLL)]
        for u in range(UNROLL):
            store(first + u, rows[u])


def link_blocks(neighbours):
    count = neighbours.shape[1]
    return neighbours.reshape(4, count // LANES, LANES).transpose(1, 0, 2).reshape(-1, LANES)


def gather_blocks(count, links, source, target):
    line = lax.broadcasted_iota(jnp.int32, (8, LANES), 0)
    slot = slot_of_lane((8, LANES))

    def body(block, carry):
        first = pl.multiple_of(block * LANES, LANES)
        mine = links.at[pl.ds(pl.multiple_of(block * (4 * LANES), 4 * LANES), 4 * LANES)]
        for group in range(0, LANES, 8):
            faces = []
            for f in range(4):
                together = jnp.broadcast_to(source[pl.ds(mine[f * LANES + group], 1), :], (8, LANES))
                for u in range(1, 8):
                    row = jnp.broadcast_to(source[pl.ds(mine[f * LANES + group + u], 1), :], (8, LANES))
                    together = jnp.where(line == u, row, together)
                faces.append(together)
            result = faces[0]
            for f in range(1, 4):
                result = jnp.where(slot == f, faces[f], result)
            target[pl.ds(pl.multiple_of(first + group, 8), 8), :] = result
        return carry

    lax.fori_loop(0, count // LANES, body, 0)


def packed(faces):
    return jnp.concatenate([pad_rows(faces[:, f, :], SLOT) for f in range(4)], axis=0)


def repeated(face):
    return stacked_factor(jnp.concatenate([pad_rows(face, SLOT)] * 4, axis=0).T, 0)


def near_half(width):
    return (1 - lax.axis_index("space") % 2) * width


def unpack(source, target, first):
    quarter = source.shape[0]
    for q in range(4):
        start = pl.multiple_of(first + q * quarter, quarter)
        target[pl.ds(start, quarter), :] = repeat_slot(flat(source)[...], q)


def clear(sums):
    flat(sums)[...] = jnp.zeros((sums.shape[0], LANES), jnp.float32)


def dense_sums(block, links, faces, parts_ref, acc):
    lines = TILE // LANES
    first = pl.multiple_of(block * TILE, TILE)
    places, parts = [], []
    for i, f in enumerate(faces):
        for line in range(lines):
            places.append(links[pl.ds((block * lines + line) * 4 + f, 1), :])
        parts.append(parts_ref[i, :, pl.ds(first, TILE)])
    places, parts = jnp.concatenate(places, axis=1), jnp.concatenate(parts, axis=1)
    width = places.shape[1]
    lane = lax.broadcasted_iota(jnp.int32, (TILE, width), 0)
    one = jnp.where((places & (TILE - 1)) == lane, 1.0, 0.0).astype(jnp.bfloat16)
    high = places // TILE
    count = acc.shape[0] // parts.shape[0]
    masked = [jnp.where(high == h, parts, 0.0).astype(jnp.bfloat16) for h in range(count)]
    acc[...] += dot(jnp.concatenate(masked, axis=0), one, 1, 1)


def adjoint_sums(
    width,
    links_in,
    link_lines,
    multipliers,
    lift,
    sums_in,
    sums_rows,
    dense,
    to_near,
    to_far,
    half_rows,
    parts,
    acc,
    links,
    arrived,
):
    del sums_in
    fetch = pltpu.make_async_copy(links_in, links, arrived)
    fetch.start()
    rows = lift.shape[2]
    count = dense.shape[1]
    quarter = width // 4
    half, sums = flat(half_rows), flat(sums_rows)
    field = stacked_field(load_field(multipliers, rows))
    transposed = field.T
    by_row, by_product = range(4 - DENSE), range(4 - DENSE, 4)
    for f in by_row:
        half[f * count : (f + 1) * count, :] = dot(transposed, repeated(0.5 * lift[:, f, :]), 1, 0)
    for i, f in enumerate(by_product):
        face = dot(stacked_factor(pad_rows(0.5 * lift[:, f, :], SLOT), 1), field, 1, 0)
        high, low = halves(face)
        parts[i] = jnp.concatenate([high.astype(jnp.float32), low.astype(jnp.float32)], axis=0)
    acc[...] = jnp.zeros(acc.shape, jnp.float32)
    fetch.wait()

    def body(block, carry):
        dense_sums(block, link_lines, by_product, parts, acc)
        for line in range(TILE // LANES):
            first = block * TILE + line * LANES
            mine = links.at[pl.ds(pl.multiple_of((block * TILE + line * LANES) * 4, 4 * LANES), 4 * LANES)]
            for f in by_row:
                for group in range(0, LANES, 8):
                    rows = half[pl.ds(pl.multiple_of(f * count + first + group, 8), 8), :]
                    for u in range(8):
                        sums[pl.ds(mine[f * LANES + group + u], 1), :] = rows[u : u + 1, :]
        return carry

    lax.fori_loop(0, count // TILE, body, 0)

    def place(h):
        start = pl.multiple_of(h * 2 * SLOT, 2 * SLOT)
        return acc[pl.ds(start, SLOT), :] + acc[pl.ds(pl.multiple_of(start + SLOT, SLOT), SLOT), :]

    near = near_half(width)
    for out, start in ((to_near, near), (to_far, width - near)):
        starts = [pl.multiple_of(4 * count + start + q * quarter, quarter) for q in range(4)]
        added = jnp.concatenate([place((4 * count + start) // TILE + q) for q in range(4)], axis=0).T
        flat(out)[...] = choose_slots([sums[pl.ds(start, quarter), :] for start in starts]) + added
    per_face = count // TILE
    for f in range(4):
        for t in range(per_face):
            dense[f * SLOT : (f + 1) * SLOT, t * TILE : (t + 1) * TILE] = place(f * per_face + t)


def adjoint_inner(multipliers, coefficients, sums_rows, dense, interior, lift, extract, partial, extra_rows):
    rows, count = partial.shape
    sums = flat(sums_rows)
    state = load_field(multipliers, rows)
    coefs = load_field(coefficients, rows)
    field = stacked_field(state)
    inner = dot(stacked_factor(interior[...].T, 1), field, 1, 0)
    own = dot(stacked_factor(0.5 * packed(lift), 1), field, 1, 0) + dense[...]
    moved = choose_slots([sums[f * count : (f + 1) * count, :] for f in range(4)])
    back = packed(extract).T
    partial[...] = state + coefs * inner[:rows] + from_columns(back, own) + from_rows(back, moved)
    flat(extra_rows)[...] = jnp.zeros((extra_rows.shape[0], LANES), jnp.float32)


def spread(first, width, sends, received_rows, extra_rows):
    def scatter(base, together):
        mine = received_rows.at[pl.ds(base, together)]
        places = sends.at[pl.ds(first + base, together)]

        def store(u, row):
            extra_rows[places[u]] = row

        move(together, lambda u: mine[u], store)

    for_rows(width, scatter)


def join_near(width, sends_in, from_near, extra_in, extra_rows, received_rows, sends, arrived):
    del extra_in
    fetch = pltpu.make_async_copy(sends_in, sends, arrived)
    fetch.start()
    unpack(from_near, flat(received_rows), 0)
    fetch.wait()
    spread(near_half(width), width, sends, received_rows, extra_rows)


def pick(first, width, sends, pool_rows, out):
    quarter = width // 4
    for q in range(4):
        lanes = slice(q * SLOT, (q + 1) * SLOT)

        def group(base, together):
            places = sends.at[pl.ds(first + q * quarter + base, together)]
            mine = out.at[pl.ds(base, together)]

            def store(u, row):
                mine[u, :, lanes] = row

            move(together, lambda u: pool_rows[places[u], :, lanes], store)

        for_rows(quarter, group)


def join_far(
    width,
    sends_in,
    partial,
    earlier,
    from_far,
    extra_in,
    extract,
    combined,
    to_far,
    pool_rows,
    extra_rows,
    received_rows,
    sends,
    arrived,
):
    del extra_in
    fetch = pltpu.make_async_copy(sends_in, sends, arrived)
    fetch.start()
    rows, count = partial.shape
    extra, pool = flat(extra_rows), flat(pool_rows)
    pool[4 * count + 2 * width :, :] = jnp.zeros((8, LANES), jnp.float32)
    unpack(from_far, flat(received_rows), 0)
    far = width - near_half(width)
    fetch.wait()
    spread(far, width, sends, received_rows, extra_rows)
    dfaces = choose_slots([extra[f * count : (f + 1) * count, :] for f in range(4)])
    total = partial[...] - load_field(earlier, rows) + from_rows(packed(extract).T, dfaces)
    store_field(combined, total)
    transposed = stacked_field(total).T
    for f in range(4):
        pool[f * count : (f + 1) * count, :] = dot(transposed, repeated(extract[:, f, :]), 1, 0)
    pick(far, width, sends, pool_rows, to_far)


def pick_near(width, sends_in, pool_rows, to_near, sends, arrived):
    fetch = pltpu.make_async_copy(sends_in, sends, arrived)
    fetch.start()
    fetch.wait()
    pick(near_half(width), width, sends, pool_rows, to_near)


def tangent_inner(
    width, combined, coefficients, interior, extract, lift, pool_in, from_far, base, pool_rows
):
    del pool_in
    rows, count = base.shape
    unpack(from_far, flat(pool_rows), 4 * count + width - near_half(width))
    state = load_field(combined, rows)
    scaled = load_field(coefficients, rows) * state
    inner = dot(stacked_factor(interior[...], 1), stacked_field(scaled), 1, 0)
    faces = dot(stacked_factor(packed(extract), 1), stacked_field(state), 1, 0)
    base[...] = state + inner[:rows] + from_columns(0.5 * packed(lift).T, faces)


def tangent_across(width, links_in, base, pool_in, from_near, lift, forward, pool_rows, across_rows, links, arrived):
    del pool_in
    fetch = pltpu.make_async_copy(links_in, links, arrived)
    fetch.start()
    count = base.shape[1]
    unpack(from_near, flat(pool_rows), 4 * count + near_half(width))
    fetch.wait()
    gather_blocks(count, links, flat(pool_rows), flat(across_rows))
    store_field(forward, base[...] + from_rows(0.5 * packed(lift).T, flat(across_rows)[...]))


def call(kernel, outs, operands, scratch=(), table=None, aliases=None, flops=0, buffers=()):
    outs = [out if isinstance(out, jax.ShapeDtypeStruct) else jax.ShapeDtypeStruct(out, jnp.float32) for out in outs]
    buffers = [pltpu.VMEM((rows, 1, LANES), jnp.float32) for rows in scratch] + list(buffers)
    if table is not None:
        buffers += [pltpu.SMEM((table,), jnp.int32), pltpu.SemaphoreType.DMA]
    function = kernel.func if isinstance(kernel, functools.partial) else kernel
    return pl.pallas_call(
        kernel,
        out_shape=outs,
        in_specs=[pl.BlockSpec(memory_space=pltpu.VMEM)] * len(operands),
        out_specs=[pl.BlockSpec(memory_space=pltpu.VMEM)] * len(outs),
        scratch_shapes=buffers,
        input_output_aliases=aliases or {},
        compiler_params=pltpu.CompilerParams(vmem_limit_bytes=VMEM_LIMIT),
        cost_estimate=pl.CostEstimate(flops=flops * 10**9, bytes_accessed=0, transcendentals=0),
        name=function.__name__,
    )(*operands)


def exchange(to_near, to_far, axis):
    devices = lax.axis_size(axis)
    near = [(i, i ^ 1) for i in range(devices)]
    far = [(i, (i + (1 if i % 2 else -1)) % devices) for i in range(devices)]
    return lax.ppermute(to_near, axis, near), lax.ppermute(to_far, axis, far)


def from_behind(array, axis, by):
    devices = lax.axis_size(axis)
    pairs = [(i, i + by) for i in range(devices) if 0 <= i + by < devices]
    return lax.ppermute(array, axis, pairs)


def per_device(multipliers, coefficients, neighbours, send_list, interior, extract, lift):
    rows, count = multipliers.shape[1:]
    width = send_list.shape[0] // 2
    lines = (rows * count // LANES, LANES)
    message = (width // 4, 1, LANES)
    face_rows = (4 * count, 1, LANES)
    pool_rows = (4 * count + 2 * width + 8, 1, LANES)
    own = multipliers.reshape(lines)
    coefs = coefficients.reshape(lines)
    link_lines = link_blocks(neighbours)
    links = link_lines.reshape(-1)
    lift, extract = lift.transpose(2, 0, 1), extract.transpose(1, 0, 2)
    earlier = from_behind(own, "tm", 1)
    (sums,) = call(clear, [pool_rows], (), flops=3)
    sums, dense, to_near, to_far = call(
        functools.partial(adjoint_sums, width),
        [pool_rows, (LANES, count), message, message],
        (links, link_lines, own, lift, sums),
        scratch=((4 - DENSE) * count,),
        buffers=(
            pltpu.VMEM((DENSE, 2 * SLOT, count), jnp.float32),
            pltpu.VMEM(((4 * count + 2 * width) // TILE * 2 * SLOT, TILE), jnp.float32),
        ),
        table=4 * count,
        aliases={4: 0},
        flops=9,
    )
    from_near, from_far = exchange(to_near, to_far, "space")
    partial, extra = call(
        adjoint_inner, [(rows, count), face_rows], (own, coefs, sums, dense, interior, lift, extract), flops=2
    )
    (extra,) = call(
        functools.partial(join_near, width),
        [face_rows],
        (send_list, from_near, extra),
        scratch=(width,),
        table=2 * width,
        aliases={2: 0},
        flops=1,
    )
    combined, to_far, pool, _ = call(
        functools.partial(join_far, width),
        [lines, message, pool_rows, face_rows],
        (send_list, partial, earlier, from_far, extra, extract),
        scratch=(width,),
        table=2 * width,
        aliases={4: 3},
        flops=5,
    )
    (to_near,) = call(
        functools.partial(pick_near, width), [message], (send_list, pool), table=2 * width, flops=2
    )
    later = from_behind(combined, "tm", -1)
    from_near, from_far = exchange(to_near, to_far, "space")
    base, pool = call(
        functools.partial(tangent_inner, width),
        [(rows, count), pool_rows],
        (combined, coefs, interior, extract, lift, pool, from_far),
        aliases={5: 1},
        flops=4,
    )
    forward, _ = call(
        functools.partial(tangent_across, width),
        [lines, pool_rows],
        (links, base, pool, from_near, lift),
        scratch=(count,),
        table=4 * count,
        aliases={2: 1},
    )
    return (forward - later).reshape(1, rows, count)


def solution(mesh):
    placed = (
        P(("groups", "tm"), None, "space"),
        P(("groups", "tm"), None, "space"),
        P(None, "space"),
        P("space"),
        P(),
        P(),
        P(),
    )
    return jax.shard_map(
        per_device,
        mesh=mesh,
        in_specs=placed,
        out_specs=P(("groups", "tm"), None, "space"),
        check_vma=False,
    )
```

```python
import functools

import jax
import jax.numpy as jnp
from jax import lax
from jax.experimental import pallas as pl
from jax.experimental.pallas import tpu as pltpu
from jax.sharding import PartitionSpec as P

LANES = 128
SLOT = 32
DEPTH = 64
UNROLL = 32
TILE = 256
EXTRA = 3
VMEM_LIMIT = 32 * 1024 * 1024


def pad_rows(value, rows):
    missing = rows - value.shape[0]
    if missing == 0:
        return value
    return jnp.concatenate([value, jnp.zeros((missing, value.shape[1]), value.dtype)], axis=0)


def pad_columns(value, columns):
    missing = columns - value.shape[1]
    if missing == 0:
        return value
    return jnp.concatenate([value, jnp.zeros((value.shape[0], missing), value.dtype)], axis=1)


def halves(value):
    high = value.astype(jnp.bfloat16)
    low = (value - high.astype(jnp.float32)).astype(jnp.bfloat16)
    return high, low


def dot(left, right, left_dim, right_dim):
    dims = (((left_dim,), (right_dim,)), ((), ()))
    return lax.dot_general(left, right, dims, preferred_element_type=jnp.float32)


def stacked_field(field):
    high, low = halves(pad_rows(field, DEPTH))
    return jnp.concatenate([high, low, high], axis=0)


def stacked_factor(matrix, axis):
    padded = pad_rows(matrix, DEPTH) if axis == 0 else pad_columns(matrix, DEPTH)
    high, low = halves(padded)
    return jnp.concatenate([high, high, low], axis=axis)


def from_rows(matrix, table):
    rows = matrix.shape[0]
    high, low = halves(pad_rows(matrix, DEPTH))
    left = jnp.concatenate(
        [jnp.concatenate([high, high], axis=1), jnp.concatenate([low, jnp.zeros_like(low)], axis=1)], axis=0
    )
    both = dot(left, jnp.concatenate(halves(table), axis=1), 1, 1)
    return (both[:DEPTH] + both[DEPTH:])[:rows]


def from_columns(matrix, table):
    rows = matrix.shape[0]
    high, low = halves(pad_rows(matrix, DEPTH))
    left = jnp.concatenate(
        [jnp.concatenate([high, high], axis=1), jnp.concatenate([low, jnp.zeros_like(low)], axis=1)], axis=0
    )
    both = dot(left, jnp.concatenate(halves(table), axis=0), 1, 0)
    return (both[:DEPTH] + both[DEPTH:])[:rows]


def slot_of_lane(shape):
    return lax.broadcasted_iota(jnp.int32, shape, 1) // SLOT


def choose_slots(blocks):
    slot = slot_of_lane(blocks[0].shape)
    result = blocks[0]
    for q in range(1, len(blocks)):
        result = jnp.where(slot == q, blocks[q], result)
    return result


def repeat_slot(block, q):
    only = jnp.where(slot_of_lane(block.shape) == q, block, 0.0)
    twice = only + pltpu.roll(only, SLOT, 1)
    return twice + pltpu.roll(twice, 2 * SLOT, 1)


def flat(ref):
    return ref.reshape(ref.shape[0], ref.shape[2])


def load_field(ref, rows):
    tiles = ref.shape[0] // rows
    return jnp.concatenate([ref[pl.ds(t, rows, stride=tiles), :] for t in range(tiles)], axis=1)


def store_field(ref, field):
    rows, count = field.shape
    tiles = count // LANES
    for t in range(tiles):
        ref[pl.ds(t, rows, stride=tiles), :] = field[:, t * LANES : (t + 1) * LANES]


def for_rows(count, step):
    together = min(count, 256)

    def body(i, carry):
        step(pl.multiple_of(i * together, together), together)
        return carry

    lax.fori_loop(0, count // together, body, 0)


def move(count, load, store):
    for first in range(0, count, UNROLL):
        rows = [load(u) for u in range(first, first + UNROLL)]
        for u in range(UNROLL):
            store(first + u, rows[u])


def link_blocks(neighbours):
    count = neighbours.shape[1]
    return neighbours.reshape(4, count // LANES, LANES).transpose(1, 0, 2).reshape(-1, LANES)


def gather_blocks(count, links, source, target):
    line = lax.broadcasted_iota(jnp.int32, (8, LANES), 0)
    slot = slot_of_lane((8, LANES))

    def body(block, carry):
        first = pl.multiple_of(block * LANES, LANES)
        mine = links.at[pl.ds(pl.multiple_of(block * (4 * LANES), 4 * LANES), 4 * LANES)]
        for group in range(0, LANES, 8):
            faces = []
            for f in range(4):
                together = jnp.broadcast_to(source[pl.ds(mine[f * LANES + group], 1), :], (8, LANES))
                for u in range(1, 8):
                    row = jnp.broadcast_to(source[pl.ds(mine[f * LANES + group + u], 1), :], (8, LANES))
                    together = jnp.where(line == u, row, together)
                faces.append(together)
            result = faces[0]
            for f in range(1, 4):
                result = jnp.where(slot == f, faces[f], result)
            target[pl.ds(pl.multiple_of(first + group, 8), 8), :] = result
        return carry

    lax.fori_loop(0, count // LANES, body, 0)


def packed(faces):
    return jnp.concatenate([pad_rows(faces[:, f, :], SLOT) for f in range(4)], axis=0)


def repeated(face):
    return stacked_factor(jnp.concatenate([pad_rows(face, SLOT)] * 4, axis=0).T, 0)


def near_half(width):
    return (1 - lax.axis_index("space") % 2) * width


def unpack(source, target, first):
    quarter = source.shape[0]
    for q in range(4):
        start = pl.multiple_of(first + q * quarter, quarter)
        target[pl.ds(start, quarter), :] = repeat_slot(flat(source)[...], q)


def clear(sums):
    flat(sums)[...] = jnp.zeros((sums.shape[0], LANES), jnp.float32)


def dense_sums(face, index, block, links, parts_ref, acc):
    lines = TILE // LANES
    places = [links[pl.ds((block * lines + line) * 4 + face, 1), :] for line in range(lines)]
    places = jnp.concatenate(places, axis=1)
    parts = parts_ref[index, :, pl.ds(pl.multiple_of(block * TILE, TILE), TILE)]
    lane = lax.broadcasted_iota(jnp.int32, (TILE, TILE), 0)
    one = jnp.where((places & (TILE - 1)) == lane, 1.0, 0.0).astype(jnp.bfloat16)
    high = places // TILE
    count = acc.shape[0] // parts.shape[0]
    masked = [jnp.where(high == h, parts, 0.0).astype(jnp.bfloat16) for h in range(count)]
    acc[...] += dot(jnp.concatenate(masked, axis=0), one, 1, 1)


def adjoint_sums(
    width,
    links_in,
    link_lines,
    multipliers,
    lift,
    sums_in,
    sums_rows,
    dense,
    to_near,
    to_far,
    half_rows,
    parts,
    acc,
    links,
    arrived,
):
    del sums_in
    fetch = pltpu.make_async_copy(links_in, links, arrived)
    fetch.start()
    rows = lift.shape[2]
    count = dense.shape[1]
    quarter = width // 4
    half, sums = flat(half_rows), flat(sums_rows)
    field = stacked_field(load_field(multipliers, rows))
    transposed = field.T
    for f in range(3):
        half[f * count : (f + 1) * count, :] = dot(transposed, repeated(0.5 * lift[:, f, :]), 1, 0)
    for i, f in enumerate((3, 2)):
        face = dot(stacked_factor(pad_rows(0.5 * lift[:, f, :], SLOT), 1), field, 1, 0)
        high, low = halves(face)
        parts[i] = jnp.concatenate([high.astype(jnp.float32), low.astype(jnp.float32)], axis=0)
    acc[...] = jnp.zeros(acc.shape, jnp.float32)
    fetch.wait()

    blocks, lines = count // TILE, count // LANES
    steps, skipped = blocks + EXTRA, EXTRA * (TILE // LANES)
    each = pl.cdiv(3 * lines - skipped, steps)

    def body(step, carry):
        second = step // blocks
        dense_sums(3 - second, second, step - second * blocks, link_lines, parts, acc)
        for u in range(each):
            at = step * each + u
            face = jnp.minimum(at // lines, 2)
            line = jnp.minimum(at - face * lines + jnp.where(face == 2, skipped, 0), lines - 1)
            mine = links.at[pl.ds(pl.multiple_of((line * 4 + face) * LANES, LANES), LANES)]
            first = pl.multiple_of((face * lines + line) * LANES, LANES)
            for group in range(0, LANES, 8):
                rows = half[pl.ds(pl.multiple_of(first + group, 8), 8), :]
                for v in range(8):
                    sums[pl.ds(mine[group + v], 1), :] = rows[v : v + 1, :]
        return carry

    lax.fori_loop(0, steps, body, 0)

    def place(h):
        start = pl.multiple_of(h * 2 * SLOT, 2 * SLOT)
        return acc[pl.ds(start, SLOT), :] + acc[pl.ds(pl.multiple_of(start + SLOT, SLOT), SLOT), :]

    near = near_half(width)
    for out, start in ((to_near, near), (to_far, width - near)):
        starts = [pl.multiple_of(4 * count + start + q * quarter, quarter) for q in range(4)]
        added = jnp.concatenate([place((4 * count + start) // TILE + q) for q in range(4)], axis=0).T
        flat(out)[...] = choose_slots([sums[pl.ds(start, quarter), :] for start in starts]) + added
    per_face = count // TILE
    for f in range(4):
        for t in range(per_face):
            dense[f * SLOT : (f + 1) * SLOT, t * TILE : (t + 1) * TILE] = place(f * per_face + t)


def adjoint_inner(multipliers, coefficients, sums_rows, dense, interior, lift, extract, partial, extra_rows):
    rows, count = partial.shape
    sums = flat(sums_rows)
    state = load_field(multipliers, rows)
    coefs = load_field(coefficients, rows)
    field = stacked_field(state)
    inner = dot(stacked_factor(interior[...].T, 1), field, 1, 0)
    own = dot(stacked_factor(0.5 * packed(lift), 1), field, 1, 0) + dense[...]
    moved = choose_slots([sums[f * count : (f + 1) * count, :] for f in range(4)])
    back = packed(extract).T
    partial[...] = state + coefs * inner[:rows] + from_columns(back, own) + from_rows(back, moved)
    flat(extra_rows)[...] = jnp.zeros((extra_rows.shape[0], LANES), jnp.float32)


def spread(first, width, sends, received_rows, extra_rows):
    def scatter(base, together):
        mine = received_rows.at[pl.ds(base, together)]
        places = sends.at[pl.ds(first + base, together)]

        def store(u, row):
            extra_rows[places[u]] = row

        move(together, lambda u: mine[u], store)

    for_rows(width, scatter)


def join_near(width, sends_in, from_near, extra_in, extra_rows, received_rows, sends, arrived):
    del extra_in
    fetch = pltpu.make_async_copy(sends_in, sends, arrived)
    fetch.start()
    unpack(from_near, flat(received_rows), 0)
    fetch.wait()
    spread(near_half(width), width, sends, received_rows, extra_rows)


def pick(first, width, sends, pool_rows, out):
    quarter = width // 4
    for q in range(4):
        lanes = slice(q * SLOT, (q + 1) * SLOT)

        def group(base, together):
            places = sends.at[pl.ds(first + q * quarter + base, together)]
            mine = out.at[pl.ds(base, together)]

            def store(u, row):
                mine[u, :, lanes] = row

            move(together, lambda u: pool_rows[places[u], :, lanes], store)

        for_rows(quarter, group)


def join_far(
    width,
    sends_in,
    partial,
    earlier,
    from_far,
    extra_in,
    extract,
    combined,
    to_far,
    pool_rows,
    extra_rows,
    received_rows,
    sends,
    arrived,
):
    del extra_in
    fetch = pltpu.make_async_copy(sends_in, sends, arrived)
    fetch.start()
    rows, count = partial.shape
    extra, pool = flat(extra_rows), flat(pool_rows)
    pool[4 * count + 2 * width :, :] = jnp.zeros((8, LANES), jnp.float32)
    unpack(from_far, flat(received_rows), 0)
    far = width - near_half(width)
    fetch.wait()
    spread(far, width, sends, received_rows, extra_rows)
    dfaces = choose_slots([extra[f * count : (f + 1) * count, :] for f in range(4)])
    total = partial[...] - load_field(earlier, rows) + from_rows(packed(extract).T, dfaces)
    store_field(combined, total)
    transposed = stacked_field(total).T
    for f in range(4):
        pool[f * count : (f + 1) * count, :] = dot(transposed, repeated(extract[:, f, :]), 1, 0)
    pick(far, width, sends, pool_rows, to_far)


def pick_near(width, sends_in, pool_rows, to_near, sends, arrived):
    fetch = pltpu.make_async_copy(sends_in, sends, arrived)
    fetch.start()
    fetch.wait()
    pick(near_half(width), width, sends, pool_rows, to_near)


def take_far(width, pool_in, from_far, pool_rows):
    del pool_in
    start = pool_rows.shape[0] - 8 - width - near_half(width)
    unpack(from_far, flat(pool_rows), pl.multiple_of(start, LANES))


def tangent_inner(combined, coefficients, interior, extract, lift, base):
    rows, count = base.shape
    state = load_field(combined, rows)
    scaled = load_field(coefficients, rows) * state
    inner = dot(stacked_factor(interior[...], 1), stacked_field(scaled), 1, 0)
    faces = dot(stacked_factor(packed(extract), 1), stacked_field(state), 1, 0)
    base[...] = state + inner[:rows] + from_columns(0.5 * packed(lift).T, faces)


def tangent_across(width, links_in, base, pool_in, from_near, lift, forward, pool_rows, across_rows, links, arrived):
    del pool_in
    fetch = pltpu.make_async_copy(links_in, links, arrived)
    fetch.start()
    count = base.shape[1]
    unpack(from_near, flat(pool_rows), 4 * count + near_half(width))
    fetch.wait()
    gather_blocks(count, links, flat(pool_rows), flat(across_rows))
    store_field(forward, base[...] + from_rows(0.5 * packed(lift).T, flat(across_rows)[...]))


def call(kernel, outs, operands, scratch=(), table=None, aliases=None, flops=0, buffers=()):
    outs = [out if isinstance(out, jax.ShapeDtypeStruct) else jax.ShapeDtypeStruct(out, jnp.float32) for out in outs]
    buffers = [pltpu.VMEM((rows, 1, LANES), jnp.float32) for rows in scratch] + list(buffers)
    if table is not None:
        buffers += [pltpu.SMEM((table,), jnp.int32), pltpu.SemaphoreType.DMA]
    function = kernel.func if isinstance(kernel, functools.partial) else kernel
    return pl.pallas_call(
        kernel,
        out_shape=outs,
        in_specs=[pl.BlockSpec(memory_space=pltpu.VMEM)] * len(operands),
        out_specs=[pl.BlockSpec(memory_space=pltpu.VMEM)] * len(outs),
        scratch_shapes=buffers,
        input_output_aliases=aliases or {},
        compiler_params=pltpu.CompilerParams(vmem_limit_bytes=VMEM_LIMIT),
        cost_estimate=pl.CostEstimate(flops=int(flops * 10**9), bytes_accessed=0, transcendentals=0),
        name=function.__name__,
    )(*operands)


def exchange(to_near, to_far, axis):
    devices = lax.axis_size(axis)
    near = [(i, i ^ 1) for i in range(devices)]
    far = [(i, (i + (1 if i % 2 else -1)) % devices) for i in range(devices)]
    return lax.ppermute(to_near, axis, near), lax.ppermute(to_far, axis, far)


def from_behind(array, axis, by):
    devices = lax.axis_size(axis)
    pairs = [(i, i + by) for i in range(devices) if 0 <= i + by < devices]
    return lax.ppermute(array, axis, pairs)


def per_device(multipliers, coefficients, neighbours, send_list, interior, extract, lift):
    rows, count = multipliers.shape[1:]
    width = send_list.shape[0] // 2
    lines = (rows * count // LANES, LANES)
    message = (width // 4, 1, LANES)
    face_rows = (4 * count, 1, LANES)
    pool_rows = (4 * count + 2 * width + 8, 1, LANES)
    own = multipliers.reshape(lines)
    coefs = coefficients.reshape(lines)
    link_lines = link_blocks(neighbours)
    links = link_lines.reshape(-1)
    lift, extract = lift.transpose(2, 0, 1), extract.transpose(1, 0, 2)
    earlier = from_behind(own, "tm", 1)
    (sums,) = call(clear, [pool_rows], (), flops=3)
    sums, dense, to_near, to_far = call(
        functools.partial(adjoint_sums, width),
        [pool_rows, (LANES, count), message, message],
        (links, link_lines, own, lift, sums),
        scratch=(3 * count,),
        buffers=(
            pltpu.VMEM((2, 2 * SLOT, count), jnp.float32),
            pltpu.VMEM(((4 * count + 2 * width) // TILE * 2 * SLOT, TILE), jnp.float32),
        ),
        table=4 * count,
        aliases={4: 0},
        flops=9,
    )
    from_near, from_far = exchange(to_near, to_far, "space")
    partial, extra = call(
        adjoint_inner, [(rows, count), face_rows], (own, coefs, sums, dense, interior, lift, extract), flops=2
    )
    (extra,) = call(
        functools.partial(join_near, width),
        [face_rows],
        (send_list, from_near, extra),
        scratch=(width,),
        table=2 * width,
        aliases={2: 0},
        flops=1,
    )
    combined, to_far, pool, _ = call(
        functools.partial(join_far, width),
        [lines, message, pool_rows, face_rows],
        (send_list, partial, earlier, from_far, extra, extract),
        scratch=(width,),
        table=2 * width,
        aliases={4: 3},
        flops=5,
    )
    (to_near,) = call(
        functools.partial(pick_near, width), [message], (send_list, pool), table=2 * width, flops=2
    )
    later = from_behind(combined, "tm", -1)
    from_near, from_far = exchange(to_near, to_far, "space")
    (base,) = call(tangent_inner, [(rows, count)], (combined, coefs, interior, extract, lift), flops=1)
    (pool,) = call(
        functools.partial(take_far, width), [pool_rows], (pool, from_far), aliases={0: 0}, flops=1
    )
    forward, _ = call(
        functools.partial(tangent_across, width),
        [lines, pool_rows],
        (links, base, pool, from_near, lift),
        scratch=(count,),
        table=4 * count,
        aliases={2: 1},
        flops=1,
    )
    return (forward - later).reshape(1, rows, count)


def solution(mesh):
    placed = (
        P(("groups", "tm"), None, "space"),
        P(("groups", "tm"), None, "space"),
        P(None, "space"),
        P("space"),
        P(),
        P(),
        P(),
    )
    return jax.shard_map(
        per_device,
        mesh=mesh,
        in_specs=placed,
        out_specs=P(("groups", "tm"), None, "space"),
        check_vma=False,
    )
```

```python
import functools

import jax
import jax.numpy as jnp
from jax import lax
from jax.experimental import pallas as pl
from jax.experimental.pallas import tpu as pltpu
from jax.sharding import PartitionSpec as P

LANES = 128
SLOT = 32
DEPTH = 64
UNROLL = 32
TILE = 256
EXTRA = 3
VMEM_LIMIT = 32 * 1024 * 1024


def pad_rows(value, rows):
    missing = rows - value.shape[0]
    if missing == 0:
        return value
    return jnp.concatenate([value, jnp.zeros((missing, value.shape[1]), value.dtype)], axis=0)


def pad_columns(value, columns):
    missing = columns - value.shape[1]
    if missing == 0:
        return value
    return jnp.concatenate([value, jnp.zeros((value.shape[0], missing), value.dtype)], axis=1)


def halves(value):
    high = value.astype(jnp.bfloat16)
    low = (value - high.astype(jnp.float32)).astype(jnp.bfloat16)
    return high, low


def dot(left, right, left_dim, right_dim):
    dims = (((left_dim,), (right_dim,)), ((), ()))
    return lax.dot_general(left, right, dims, preferred_element_type=jnp.float32)


def stacked_field(field):
    high, low = halves(pad_rows(field, DEPTH))
    return jnp.concatenate([high, low, high], axis=0)


def stacked_factor(matrix, axis):
    padded = pad_rows(matrix, DEPTH) if axis == 0 else pad_columns(matrix, DEPTH)
    high, low = halves(padded)
    return jnp.concatenate([high, high, low], axis=axis)


def from_rows(matrix, table):
    rows = matrix.shape[0]
    high, low = halves(pad_rows(matrix, DEPTH))
    left = jnp.concatenate(
        [jnp.concatenate([high, high], axis=1), jnp.concatenate([low, jnp.zeros_like(low)], axis=1)], axis=0
    )
    both = dot(left, jnp.concatenate(halves(table), axis=1), 1, 1)
    return (both[:DEPTH] + both[DEPTH:])[:rows]


def from_columns(matrix, table):
    rows = matrix.shape[0]
    high, low = halves(pad_rows(matrix, DEPTH))
    left = jnp.concatenate(
        [jnp.concatenate([high, high], axis=1), jnp.concatenate([low, jnp.zeros_like(low)], axis=1)], axis=0
    )
    both = dot(left, jnp.concatenate(halves(table), axis=0), 1, 0)
    return (both[:DEPTH] + both[DEPTH:])[:rows]


def slot_of_lane(shape):
    return lax.broadcasted_iota(jnp.int32, shape, 1) // SLOT


def choose_slots(blocks):
    slot = slot_of_lane(blocks[0].shape)
    result = blocks[0]
    for q in range(1, len(blocks)):
        result = jnp.where(slot == q, blocks[q], result)
    return result


def repeat_slot(block, q):
    only = jnp.where(slot_of_lane(block.shape) == q, block, 0.0)
    twice = only + pltpu.roll(only, SLOT, 1)
    return twice + pltpu.roll(twice, 2 * SLOT, 1)


def flat(ref):
    return ref.reshape(ref.shape[0], ref.shape[2])


def load_field(ref, rows):
    tiles = ref.shape[0] // rows
    return jnp.concatenate([ref[pl.ds(t, rows, stride=tiles), :] for t in range(tiles)], axis=1)


def store_field(ref, field):
    rows, count = field.shape
    tiles = count // LANES
    for t in range(tiles):
        ref[pl.ds(t, rows, stride=tiles), :] = field[:, t * LANES : (t + 1) * LANES]


def for_rows(count, step):
    together = min(count, 256)

    def body(i, carry):
        step(pl.multiple_of(i * together, together), together)
        return carry

    lax.fori_loop(0, count // together, body, 0)


def move(count, load, store):
    for first in range(0, count, UNROLL):
        rows = [load(u) for u in range(first, first + UNROLL)]
        for u in range(UNROLL):
            store(first + u, rows[u])


def link_blocks(neighbours):
    count = neighbours.shape[1]
    return neighbours.reshape(4, count // LANES, LANES).transpose(1, 0, 2).reshape(-1, LANES)


def gather_blocks(count, links, source, target):
    line = lax.broadcasted_iota(jnp.int32, (8, LANES), 0)
    slot = slot_of_lane((8, LANES))

    def body(block, carry):
        first = pl.multiple_of(block * LANES, LANES)
        mine = links.at[pl.ds(pl.multiple_of(block * (4 * LANES), 4 * LANES), 4 * LANES)]
        for group in range(0, LANES, 8):
            faces = []
            for f in range(4):
                together = jnp.broadcast_to(source[pl.ds(mine[f * LANES + group], 1), :], (8, LANES))
                for u in range(1, 8):
                    row = jnp.broadcast_to(source[pl.ds(mine[f * LANES + group + u], 1), :], (8, LANES))
                    together = jnp.where(line == u, row, together)
                faces.append(together)
            result = faces[0]
            for f in range(1, 4):
                result = jnp.where(slot == f, faces[f], result)
            target[pl.ds(pl.multiple_of(first + group, 8), 8), :] = result
        return carry

    lax.fori_loop(0, count // LANES, body, 0)


def packed(faces):
    return jnp.concatenate([pad_rows(faces[:, f, :], SLOT) for f in range(4)], axis=0)


def repeated(face):
    return stacked_factor(jnp.concatenate([pad_rows(face, SLOT)] * 4, axis=0).T, 0)


def near_half(width):
    return (1 - lax.axis_index("space") % 2) * width


def unpack(sources, target, first):
    part = sources[0].shape[0]
    for q in range(4):
        for i, source in enumerate(sources):
            start = pl.multiple_of(first + (q * len(sources) + i) * part, part)
            target[pl.ds(start, part), :] = repeat_slot(flat(source)[...], q)


def clear(sums):
    flat(sums)[...] = jnp.zeros((sums.shape[0], LANES), jnp.float32)


def dense_sums(face, index, block, links, parts_ref, acc):
    lines = TILE // LANES
    places = [links[pl.ds((block * lines + line) * 4 + face, 1), :] for line in range(lines)]
    places = jnp.concatenate(places, axis=1)
    parts = parts_ref[index, :, pl.ds(pl.multiple_of(block * TILE, TILE), TILE)]
    lane = lax.broadcasted_iota(jnp.int32, (TILE, TILE), 0)
    one = jnp.where((places & (TILE - 1)) == lane, 1.0, 0.0).astype(jnp.bfloat16)
    high = places // TILE
    count = acc.shape[0] // parts.shape[0]
    masked = [jnp.where(high == h, parts, 0.0).astype(jnp.bfloat16) for h in range(count)]
    acc[...] += dot(jnp.concatenate(masked, axis=0), one, 1, 1)


def adjoint_sums(
    width,
    links_in,
    link_lines,
    multipliers,
    lift,
    sums_in,
    sums_rows,
    dense,
    to_near,
    to_far_0,
    to_far_1,
    half_rows,
    parts,
    acc,
    links,
    arrived,
):
    del sums_in
    fetch = pltpu.make_async_copy(links_in, links, arrived)
    fetch.start()
    rows = lift.shape[2]
    count = dense.shape[1]
    quarter = width // 4
    half, sums = flat(half_rows), flat(sums_rows)
    field = stacked_field(load_field(multipliers, rows))
    transposed = field.T
    for f in range(3):
        half[f * count : (f + 1) * count, :] = dot(transposed, repeated(0.5 * lift[:, f, :]), 1, 0)
    for i, f in enumerate((3, 2)):
        face = dot(stacked_factor(pad_rows(0.5 * lift[:, f, :], SLOT), 1), field, 1, 0)
        high, low = halves(face)
        parts[i] = jnp.concatenate([high.astype(jnp.float32), low.astype(jnp.float32)], axis=0)
    acc[...] = jnp.zeros(acc.shape, jnp.float32)
    fetch.wait()

    def move_line(face, line):
        mine = links.at[pl.ds(pl.multiple_of((line * 4 + face) * LANES, LANES), LANES)]
        first = pl.multiple_of(face * count + line * LANES, LANES)
        for group in range(0, LANES, 8):
            rows = half[pl.ds(pl.multiple_of(first + group, 8), 8), :]
            for u in range(8):
                sums[pl.ds(mine[group + u], 1), :] = rows[u : u + 1, :]

    per_block = TILE // LANES
    last = count // LANES - 1
    each = pl.cdiv(last + 1 - EXTRA * per_block, EXTRA)

    def body(block, carry):
        dense_sums(3, 0, block, link_lines, parts, acc)
        for line in range(per_block):
            for f in range(2):
                move_line(f, block * per_block + line)
        return carry

    def rest(block, carry):
        dense_sums(2, 1, block, link_lines, parts, acc)
        for u in range(each):
            move_line(2, jnp.minimum(EXTRA * per_block + block * each + u, last))
        return carry

    lax.fori_loop(0, count // TILE, body, 0)
    lax.fori_loop(0, EXTRA, rest, 0)

    def place(h):
        start = pl.multiple_of(h * 2 * SLOT, 2 * SLOT)
        return acc[pl.ds(start, SLOT), :] + acc[pl.ds(pl.multiple_of(start + SLOT, SLOT), SLOT), :]

    near = near_half(width)
    messages = []
    for start in (near, width - near):
        starts = [pl.multiple_of(4 * count + start + q * quarter, quarter) for q in range(4)]
        added = jnp.concatenate([place((4 * count + start) // TILE + q) for q in range(4)], axis=0).T
        messages.append(choose_slots([sums[pl.ds(start, quarter), :] for start in starts]) + added)
    flat(to_near)[...] = messages[0]
    flat(to_far_0)[...] = messages[1][: quarter // 2]
    flat(to_far_1)[...] = messages[1][quarter // 2 :]
    per_face = count // TILE
    for f in range(4):
        for t in range(per_face):
            dense[f * SLOT : (f + 1) * SLOT, t * TILE : (t + 1) * TILE] = place(f * per_face + t)


def adjoint_inner(multipliers, coefficients, sums_rows, dense, interior, lift, extract, partial, extra_rows):
    rows, count = partial.shape
    sums = flat(sums_rows)
    state = load_field(multipliers, rows)
    coefs = load_field(coefficients, rows)
    field = stacked_field(state)
    inner = dot(stacked_factor(interior[...].T, 1), field, 1, 0)
    own = dot(stacked_factor(0.5 * packed(lift), 1), field, 1, 0) + dense[...]
    moved = choose_slots([sums[f * count : (f + 1) * count, :] for f in range(4)])
    back = packed(extract).T
    partial[...] = state + coefs * inner[:rows] + from_columns(back, own) + from_rows(back, moved)
    flat(extra_rows)[...] = jnp.zeros((extra_rows.shape[0], LANES), jnp.float32)


def spread(first, width, sends, received_rows, extra_rows):
    def scatter(base, together):
        mine = received_rows.at[pl.ds(base, together)]
        places = sends.at[pl.ds(first + base, together)]

        def store(u, row):
            extra_rows[places[u]] = row

        move(together, lambda u: mine[u], store)

    for_rows(width, scatter)


def join_near(width, sends_in, from_near, extra_in, extra_rows, received_rows, sends, arrived):
    del extra_in
    fetch = pltpu.make_async_copy(sends_in, sends, arrived)
    fetch.start()
    unpack([from_near], flat(received_rows), 0)
    fetch.wait()
    spread(near_half(width), width, sends, received_rows, extra_rows)


def pick(first, width, sends, pool_rows, out):
    quarter = width // 4
    for q in range(4):
        lanes = slice(q * SLOT, (q + 1) * SLOT)

        def group(base, together):
            places = sends.at[pl.ds(first + q * quarter + base, together)]
            mine = out.at[pl.ds(base, together)]

            def store(u, row):
                mine[u, :, lanes] = row

            move(together, lambda u: pool_rows[places[u], :, lanes], store)

        for_rows(quarter, group)


def join_far(
    width,
    sends_in,
    partial,
    earlier,
    from_far_0,
    from_far_1,
    extra_in,
    extract,
    combined,
    to_far,
    pool_rows,
    extra_rows,
    received_rows,
    sends,
    arrived,
):
    del extra_in
    fetch = pltpu.make_async_copy(sends_in, sends, arrived)
    fetch.start()
    rows, count = partial.shape
    extra, pool = flat(extra_rows), flat(pool_rows)
    pool[4 * count + 2 * width :, :] = jnp.zeros((8, LANES), jnp.float32)
    unpack([from_far_0, from_far_1], flat(received_rows), 0)
    far = width - near_half(width)
    fetch.wait()
    spread(far, width, sends, received_rows, extra_rows)
    dfaces = choose_slots([extra[f * count : (f + 1) * count, :] for f in range(4)])
    total = partial[...] - load_field(earlier, rows) + from_rows(packed(extract).T, dfaces)
    store_field(combined, total)
    transposed = stacked_field(total).T
    for f in range(4):
        pool[f * count : (f + 1) * count, :] = dot(transposed, repeated(extract[:, f, :]), 1, 0)
    pick(far, width, sends, pool_rows, to_far)


def pick_near(width, sends_in, pool_rows, to_near, sends, arrived):
    fetch = pltpu.make_async_copy(sends_in, sends, arrived)
    fetch.start()
    fetch.wait()
    pick(near_half(width), width, sends, pool_rows, to_near)


def tangent_inner(
    width, combined, coefficients, interior, extract, lift, pool_in, from_far, base, pool_rows
):
    del pool_in
    rows, count = base.shape
    unpack([from_far], flat(pool_rows), 4 * count + width - near_half(width))
    state = load_field(combined, rows)
    scaled = load_field(coefficients, rows) * state
    inner = dot(stacked_factor(interior[...], 1), stacked_field(scaled), 1, 0)
    faces = dot(stacked_factor(packed(extract), 1), stacked_field(state), 1, 0)
    base[...] = state + inner[:rows] + from_columns(0.5 * packed(lift).T, faces)


def tangent_across(width, links_in, base, pool_in, from_near, lift, forward, pool_rows, across_rows, links, arrived):
    del pool_in
    fetch = pltpu.make_async_copy(links_in, links, arrived)
    fetch.start()
    count = base.shape[1]
    unpack([from_near], flat(pool_rows), 4 * count + near_half(width))
    fetch.wait()
    gather_blocks(count, links, flat(pool_rows), flat(across_rows))
    store_field(forward, base[...] + from_rows(0.5 * packed(lift).T, flat(across_rows)[...]))


def call(kernel, outs, operands, scratch=(), table=None, aliases=None, flops=0, buffers=()):
    outs = [out if isinstance(out, jax.ShapeDtypeStruct) else jax.ShapeDtypeStruct(out, jnp.float32) for out in outs]
    buffers = [pltpu.VMEM((rows, 1, LANES), jnp.float32) for rows in scratch] + list(buffers)
    if table is not None:
        buffers += [pltpu.SMEM((table,), jnp.int32), pltpu.SemaphoreType.DMA]
    function = kernel.func if isinstance(kernel, functools.partial) else kernel
    return pl.pallas_call(
        kernel,
        out_shape=outs,
        in_specs=[pl.BlockSpec(memory_space=pltpu.VMEM)] * len(operands),
        out_specs=[pl.BlockSpec(memory_space=pltpu.VMEM)] * len(outs),
        scratch_shapes=buffers,
        input_output_aliases=aliases or {},
        compiler_params=pltpu.CompilerParams(vmem_limit_bytes=VMEM_LIMIT),
        cost_estimate=pl.CostEstimate(flops=flops * 10**9, bytes_accessed=0, transcendentals=0),
        name=function.__name__,
    )(*operands)


def exchange(to_near, to_far, axis):
    devices = lax.axis_size(axis)
    near = [(i, i ^ 1) for i in range(devices)]
    far = [(i, (i + (1 if i % 2 else -1)) % devices) for i in range(devices)]
    return lax.ppermute(to_near, axis, near), lax.ppermute(to_far, axis, far)


def from_behind(array, axis, by):
    devices = lax.axis_size(axis)
    pairs = [(i, i + by) for i in range(devices) if 0 <= i + by < devices]
    return lax.ppermute(array, axis, pairs)


def per_device(multipliers, coefficients, neighbours, send_list, interior, extract, lift):
    rows, count = multipliers.shape[1:]
    width = send_list.shape[0] // 2
    lines = (rows * count // LANES, LANES)
    message = (width // 4, 1, LANES)
    face_rows = (4 * count, 1, LANES)
    pool_rows = (4 * count + 2 * width + 8, 1, LANES)
    own = multipliers.reshape(lines)
    coefs = coefficients.reshape(lines)
    link_lines = link_blocks(neighbours)
    links = link_lines.reshape(-1)
    lift, extract = lift.transpose(2, 0, 1), extract.transpose(1, 0, 2)
    earlier = from_behind(own, "tm", 1)
    (sums,) = call(clear, [pool_rows], (), flops=3)
    part = (width // 8, 1, LANES)
    sums, dense, to_near, to_far_0, to_far_1 = call(
        functools.partial(adjoint_sums, width),
        [pool_rows, (LANES, count), message, part, part],
        (links, link_lines, own, lift, sums),
        scratch=(3 * count,),
        buffers=(
            pltpu.VMEM((2, 2 * SLOT, count), jnp.float32),
            pltpu.VMEM(((4 * count + 2 * width) // TILE * 2 * SLOT, TILE), jnp.float32),
        ),
        table=4 * count,
        aliases={4: 0},
        flops=9,
    )
    from_near, from_far_0 = exchange(to_near, to_far_0, "space")
    _, from_far_1 = exchange(to_near, to_far_1, "space")
    partial, extra = call(
        adjoint_inner, [(rows, count), face_rows], (own, coefs, sums, dense, interior, lift, extract), flops=2
    )
    (extra,) = call(
        functools.partial(join_near, width),
        [face_rows],
        (send_list, from_near, extra),
        scratch=(width,),
        table=2 * width,
        aliases={2: 0},
        flops=1,
    )
    combined, to_far, pool, _ = call(
        functools.partial(join_far, width),
        [lines, message, pool_rows, face_rows],
        (send_list, partial, earlier, from_far_0, from_far_1, extra, extract),
        scratch=(width,),
        table=2 * width,
        aliases={5: 3},
        flops=5,
    )
    (to_near,) = call(
        functools.partial(pick_near, width), [message], (send_list, pool), table=2 * width, flops=2
    )
    later = from_behind(combined, "tm", -1)
    from_near, from_far = exchange(to_near, to_far, "space")
    base, pool = call(
        functools.partial(tangent_inner, width),
        [(rows, count), pool_rows],
        (combined, coefs, interior, extract, lift, pool, from_far),
        aliases={5: 1},
        flops=4,
    )
    forward, _ = call(
        functools.partial(tangent_across, width),
        [lines, pool_rows],
        (links, base, pool, from_near, lift),
        scratch=(count,),
        table=4 * count,
        aliases={2: 1},
    )
    return (forward - later).reshape(1, rows, count)


def solution(mesh):
    placed = (
        P(("groups", "tm"), None, "space"),
        P(("groups", "tm"), None, "space"),
        P(None, "space"),
        P("space"),
        P(),
        P(),
        P(),
    )
    return jax.shard_map(
        per_device,
        mesh=mesh,
        in_specs=placed,
        out_specs=P(("groups", "tm"), None, "space"),
        check_vma=False,
    )
```

```python
import functools

import jax
import jax.numpy as jnp
from jax import lax
from jax.experimental import pallas as pl
from jax.experimental.pallas import tpu as pltpu
from jax.sharding import PartitionSpec as P

LANES = 128
SLOT = 32
DEPTH = 64
UNROLL = 32
GROUP = 16
TILE = 256
DENSE = 1
VMEM_LIMIT = 32 * 1024 * 1024


def pad_rows(value, rows):
    missing = rows - value.shape[0]
    if missing == 0:
        return value
    return jnp.concatenate([value, jnp.zeros((missing, value.shape[1]), value.dtype)], axis=0)


def pad_columns(value, columns):
    missing = columns - value.shape[1]
    if missing == 0:
        return value
    return jnp.concatenate([value, jnp.zeros((value.shape[0], missing), value.dtype)], axis=1)


def halves(value):
    high = value.astype(jnp.bfloat16)
    low = (value - high.astype(jnp.float32)).astype(jnp.bfloat16)
    return high, low


def dot(left, right, left_dim, right_dim):
    dims = (((left_dim,), (right_dim,)), ((), ()))
    return lax.dot_general(left, right, dims, preferred_element_type=jnp.float32)


def stacked_field(field):
    high, low = halves(pad_rows(field, DEPTH))
    return jnp.concatenate([high, low, high], axis=0)


def stacked_factor(matrix, axis):
    padded = pad_rows(matrix, DEPTH) if axis == 0 else pad_columns(matrix, DEPTH)
    high, low = halves(padded)
    return jnp.concatenate([high, high, low], axis=axis)


def from_rows(matrix, table):
    rows = matrix.shape[0]
    high, low = halves(pad_rows(matrix, DEPTH))
    left = jnp.concatenate(
        [jnp.concatenate([high, high], axis=1), jnp.concatenate([low, jnp.zeros_like(low)], axis=1)], axis=0
    )
    both = dot(left, jnp.concatenate(halves(table), axis=1), 1, 1)
    return (both[:DEPTH] + both[DEPTH:])[:rows]


def from_columns(matrix, table):
    rows = matrix.shape[0]
    high, low = halves(pad_rows(matrix, DEPTH))
    left = jnp.concatenate(
        [jnp.concatenate([high, high], axis=1), jnp.concatenate([low, jnp.zeros_like(low)], axis=1)], axis=0
    )
    both = dot(left, jnp.concatenate(halves(table), axis=0), 1, 0)
    return (both[:DEPTH] + both[DEPTH:])[:rows]


def slot_of_lane(shape):
    return lax.broadcasted_iota(jnp.int32, shape, 1) // SLOT


def choose_slots(blocks):
    slot = slot_of_lane(blocks[0].shape)
    result = blocks[0]
    for q in range(1, len(blocks)):
        result = jnp.where(slot == q, blocks[q], result)
    return result


def repeat_slot(block, q):
    only = jnp.where(slot_of_lane(block.shape) == q, block, 0.0)
    twice = only + pltpu.roll(only, SLOT, 1)
    return twice + pltpu.roll(twice, 2 * SLOT, 1)


def flat(ref):
    return ref.reshape(ref.shape[0], ref.shape[2])


def load_field(ref, rows):
    tiles = ref.shape[0] // rows
    return jnp.concatenate([ref[pl.ds(t, rows, stride=tiles), :] for t in range(tiles)], axis=1)


def store_field(ref, field):
    rows, count = field.shape
    tiles = count // LANES
    for t in range(tiles):
        ref[pl.ds(t, rows, stride=tiles), :] = field[:, t * LANES : (t + 1) * LANES]


def for_rows(count, step):
    together = min(count, 256)

    def body(i, carry):
        step(pl.multiple_of(i * together, together), together)
        return carry

    lax.fori_loop(0, count // together, body, 0)


def move(count, load, store):
    for first in range(0, count, UNROLL):
        rows = [load(u) for u in range(first, first + UNROLL)]
        for u in range(UNROLL):
            store(first + u, rows[u])


def link_blocks(neighbours):
    count = neighbours.shape[1]
    return neighbours.reshape(4, count // LANES, LANES).transpose(1, 0, 2).reshape(-1, LANES)


def gather_rows(count, links, source, target):
    def step(f, first, places):
        lanes = slice(f * SLOT, (f + 1) * SLOT)
        to = target.at[pl.ds(first, GROUP)]
        rows = [source[place, :, lanes] for place in places]
        for u in range(GROUP):
            to[u, :, lanes] = rows[u]

    def body(block, carry):
        first = pl.multiple_of(block * LANES, LANES)
        mine = links.at[pl.ds(pl.multiple_of(block * (4 * LANES), 4 * LANES), 4 * LANES)]
        for f in range(4):
            for group in range(0, LANES, GROUP):
                words = [mine[f * LANES + group + u] for u in range(GROUP)]
                step(f, first + group, [word & 0xFFFF for word in words])
                step(f, first + group + count // 2, [word >> 16 for word in words])
        return carry

    lax.fori_loop(0, count // (2 * LANES), body, 0)


def packed(faces):
    return jnp.concatenate([pad_rows(faces[:, f, :], SLOT) for f in range(4)], axis=0)


def repeated(face):
    return stacked_factor(jnp.concatenate([pad_rows(face, SLOT)] * 4, axis=0).T, 0)


def near_half(width):
    return (1 - lax.axis_index("space") % 2) * width


def unpack(sources, target, first):
    part = sources[0].shape[0]
    for q in range(4):
        for i, source in enumerate(sources):
            start = pl.multiple_of(first + (q * len(sources) + i) * part, part)
            target[pl.ds(start, part), :] = repeat_slot(flat(source)[...], q)


def clear(sums):
    flat(sums)[...] = jnp.zeros((sums.shape[0], LANES), jnp.float32)


def dense_sums(block, links, faces, parts_ref, acc):
    lines = TILE // LANES
    first = pl.multiple_of(block * TILE, TILE)
    places, parts = [], []
    for i, f in enumerate(faces):
        for line in range(lines):
            places.append(links[pl.ds((block * lines + line) * 4 + f, 1), :])
        parts.append(parts_ref[i, :, pl.ds(first, TILE)])
    places, parts = jnp.concatenate(places, axis=1), jnp.concatenate(parts, axis=1)
    width = places.shape[1]
    lane = lax.broadcasted_iota(jnp.int32, (TILE, width), 0)
    one = jnp.where((places & (TILE - 1)) == lane, 1.0, 0.0).astype(jnp.bfloat16)
    high = places // TILE
    count = acc.shape[0] // parts.shape[0]
    masked = [jnp.where(high == h, parts, 0.0).astype(jnp.bfloat16) for h in range(count)]
    acc[...] += dot(jnp.concatenate(masked, axis=0), one, 1, 1)


def adjoint_sums(
    width,
    links_in,
    link_lines,
    multipliers,
    lift,
    sums_in,
    sums_rows,
    dense,
    to_near,
    to_far_0,
    to_far_1,
    half_rows,
    parts,
    acc,
    links,
    arrived,
):
    del sums_in
    fetch = pltpu.make_async_copy(links_in, links, arrived)
    fetch.start()
    rows = lift.shape[2]
    count = dense.shape[1]
    quarter = width // 4
    half, sums = flat(half_rows), flat(sums_rows)
    field = stacked_field(load_field(multipliers, rows))
    transposed = field.T
    by_row, by_product = range(4 - DENSE), range(4 - DENSE, 4)
    for f in by_row:
        half[f * count : (f + 1) * count, :] = dot(transposed, repeated(0.5 * lift[:, f, :]), 1, 0)
    for i, f in enumerate(by_product):
        face = dot(stacked_factor(pad_rows(0.5 * lift[:, f, :], SLOT), 1), field, 1, 0)
        high, low = halves(face)
        parts[i] = jnp.concatenate([high.astype(jnp.float32), low.astype(jnp.float32)], axis=0)
    acc[...] = jnp.zeros(acc.shape, jnp.float32)
    fetch.wait()

    def body(block, carry):
        dense_sums(block, link_lines, by_product, parts, acc)
        for line in range(TILE // LANES):
            first = block * TILE + line * LANES
            mine = links.at[pl.ds(pl.multiple_of((block * TILE + line * LANES) * 4, 4 * LANES), 4 * LANES)]
            for f in by_row:
                for group in range(0, LANES, 8):
                    rows = half[pl.ds(pl.multiple_of(f * count + first + group, 8), 8), :]
                    for u in range(8):
                        sums[pl.ds(mine[f * LANES + group + u], 1), :] = rows[u : u + 1, :]
        return carry

    lax.fori_loop(0, count // TILE, body, 0)

    def place(h):
        start = pl.multiple_of(h * 2 * SLOT, 2 * SLOT)
        return acc[pl.ds(start, SLOT), :] + acc[pl.ds(pl.multiple_of(start + SLOT, SLOT), SLOT), :]

    near = near_half(width)
    messages = []
    for start in (near, width - near):
        starts = [pl.multiple_of(4 * count + start + q * quarter, quarter) for q in range(4)]
        added = jnp.concatenate([place((4 * count + start) // TILE + q) for q in range(4)], axis=0).T
        messages.append(choose_slots([sums[pl.ds(start, quarter), :] for start in starts]) + added)
    flat(to_near)[...] = messages[0]
    flat(to_far_0)[...] = messages[1][: quarter // 2]
    flat(to_far_1)[...] = messages[1][quarter // 2 :]
    per_face = count // TILE
    for f in range(4):
        for t in range(per_face):
            dense[f * SLOT : (f + 1) * SLOT, t * TILE : (t + 1) * TILE] = place(f * per_face + t)


def adjoint_inner(
    multipliers, coefficients, sums_rows, dense, interior, lift, extract, links, partial, extra_rows, words
):
    middle = links.shape[0] // 2
    words[...] = links[:middle, :] | (links[middle:, :] << 16)
    rows, count = partial.shape
    sums = flat(sums_rows)
    state = load_field(multipliers, rows)
    coefs = load_field(coefficients, rows)
    field = stacked_field(state)
    inner = dot(stacked_factor(interior[...].T, 1), field, 1, 0)
    own = dot(stacked_factor(0.5 * packed(lift), 1), field, 1, 0) + dense[...]
    moved = choose_slots([sums[f * count : (f + 1) * count, :] for f in range(4)])
    back = packed(extract).T
    partial[...] = state + coefs * inner[:rows] + from_columns(back, own) + from_rows(back, moved)
    flat(extra_rows)[...] = jnp.zeros((extra_rows.shape[0], LANES), jnp.float32)


def spread(first, width, sends, received_rows, extra_rows):
    def scatter(base, together):
        mine = received_rows.at[pl.ds(base, together)]
        places = sends.at[pl.ds(first + base, together)]

        def store(u, row):
            extra_rows[places[u]] = row

        move(together, lambda u: mine[u], store)

    for_rows(width, scatter)


def join_near(width, sends_in, from_near, extra_in, extra_rows, received_rows, sends, arrived):
    del extra_in
    fetch = pltpu.make_async_copy(sends_in, sends, arrived)
    fetch.start()
    unpack([from_near], flat(received_rows), 0)
    fetch.wait()
    spread(near_half(width), width, sends, received_rows, extra_rows)


def pick(first, width, sends, pool_rows, out):
    quarter = width // 4
    for q in range(4):
        lanes = slice(q * SLOT, (q + 1) * SLOT)

        def group(base, together):
            places = sends.at[pl.ds(first + q * quarter + base, together)]
            mine = out.at[pl.ds(base, together)]

            def store(u, row):
                mine[u, :, lanes] = row

            move(together, lambda u: pool_rows[places[u], :, lanes], store)

        for_rows(quarter, group)


def join_far(
    width,
    sends_in,
    partial,
    earlier,
    from_far_0,
    from_far_1,
    extra_in,
    extract,
    combined,
    to_far,
    pool_rows,
    extra_rows,
    received_rows,
    sends,
    arrived,
):
    del extra_in
    fetch = pltpu.make_async_copy(sends_in, sends, arrived)
    fetch.start()
    rows, count = partial.shape
    extra, pool = flat(extra_rows), flat(pool_rows)
    pool[4 * count + 2 * width :, :] = jnp.zeros((8, LANES), jnp.float32)
    unpack([from_far_0, from_far_1], flat(received_rows), 0)
    far = width - near_half(width)
    fetch.wait()
    spread(far, width, sends, received_rows, extra_rows)
    dfaces = choose_slots([extra[f * count : (f + 1) * count, :] for f in range(4)])
    total = partial[...] - load_field(earlier, rows) + from_rows(packed(extract).T, dfaces)
    store_field(combined, total)
    transposed = stacked_field(total).T
    for f in range(4):
        pool[f * count : (f + 1) * count, :] = dot(transposed, repeated(extract[:, f, :]), 1, 0)
    pick(far, width, sends, pool_rows, to_far)


def pick_near(width, sends_in, pool_rows, to_near, sends, arrived):
    fetch = pltpu.make_async_copy(sends_in, sends, arrived)
    fetch.start()
    fetch.wait()
    pick(near_half(width), width, sends, pool_rows, to_near)


def tangent_inner(
    width, combined, coefficients, interior, extract, lift, pool_in, from_far, base, pool_rows
):
    del pool_in
    rows, count = base.shape
    unpack([from_far], flat(pool_rows), 4 * count + width - near_half(width))
    state = load_field(combined, rows)
    scaled = load_field(coefficients, rows) * state
    inner = dot(stacked_factor(interior[...], 1), stacked_field(scaled), 1, 0)
    faces = dot(stacked_factor(packed(extract), 1), stacked_field(state), 1, 0)
    base[...] = state + inner[:rows] + from_columns(0.5 * packed(lift).T, faces)


def tangent_across(width, links_in, base, pool_in, from_near, lift, forward, pool_rows, across_rows, links, arrived):
    del pool_in
    fetch = pltpu.make_async_copy(links_in, links, arrived)
    fetch.start()
    count = base.shape[1]
    unpack([from_near], flat(pool_rows), 4 * count + near_half(width))
    fetch.wait()
    gather_rows(count, links, pool_rows, across_rows)
    store_field(forward, base[...] + from_rows(0.5 * packed(lift).T, flat(across_rows)[...]))


def call(kernel, outs, operands, scratch=(), table=None, aliases=None, flops=0, buffers=()):
    outs = [out if isinstance(out, jax.ShapeDtypeStruct) else jax.ShapeDtypeStruct(out, jnp.float32) for out in outs]
    buffers = [pltpu.VMEM((rows, 1, LANES), jnp.float32) for rows in scratch] + list(buffers)
    if table is not None:
        buffers += [pltpu.SMEM((table,), jnp.int32), pltpu.SemaphoreType.DMA]
    function = kernel.func if isinstance(kernel, functools.partial) else kernel
    return pl.pallas_call(
        kernel,
        out_shape=outs,
        in_specs=[pl.BlockSpec(memory_space=pltpu.VMEM)] * len(operands),
        out_specs=[pl.BlockSpec(memory_space=pltpu.VMEM)] * len(outs),
        scratch_shapes=buffers,
        input_output_aliases=aliases or {},
        compiler_params=pltpu.CompilerParams(vmem_limit_bytes=VMEM_LIMIT),
        cost_estimate=pl.CostEstimate(flops=flops * 10**9, bytes_accessed=0, transcendentals=0),
        name=function.__name__,
    )(*operands)


def exchange(to_near, to_far, axis):
    devices = lax.axis_size(axis)
    near = [(i, i ^ 1) for i in range(devices)]
    far = [(i, (i + (1 if i % 2 else -1)) % devices) for i in range(devices)]
    return lax.ppermute(to_near, axis, near), lax.ppermute(to_far, axis, far)


def from_behind(array, axis, by):
    devices = lax.axis_size(axis)
    pairs = [(i, i + by) for i in range(devices) if 0 <= i + by < devices]
    return lax.ppermute(array, axis, pairs)


def per_device(multipliers, coefficients, neighbours, send_list, interior, extract, lift):
    rows, count = multipliers.shape[1:]
    width = send_list.shape[0] // 2
    lines = (rows * count // LANES, LANES)
    message = (width // 4, 1, LANES)
    face_rows = (4 * count, 1, LANES)
    pool_rows = (4 * count + 2 * width + 8, 1, LANES)
    own = multipliers.reshape(lines)
    coefs = coefficients.reshape(lines)
    link_lines = link_blocks(neighbours)
    links = link_lines.reshape(-1)
    lift, extract = lift.transpose(2, 0, 1), extract.transpose(1, 0, 2)
    earlier = from_behind(own, "tm", 1)
    (sums,) = call(clear, [pool_rows], (), flops=3)
    part = (width // 8, 1, LANES)
    sums, dense, to_near, to_far_0, to_far_1 = call(
        functools.partial(adjoint_sums, width),
        [pool_rows, (LANES, count), message, part, part],
        (links, link_lines, own, lift, sums),
        scratch=((4 - DENSE) * count,),
        buffers=(
            pltpu.VMEM((DENSE, 2 * SLOT, count), jnp.float32),
            pltpu.VMEM(((4 * count + 2 * width) // TILE * 2 * SLOT, TILE), jnp.float32),
        ),
        table=4 * count,
        aliases={4: 0},
        flops=9,
    )
    from_near, from_far_0 = exchange(to_near, to_far_0, "space")
    _, from_far_1 = exchange(to_near, to_far_1, "space")
    partial, extra, words = call(
        adjoint_inner,
        [(rows, count), face_rows, jax.ShapeDtypeStruct((link_lines.shape[0] // 2, LANES), jnp.int32)],
        (own, coefs, sums, dense, interior, lift, extract, link_lines),
        flops=2,
    )
    (extra,) = call(
        functools.partial(join_near, width),
        [face_rows],
        (send_list, from_near, extra),
        scratch=(width,),
        table=2 * width,
        aliases={2: 0},
        flops=1,
    )
    combined, to_far, pool, _ = call(
        functools.partial(join_far, width),
        [lines, message, pool_rows, face_rows],
        (send_list, partial, earlier, from_far_0, from_far_1, extra, extract),
        scratch=(width,),
        table=2 * width,
        aliases={5: 3},
        flops=5,
    )
    (to_near,) = call(
        functools.partial(pick_near, width), [message], (send_list, pool), table=2 * width, flops=2
    )
    later = from_behind(combined, "tm", -1)
    from_near, from_far = exchange(to_near, to_far, "space")
    base, pool = call(
        functools.partial(tangent_inner, width),
        [(rows, count), pool_rows],
        (combined, coefs, interior, extract, lift, pool, from_far),
        aliases={5: 1},
        flops=4,
    )
    forward, _ = call(
        functools.partial(tangent_across, width),
        [lines, pool_rows],
        (words.reshape(-1), base, pool, from_near, lift),
        scratch=(count,),
        table=2 * count,
        aliases={2: 1},
    )
    return (forward - later).reshape(1, rows, count)


def solution(mesh):
    placed = (
        P(("groups", "tm"), None, "space"),
        P(("groups", "tm"), None, "space"),
        P(None, "space"),
        P("space"),
        P(),
        P(),
        P(),
    )
    return jax.shard_map(
        per_device,
        mesh=mesh,
        in_specs=placed,
        out_specs=P(("groups", "tm"), None, "space"),
        check_vma=False,
    )
```

```python
import functools

import jax
import jax.numpy as jnp
from jax import lax
from jax.experimental import pallas as pl
from jax.experimental.pallas import tpu as pltpu
from jax.sharding import PartitionSpec as P

LANES = 128
SLOT = 32
DEPTH = 64
UNROLL = 32
GROUP = 16
TILE = 256
DENSE = 1
VMEM_LIMIT = 32 * 1024 * 1024


def pad_rows(value, rows):
    missing = rows - value.shape[0]
    if missing == 0:
        return value
    return jnp.concatenate([value, jnp.zeros((missing, value.shape[1]), value.dtype)], axis=0)


def pad_columns(value, columns):
    missing = columns - value.shape[1]
    if missing == 0:
        return value
    return jnp.concatenate([value, jnp.zeros((value.shape[0], missing), value.dtype)], axis=1)


def halves(value):
    high = value.astype(jnp.bfloat16)
    low = (value - high.astype(jnp.float32)).astype(jnp.bfloat16)
    return high, low


def dot(left, right, left_dim, right_dim):
    dims = (((left_dim,), (right_dim,)), ((), ()))
    return lax.dot_general(left, right, dims, preferred_element_type=jnp.float32)


def stacked_field(field):
    high, low = halves(pad_rows(field, DEPTH))
    return jnp.concatenate([high, low, high], axis=0)


def stacked_factor(matrix, axis):
    padded = pad_rows(matrix, DEPTH) if axis == 0 else pad_columns(matrix, DEPTH)
    high, low = halves(padded)
    return jnp.concatenate([high, high, low], axis=axis)


def from_rows(matrix, table):
    rows = matrix.shape[0]
    high, low = halves(pad_rows(matrix, DEPTH))
    left = jnp.concatenate(
        [jnp.concatenate([high, high], axis=1), jnp.concatenate([low, jnp.zeros_like(low)], axis=1)], axis=0
    )
    both = dot(left, jnp.concatenate(halves(table), axis=1), 1, 1)
    return (both[:DEPTH] + both[DEPTH:])[:rows]


def from_columns(matrix, table):
    rows = matrix.shape[0]
    high, low = halves(pad_rows(matrix, DEPTH))
    left = jnp.concatenate(
        [jnp.concatenate([high, high], axis=1), jnp.concatenate([low, jnp.zeros_like(low)], axis=1)], axis=0
    )
    both = dot(left, jnp.concatenate(halves(table), axis=0), 1, 0)
    return (both[:DEPTH] + both[DEPTH:])[:rows]


def slot_of_lane(shape):
    return lax.broadcasted_iota(jnp.int32, shape, 1) // SLOT


def choose_slots(blocks):
    slot = slot_of_lane(blocks[0].shape)
    result = blocks[0]
    for q in range(1, len(blocks)):
        result = jnp.where(slot == q, blocks[q], result)
    return result


def repeat_slot(block, q):
    only = jnp.where(slot_of_lane(block.shape) == q, block, 0.0)
    twice = only + pltpu.roll(only, SLOT, 1)
    return twice + pltpu.roll(twice, 2 * SLOT, 1)


def flat(ref):
    return ref.reshape(ref.shape[0], ref.shape[2])


def load_field(ref, rows):
    tiles = ref.shape[0] // rows
    return jnp.concatenate([ref[pl.ds(t, rows, stride=tiles), :] for t in range(tiles)], axis=1)


def store_field(ref, field):
    rows, count = field.shape
    tiles = count // LANES
    for t in range(tiles):
        ref[pl.ds(t, rows, stride=tiles), :] = field[:, t * LANES : (t + 1) * LANES]


def for_rows(count, step):
    together = min(count, 256)

    def body(i, carry):
        step(pl.multiple_of(i * together, together), together)
        return carry

    lax.fori_loop(0, count // together, body, 0)


def move(count, load, store):
    for first in range(0, count, UNROLL):
        rows = [load(u) for u in range(first, first + UNROLL)]
        for u in range(UNROLL):
            store(first + u, rows[u])


def link_blocks(neighbours):
    count = neighbours.shape[1]
    return neighbours.reshape(4, count // LANES, LANES).transpose(1, 0, 2).reshape(-1, LANES)


def gather_rows(count, links, source, target):
    def step(f, first, places):
        lanes = slice(f * SLOT, (f + 1) * SLOT)
        to = target.at[pl.ds(first, GROUP)]
        rows = [source[place, :, lanes] for place in places]
        for u in range(GROUP):
            to[u, :, lanes] = rows[u]

    def body(block, carry):
        first = pl.multiple_of(block * LANES, LANES)
        mine = links.at[pl.ds(pl.multiple_of(block * (4 * LANES), 4 * LANES), 4 * LANES)]
        for f in range(4):
            for group in range(0, LANES, GROUP):
                words = [mine[f * LANES + group + u] for u in range(GROUP)]
                step(f, first + group, [word & 0xFFFF for word in words])
                step(f, first + group + count // 2, [word >> 16 for word in words])
        return carry

    lax.fori_loop(0, count // (2 * LANES), body, 0)


def packed(faces):
    return jnp.concatenate([pad_rows(faces[:, f, :], SLOT) for f in range(4)], axis=0)


def repeated(face):
    return stacked_factor(jnp.concatenate([pad_rows(face, SLOT)] * 4, axis=0).T, 0)


def near_half(width):
    return (1 - lax.axis_index("space") % 2) * width


def unpack(source, target, first):
    quarter = source.shape[0]
    for q in range(4):
        start = pl.multiple_of(first + q * quarter, quarter)
        target[pl.ds(start, quarter), :] = repeat_slot(flat(source)[...], q)


def clear(sums):
    flat(sums)[...] = jnp.zeros((sums.shape[0], LANES), jnp.float32)


def dense_sums(block, links, faces, parts_ref, acc):
    lines = TILE // LANES
    first = pl.multiple_of(block * TILE, TILE)
    places, parts = [], []
    for i, f in enumerate(faces):
        for line in range(lines):
            places.append(links[pl.ds((block * lines + line) * 4 + f, 1), :])
        parts.append(parts_ref[i, :, pl.ds(first, TILE)])
    places, parts = jnp.concatenate(places, axis=1), jnp.concatenate(parts, axis=1)
    width = places.shape[1]
    lane = lax.broadcasted_iota(jnp.int32, (TILE, width), 0)
    one = jnp.where((places & (TILE - 1)) == lane, 1.0, 0.0).astype(jnp.bfloat16)
    high = places // TILE
    count = acc.shape[0] // parts.shape[0]
    masked = [jnp.where(high == h, parts, 0.0).astype(jnp.bfloat16) for h in range(count)]
    acc[...] += dot(jnp.concatenate(masked, axis=0), one, 1, 1)


def adjoint_sums(
    width,
    links_in,
    link_lines,
    multipliers,
    lift,
    sums_in,
    sums_rows,
    dense,
    to_near,
    to_far,
    half_rows,
    parts,
    acc,
    links,
    arrived,
):
    del sums_in
    fetch = pltpu.make_async_copy(links_in, links, arrived)
    fetch.start()
    rows = lift.shape[2]
    count = dense.shape[1]
    quarter = width // 4
    half, sums = flat(half_rows), flat(sums_rows)
    field = stacked_field(load_field(multipliers, rows))
    transposed = field.T
    by_row, by_product = range(4 - DENSE), range(4 - DENSE, 4)
    for f in by_row:
        half[f * count : (f + 1) * count, :] = dot(transposed, repeated(0.5 * lift[:, f, :]), 1, 0)
    for i, f in enumerate(by_product):
        face = dot(stacked_factor(pad_rows(0.5 * lift[:, f, :], SLOT), 1), field, 1, 0)
        high, low = halves(face)
        parts[i] = jnp.concatenate([high.astype(jnp.float32), low.astype(jnp.float32)], axis=0)
    acc[...] = jnp.zeros(acc.shape, jnp.float32)
    fetch.wait()

    def body(block, carry):
        dense_sums(block, link_lines, by_product, parts, acc)
        for line in range(TILE // LANES):
            first = block * TILE + line * LANES
            mine = links.at[pl.ds(pl.multiple_of((block * TILE + line * LANES) * 4, 4 * LANES), 4 * LANES)]
            for f in by_row:
                for group in range(0, LANES, 8):
                    rows = half[pl.ds(pl.multiple_of(f * count + first + group, 8), 8), :]
                    for u in range(8):
                        sums[pl.ds(mine[f * LANES + group + u], 1), :] = rows[u : u + 1, :]
        return carry

    lax.fori_loop(0, count // TILE, body, 0)

    def place(h):
        start = pl.multiple_of(h * 2 * SLOT, 2 * SLOT)
        return acc[pl.ds(start, SLOT), :] + acc[pl.ds(pl.multiple_of(start + SLOT, SLOT), SLOT), :]

    near = near_half(width)
    for out, start in ((to_near, near), (to_far, width - near)):
        starts = [pl.multiple_of(4 * count + start + q * quarter, quarter) for q in range(4)]
        added = jnp.concatenate([place((4 * count + start) // TILE + q) for q in range(4)], axis=0).T
        flat(out)[...] = choose_slots([sums[pl.ds(start, quarter), :] for start in starts]) + added
    per_face = count // TILE
    for f in range(4):
        for t in range(per_face):
            dense[f * SLOT : (f + 1) * SLOT, t * TILE : (t + 1) * TILE] = place(f * per_face + t)


def adjoint_inner(
    multipliers, coefficients, sums_rows, dense, interior, lift, extract, links, partial, extra_rows, words
):
    middle = links.shape[0] // 2
    words[...] = links[:middle, :] | (links[middle:, :] << 16)
    rows, count = partial.shape
    sums = flat(sums_rows)
    state = load_field(multipliers, rows)
    coefs = load_field(coefficients, rows)
    field = stacked_field(state)
    inner = dot(stacked_factor(interior[...].T, 1), field, 1, 0)
    own = dot(stacked_factor(0.5 * packed(lift), 1), field, 1, 0) + dense[...]
    moved = choose_slots([sums[f * count : (f + 1) * count, :] for f in range(4)])
    back = packed(extract).T
    partial[...] = state + coefs * inner[:rows] + from_columns(back, own) + from_rows(back, moved)
    flat(extra_rows)[...] = jnp.zeros((extra_rows.shape[0], LANES), jnp.float32)


def spread(first, width, sends, received_rows, extra_rows):
    def scatter(base, together):
        mine = received_rows.at[pl.ds(base, together)]
        places = sends.at[pl.ds(first + base, together)]

        def store(u, row):
            extra_rows[places[u]] = row

        move(together, lambda u: mine[u], store)

    for_rows(width, scatter)


def join_near(width, sends_in, from_near, extra_in, extra_rows, received_rows, sends, arrived):
    del extra_in
    fetch = pltpu.make_async_copy(sends_in, sends, arrived)
    fetch.start()
    unpack(from_near, flat(received_rows), 0)
    fetch.wait()
    spread(near_half(width), width, sends, received_rows, extra_rows)


def pick(first, width, sends, pool_rows, out):
    quarter = width // 4
    for q in range(4):
        lanes = slice(q * SLOT, (q + 1) * SLOT)

        def group(base, together):
            places = sends.at[pl.ds(first + q * quarter + base, together)]
            mine = out.at[pl.ds(base, together)]

            def store(u, row):
                mine[u, :, lanes] = row

            move(together, lambda u: pool_rows[places[u], :, lanes], store)

        for_rows(quarter, group)


def join_far(
    width,
    sends_in,
    partial,
    earlier,
    from_far,
    extra_in,
    extract,
    combined,
    to_far,
    pool_rows,
    extra_rows,
    received_rows,
    sends,
    arrived,
):
    del extra_in
    fetch = pltpu.make_async_copy(sends_in, sends, arrived)
    fetch.start()
    rows, count = partial.shape
    extra, pool = flat(extra_rows), flat(pool_rows)
    pool[4 * count + 2 * width :, :] = jnp.zeros((8, LANES), jnp.float32)
    unpack(from_far, flat(received_rows), 0)
    far = width - near_half(width)
    fetch.wait()
    spread(far, width, sends, received_rows, extra_rows)
    dfaces = choose_slots([extra[f * count : (f + 1) * count, :] for f in range(4)])
    total = partial[...] - load_field(earlier, rows) + from_rows(packed(extract).T, dfaces)
    store_field(combined, total)
    transposed = stacked_field(total).T
    for f in range(4):
        pool[f * count : (f + 1) * count, :] = dot(transposed, repeated(extract[:, f, :]), 1, 0)
    pick(far, width, sends, pool_rows, to_far)


def pick_near(width, sends_in, pool_rows, to_near, sends, arrived):
    fetch = pltpu.make_async_copy(sends_in, sends, arrived)
    fetch.start()
    fetch.wait()
    pick(near_half(width), width, sends, pool_rows, to_near)


def tangent_inner(
    width, combined, coefficients, interior, extract, lift, pool_in, from_far, base, pool_rows
):
    del pool_in
    rows, count = base.shape
    unpack(from_far, flat(pool_rows), 4 * count + width - near_half(width))
    state = load_field(combined, rows)
    scaled = load_field(coefficients, rows) * state
    inner = dot(stacked_factor(interior[...], 1), stacked_field(scaled), 1, 0)
    faces = dot(stacked_factor(packed(extract), 1), stacked_field(state), 1, 0)
    base[...] = state + inner[:rows] + from_columns(0.5 * packed(lift).T, faces)


def tangent_across(width, links_in, base, pool_in, from_near, lift, forward, pool_rows, across_rows, links, arrived):
    del pool_in
    fetch = pltpu.make_async_copy(links_in, links, arrived)
    fetch.start()
    count = base.shape[1]
    unpack(from_near, flat(pool_rows), 4 * count + near_half(width))
    fetch.wait()
    gather_rows(count, links, pool_rows, across_rows)
    store_field(forward, base[...] + from_rows(0.5 * packed(lift).T, flat(across_rows)[...]))


def call(kernel, outs, operands, scratch=(), table=None, aliases=None, flops=0, buffers=()):
    outs = [out if isinstance(out, jax.ShapeDtypeStruct) else jax.ShapeDtypeStruct(out, jnp.float32) for out in outs]
    buffers = [pltpu.VMEM((rows, 1, LANES), jnp.float32) for rows in scratch] + list(buffers)
    if table is not None:
        buffers += [pltpu.SMEM((table,), jnp.int32), pltpu.SemaphoreType.DMA]
    function = kernel.func if isinstance(kernel, functools.partial) else kernel
    return pl.pallas_call(
        kernel,
        out_shape=outs,
        in_specs=[pl.BlockSpec(memory_space=pltpu.VMEM)] * len(operands),
        out_specs=[pl.BlockSpec(memory_space=pltpu.VMEM)] * len(outs),
        scratch_shapes=buffers,
        input_output_aliases=aliases or {},
        compiler_params=pltpu.CompilerParams(vmem_limit_bytes=VMEM_LIMIT),
        cost_estimate=pl.CostEstimate(flops=flops * 10**9, bytes_accessed=0, transcendentals=0),
        name=function.__name__,
    )(*operands)


def exchange(to_near, to_far, axis):
    devices = lax.axis_size(axis)
    near = [(i, i ^ 1) for i in range(devices)]
    far = [(i, (i + (1 if i % 2 else -1)) % devices) for i in range(devices)]
    return lax.ppermute(to_near, axis, near), lax.ppermute(to_far, axis, far)


def from_behind(array, axis, by):
    devices = lax.axis_size(axis)
    pairs = [(i, i + by) for i in range(devices) if 0 <= i + by < devices]
    return lax.ppermute(array, axis, pairs)


def per_device(multipliers, coefficients, neighbours, send_list, interior, extract, lift):
    rows, count = multipliers.shape[1:]
    width = send_list.shape[0] // 2
    lines = (rows * count // LANES, LANES)
    message = (width // 4, 1, LANES)
    face_rows = (4 * count, 1, LANES)
    pool_rows = (4 * count + 2 * width + 8, 1, LANES)
    own = multipliers.reshape(lines)
    coefs = coefficients.reshape(lines)
    link_lines = link_blocks(neighbours)
    links = link_lines.reshape(-1)
    lift, extract = lift.transpose(2, 0, 1), extract.transpose(1, 0, 2)
    earlier = from_behind(own, "tm", 1)
    (sums,) = call(clear, [pool_rows], (), flops=3)
    sums, dense, to_near, to_far = call(
        functools.partial(adjoint_sums, width),
        [pool_rows, (LANES, count), message, message],
        (links, link_lines, own, lift, sums),
        scratch=((4 - DENSE) * count,),
        buffers=(
            pltpu.VMEM((DENSE, 2 * SLOT, count), jnp.float32),
            pltpu.VMEM(((4 * count + 2 * width) // TILE * 2 * SLOT, TILE), jnp.float32),
        ),
        table=4 * count,
        aliases={4: 0},
        flops=9,
    )
    from_near, from_far = exchange(to_near, to_far, "space")
    partial, extra, words = call(
        adjoint_inner,
        [(rows, count), face_rows, jax.ShapeDtypeStruct((link_lines.shape[0] // 2, LANES), jnp.int32)],
        (own, coefs, sums, dense, interior, lift, extract, link_lines),
        flops=2,
    )
    (extra,) = call(
        functools.partial(join_near, width),
        [face_rows],
        (send_list, from_near, extra),
        scratch=(width,),
        table=2 * width,
        aliases={2: 0},
        flops=1,
    )
    combined, to_far, pool, _ = call(
        functools.partial(join_far, width),
        [lines, message, pool_rows, face_rows],
        (send_list, partial, earlier, from_far, extra, extract),
        scratch=(width,),
        table=2 * width,
        aliases={4: 3},
        flops=5,
    )
    (to_near,) = call(
        functools.partial(pick_near, width), [message], (send_list, pool), table=2 * width, flops=2
    )
    later = from_behind(combined, "tm", -1)
    from_near, from_far = exchange(to_near, to_far, "space")
    base, pool = call(
        functools.partial(tangent_inner, width),
        [(rows, count), pool_rows],
        (combined, coefs, interior, extract, lift, pool, from_far),
        aliases={5: 1},
        flops=4,
    )
    forward, _ = call(
        functools.partial(tangent_across, width),
        [lines, pool_rows],
        (words.reshape(-1), base, pool, from_near, lift),
        scratch=(count,),
        table=2 * count,
        aliases={2: 1},
    )
    return (forward - later).reshape(1, rows, count)


def solution(mesh):
    placed = (
        P(("groups", "tm"), None, "space"),
        P(("groups", "tm"), None, "space"),
        P(None, "space"),
        P("space"),
        P(),
        P(),
        P(),
    )
    return jax.shard_map(
        per_device,
        mesh=mesh,
        in_specs=placed,
        out_specs=P(("groups", "tm"), None, "space"),
        check_vma=False,
    )
```

```python
import functools

import jax
import jax.numpy as jnp
from jax import lax
from jax.experimental import pallas as pl
from jax.experimental.pallas import tpu as pltpu
from jax.sharding import PartitionSpec as P

LANES = 128
SLOT = 32
DEPTH = 64
UNROLL = 32
GROUP = 16
TILE = 256
DENSE = 1
VMEM_LIMIT = 32 * 1024 * 1024


def pad_rows(value, rows):
    missing = rows - value.shape[0]
    if missing == 0:
        return value
    return jnp.concatenate([value, jnp.zeros((missing, value.shape[1]), value.dtype)], axis=0)


def pad_columns(value, columns):
    missing = columns - value.shape[1]
    if missing == 0:
        return value
    return jnp.concatenate([value, jnp.zeros((value.shape[0], missing), value.dtype)], axis=1)


def halves(value):
    high = value.astype(jnp.bfloat16)
    low = (value - high.astype(jnp.float32)).astype(jnp.bfloat16)
    return high, low


def dot(left, right, left_dim, right_dim):
    dims = (((left_dim,), (right_dim,)), ((), ()))
    return lax.dot_general(left, right, dims, preferred_element_type=jnp.float32)


def stacked_field(field):
    high, low = halves(pad_rows(field, DEPTH))
    return jnp.concatenate([high, low, high], axis=0)


def stacked_factor(matrix, axis):
    padded = pad_rows(matrix, DEPTH) if axis == 0 else pad_columns(matrix, DEPTH)
    high, low = halves(padded)
    return jnp.concatenate([high, high, low], axis=axis)


def from_rows(matrix, table):
    rows = matrix.shape[0]
    high, low = halves(pad_rows(matrix, DEPTH))
    left = jnp.concatenate(
        [jnp.concatenate([high, high], axis=1), jnp.concatenate([low, jnp.zeros_like(low)], axis=1)], axis=0
    )
    both = dot(left, jnp.concatenate(halves(table), axis=1), 1, 1)
    return (both[:DEPTH] + both[DEPTH:])[:rows]


def from_columns(matrix, table):
    rows = matrix.shape[0]
    high, low = halves(pad_rows(matrix, DEPTH))
    left = jnp.concatenate(
        [jnp.concatenate([high, high], axis=1), jnp.concatenate([low, jnp.zeros_like(low)], axis=1)], axis=0
    )
    both = dot(left, jnp.concatenate(halves(table), axis=0), 1, 0)
    return (both[:DEPTH] + both[DEPTH:])[:rows]


def slot_of_lane(shape):
    return lax.broadcasted_iota(jnp.int32, shape, 1) // SLOT


def choose_slots(blocks):
    slot = slot_of_lane(blocks[0].shape)
    result = blocks[0]
    for q in range(1, len(blocks)):
        result = jnp.where(slot == q, blocks[q], result)
    return result


def repeat_slot(block, q):
    only = jnp.where(slot_of_lane(block.shape) == q, block, 0.0)
    twice = only + pltpu.roll(only, SLOT, 1)
    return twice + pltpu.roll(twice, 2 * SLOT, 1)


def flat(ref):
    return ref.reshape(ref.shape[0], ref.shape[2])


def load_field(ref, rows):
    tiles = ref.shape[0] // rows
    return jnp.concatenate([ref[pl.ds(t, rows, stride=tiles), :] for t in range(tiles)], axis=1)


def store_field(ref, field):
    rows, count = field.shape
    tiles = count // LANES
    for t in range(tiles):
        ref[pl.ds(t, rows, stride=tiles), :] = field[:, t * LANES : (t + 1) * LANES]


def for_rows(count, step):
    together = min(count, 256)

    def body(i, carry):
        step(pl.multiple_of(i * together, together), together)
        return carry

    lax.fori_loop(0, count // together, body, 0)


def move(count, load, store):
    for first in range(0, count, UNROLL):
        rows = [load(u) for u in range(first, first + UNROLL)]
        for u in range(UNROLL):
            store(first + u, rows[u])


def link_blocks(neighbours):
    count = neighbours.shape[1]
    return neighbours.reshape(4, count // LANES, LANES).transpose(1, 0, 2).reshape(-1, LANES)


def gather_rows(count, links, source, target):
    def step(f, first, places):
        lanes = slice(f * SLOT, (f + 1) * SLOT)
        to = target.at[pl.ds(first, GROUP)]
        rows = [source[place, :, lanes] for place in places]
        for u in range(GROUP):
            to[u, :, lanes] = rows[u]

    def body(block, carry):
        first = pl.multiple_of(block * LANES, LANES)
        mine = links.at[pl.ds(pl.multiple_of(block * (4 * LANES), 4 * LANES), 4 * LANES)]
        for f in range(4):
            for group in range(0, LANES, GROUP):
                words = [mine[f * LANES + group + u] for u in range(GROUP)]
                step(f, first + group, [word & 0xFFFF for word in words])
                step(f, first + group + count // 2, [word >> 16 for word in words])
        return carry

    lax.fori_loop(0, count // (2 * LANES), body, 0)


def packed(faces):
    return jnp.concatenate([pad_rows(faces[:, f, :], SLOT) for f in range(4)], axis=0)


def repeated(face):
    return stacked_factor(jnp.concatenate([pad_rows(face, SLOT)] * 4, axis=0).T, 0)


def near_half(width):
    return (1 - lax.axis_index("space") % 2) * width


def unpack(source, target, first):
    quarter = source.shape[0]
    for q in range(4):
        start = pl.multiple_of(first + q * quarter, quarter)
        target[pl.ds(start, quarter), :] = repeat_slot(flat(source)[...], q)


def clear(sums):
    flat(sums)[...] = jnp.zeros((sums.shape[0], LANES), jnp.float32)


def dense_sums(block, links, faces, parts_ref, acc):
    lines = TILE // LANES
    first = pl.multiple_of(block * TILE, TILE)
    places, parts = [], []
    for i, f in enumerate(faces):
        for line in range(lines):
            places.append(links[pl.ds((block * lines + line) * 4 + f, 1), :])
        parts.append(parts_ref[i, :, pl.ds(first, TILE)])
    places, parts = jnp.concatenate(places, axis=1), jnp.concatenate(parts, axis=1)
    width = places.shape[1]
    lane = lax.broadcasted_iota(jnp.int32, (TILE, width), 0)
    one = jnp.where((places & (TILE - 1)) == lane, 1.0, 0.0).astype(jnp.bfloat16)
    high = places // TILE
    count = acc.shape[0] // parts.shape[0]
    masked = [jnp.where(high == h, parts, 0.0).astype(jnp.bfloat16) for h in range(count)]
    acc[...] += dot(jnp.concatenate(masked, axis=0), one, 1, 1)


def place(acc, tile):
    start = pl.multiple_of(tile * 2 * SLOT, 2 * SLOT)
    return acc[pl.ds(start, SLOT), :] + acc[pl.ds(pl.multiple_of(start + SLOT, SLOT), SLOT), :]


def adjoint_sums(
    width,
    links_in,
    link_lines,
    multipliers,
    lift,
    sums_in,
    sums_rows,
    acc,
    to_near,
    to_far,
    half_rows,
    parts,
    links,
    arrived,
):
    del sums_in
    fetch = pltpu.make_async_copy(links_in, links, arrived)
    fetch.start()
    rows = lift.shape[2]
    count = parts.shape[2]
    quarter = width // 4
    half, sums = flat(half_rows), flat(sums_rows)
    field = stacked_field(load_field(multipliers, rows))
    transposed = field.T
    by_row, by_product = range(4 - DENSE), range(4 - DENSE, 4)
    for f in by_row:
        half[f * count : (f + 1) * count, :] = dot(transposed, repeated(0.5 * lift[:, f, :]), 1, 0)
    for i, f in enumerate(by_product):
        face = dot(stacked_factor(pad_rows(0.5 * lift[:, f, :], SLOT), 1), field, 1, 0)
        high, low = halves(face)
        parts[i] = jnp.concatenate([high.astype(jnp.float32), low.astype(jnp.float32)], axis=0)
    acc[...] = jnp.zeros(acc.shape, jnp.float32)
    fetch.wait()

    def body(block, carry):
        dense_sums(block, link_lines, by_product, parts, acc)
        for line in range(TILE // LANES):
            first = block * TILE + line * LANES
            mine = links.at[pl.ds(pl.multiple_of((block * TILE + line * LANES) * 4, 4 * LANES), 4 * LANES)]
            for f in by_row:
                for group in range(0, LANES, 8):
                    rows = half[pl.ds(pl.multiple_of(f * count + first + group, 8), 8), :]
                    for u in range(8):
                        sums[pl.ds(mine[f * LANES + group + u], 1), :] = rows[u : u + 1, :]
        return carry

    lax.fori_loop(0, count // TILE, body, 0)

    near = near_half(width)
    for out, start in ((to_near, near), (to_far, width - near)):
        starts = [pl.multiple_of(4 * count + start + q * quarter, quarter) for q in range(4)]
        added = jnp.concatenate([place(acc, (4 * count + start) // TILE + q) for q in range(4)], axis=0).T
        flat(out)[...] = choose_slots([sums[pl.ds(start, quarter), :] for start in starts]) + added


def adjoint_inner(
    multipliers, coefficients, sums_rows, acc, interior, lift, extract, links, partial, extra_rows, words
):
    middle = links.shape[0] // 2
    words[...] = links[:middle, :] | (links[middle:, :] << 16)
    rows, count = partial.shape
    sums = flat(sums_rows)
    state = load_field(multipliers, rows)
    coefs = load_field(coefficients, rows)
    field = stacked_field(state)
    inner = dot(stacked_factor(interior[...].T, 1), field, 1, 0)
    tiles = count // TILE
    dense = [jnp.concatenate([place(acc, f * tiles + t) for t in range(tiles)], axis=1) for f in range(4)]
    own = dot(stacked_factor(0.5 * packed(lift), 1), field, 1, 0) + jnp.concatenate(dense, axis=0)
    moved = choose_slots([sums[f * count : (f + 1) * count, :] for f in range(4)])
    back = packed(extract).T
    partial[...] = state + coefs * inner[:rows] + from_columns(back, own) + from_rows(back, moved)
    flat(extra_rows)[...] = jnp.zeros((extra_rows.shape[0], LANES), jnp.float32)


def spread(first, width, sends, received_rows, extra_rows):
    def scatter(base, together):
        mine = received_rows.at[pl.ds(base, together)]
        places = sends.at[pl.ds(first + base, together)]

        def store(u, row):
            extra_rows[places[u]] = row

        move(together, lambda u: mine[u], store)

    for_rows(width, scatter)


def join_near(width, sends_in, from_near, extra_in, extra_rows, received_rows, sends, arrived):
    del extra_in
    fetch = pltpu.make_async_copy(sends_in, sends, arrived)
    fetch.start()
    unpack(from_near, flat(received_rows), 0)
    fetch.wait()
    spread(near_half(width), width, sends, received_rows, extra_rows)


def pick(first, width, sends, pool_rows, out):
    quarter = width // 4
    for q in range(4):
        lanes = slice(q * SLOT, (q + 1) * SLOT)

        def group(base, together):
            places = sends.at[pl.ds(first + q * quarter + base, together)]
            mine = out.at[pl.ds(base, together)]

            def store(u, row):
                mine[u, :, lanes] = row

            move(together, lambda u: pool_rows[places[u], :, lanes], store)

        for_rows(quarter, group)


def join_far(
    width,
    sends_in,
    partial,
    earlier,
    from_far,
    extra_in,
    extract,
    combined,
    to_far,
    pool_rows,
    extra_rows,
    received_rows,
    sends,
    arrived,
):
    del extra_in
    fetch = pltpu.make_async_copy(sends_in, sends, arrived)
    fetch.start()
    rows, count = partial.shape
    extra, pool = flat(extra_rows), flat(pool_rows)
    pool[4 * count + 2 * width :, :] = jnp.zeros((8, LANES), jnp.float32)
    unpack(from_far, flat(received_rows), 0)
    far = width - near_half(width)
    fetch.wait()
    spread(far, width, sends, received_rows, extra_rows)
    dfaces = choose_slots([extra[f * count : (f + 1) * count, :] for f in range(4)])
    total = partial[...] - load_field(earlier, rows) + from_rows(packed(extract).T, dfaces)
    store_field(combined, total)
    transposed = stacked_field(total).T
    for f in range(4):
        pool[f * count : (f + 1) * count, :] = dot(transposed, repeated(extract[:, f, :]), 1, 0)
    pick(far, width, sends, pool_rows, to_far)


def pick_near(width, sends_in, pool_rows, to_near, sends, arrived):
    fetch = pltpu.make_async_copy(sends_in, sends, arrived)
    fetch.start()
    fetch.wait()
    pick(near_half(width), width, sends, pool_rows, to_near)


def tangent_inner(
    width, combined, coefficients, interior, extract, lift, pool_in, from_far, base, pool_rows
):
    del pool_in
    rows, count = base.shape
    unpack(from_far, flat(pool_rows), 4 * count + width - near_half(width))
    state = load_field(combined, rows)
    scaled = load_field(coefficients, rows) * state
    inner = dot(stacked_factor(interior[...], 1), stacked_field(scaled), 1, 0)
    faces = dot(stacked_factor(packed(extract), 1), stacked_field(state), 1, 0)
    base[...] = state + inner[:rows] + from_columns(0.5 * packed(lift).T, faces)


def tangent_across(width, links_in, base, pool_in, from_near, lift, forward, pool_rows, across_rows, links, arrived):
    del pool_in
    fetch = pltpu.make_async_copy(links_in, links, arrived)
    fetch.start()
    count = base.shape[1]
    unpack(from_near, flat(pool_rows), 4 * count + near_half(width))
    fetch.wait()
    gather_rows(count, links, pool_rows, across_rows)
    store_field(forward, base[...] + from_rows(0.5 * packed(lift).T, flat(across_rows)[...]))


def call(kernel, outs, operands, scratch=(), table=None, aliases=None, flops=0, buffers=()):
    outs = [out if isinstance(out, jax.ShapeDtypeStruct) else jax.ShapeDtypeStruct(out, jnp.float32) for out in outs]
    buffers = [pltpu.VMEM((rows, 1, LANES), jnp.float32) for rows in scratch] + list(buffers)
    if table is not None:
        buffers += [pltpu.SMEM((table,), jnp.int32), pltpu.SemaphoreType.DMA]
    function = kernel.func if isinstance(kernel, functools.partial) else kernel
    return pl.pallas_call(
        kernel,
        out_shape=outs,
        in_specs=[pl.BlockSpec(memory_space=pltpu.VMEM)] * len(operands),
        out_specs=[pl.BlockSpec(memory_space=pltpu.VMEM)] * len(outs),
        scratch_shapes=buffers,
        input_output_aliases=aliases or {},
        compiler_params=pltpu.CompilerParams(vmem_limit_bytes=VMEM_LIMIT),
        cost_estimate=pl.CostEstimate(flops=flops * 10**9, bytes_accessed=0, transcendentals=0),
        name=function.__name__,
    )(*operands)


def exchange(to_near, to_far, axis):
    devices = lax.axis_size(axis)
    near = [(i, i ^ 1) for i in range(devices)]
    far = [(i, (i + (1 if i % 2 else -1)) % devices) for i in range(devices)]
    return lax.ppermute(to_near, axis, near), lax.ppermute(to_far, axis, far)


def from_behind(array, axis, by):
    devices = lax.axis_size(axis)
    pairs = [(i, i + by) for i in range(devices) if 0 <= i + by < devices]
    return lax.ppermute(array, axis, pairs)


def per_device(multipliers, coefficients, neighbours, send_list, interior, extract, lift):
    rows, count = multipliers.shape[1:]
    width = send_list.shape[0] // 2
    lines = (rows * count // LANES, LANES)
    message = (width // 4, 1, LANES)
    face_rows = (4 * count, 1, LANES)
    pool_rows = (4 * count + 2 * width + 8, 1, LANES)
    own = multipliers.reshape(lines)
    coefs = coefficients.reshape(lines)
    link_lines = link_blocks(neighbours)
    links = link_lines.reshape(-1)
    lift, extract = lift.transpose(2, 0, 1), extract.transpose(1, 0, 2)
    earlier = from_behind(own, "tm", 1)
    (sums,) = call(clear, [pool_rows], (), flops=3)
    sums, dense, to_near, to_far = call(
        functools.partial(adjoint_sums, width),
        [pool_rows, ((4 * count + 2 * width) // TILE * 2 * SLOT, TILE), message, message],
        (links, link_lines, own, lift, sums),
        scratch=((4 - DENSE) * count,),
        buffers=(
            pltpu.VMEM((DENSE, 2 * SLOT, count), jnp.float32),
        ),
        table=4 * count,
        aliases={4: 0},
        flops=9,
    )
    from_near, from_far = exchange(to_near, to_far, "space")
    partial, extra, words = call(
        adjoint_inner,
        [(rows, count), face_rows, jax.ShapeDtypeStruct((link_lines.shape[0] // 2, LANES), jnp.int32)],
        (own, coefs, sums, dense, interior, lift, extract, link_lines),
        flops=2,
    )
    (extra,) = call(
        functools.partial(join_near, width),
        [face_rows],
        (send_list, from_near, extra),
        scratch=(width,),
        table=2 * width,
        aliases={2: 0},
        flops=1,
    )
    combined, to_far, pool, _ = call(
        functools.partial(join_far, width),
        [lines, message, pool_rows, face_rows],
        (send_list, partial, earlier, from_far, extra, extract),
        scratch=(width,),
        table=2 * width,
        aliases={4: 3},
        flops=5,
    )
    (to_near,) = call(
        functools.partial(pick_near, width), [message], (send_list, pool), table=2 * width, flops=2
    )
    later = from_behind(combined, "tm", -1)
    from_near, from_far = exchange(to_near, to_far, "space")
    base, pool = call(
        functools.partial(tangent_inner, width),
        [(rows, count), pool_rows],
        (combined, coefs, interior, extract, lift, pool, from_far),
        aliases={5: 1},
        flops=4,
    )
    forward, _ = call(
        functools.partial(tangent_across, width),
        [lines, pool_rows],
        (words.reshape(-1), base, pool, from_near, lift),
        scratch=(count,),
        table=2 * count,
        aliases={2: 1},
    )
    return (forward - later).reshape(1, rows, count)


def solution(mesh):
    placed = (
        P(("groups", "tm"), None, "space"),
        P(("groups", "tm"), None, "space"),
        P(None, "space"),
        P("space"),
        P(),
        P(),
        P(),
    )
    return jax.shard_map(
        per_device,
        mesh=mesh,
        in_specs=placed,
        out_specs=P(("groups", "tm"), None, "space"),
        check_vma=False,
    )
```
